32 devices in a mesh: dp: 2 (over y), fsdp: 16 (over z, x, core).
Axes of the slice: x: 2, y: 2, z: 4, core: 2. Of those that a mesh axis runs over, the one named last changes fastest.
Arguments:
- target: bfloat16 [64, 1200, 256], P(('dp', 'fsdp')), may hold values from -6 to 6
- memory: bfloat16 [64, 2048, 256], P(('dp', 'fsdp')), may hold values from -6 to 6
- memory_pos: bfloat16 [64, 2048, 256], P(('dp', 'fsdp')), may hold values from -1 to 1
- segment: int32 [64, 2048], P(('dp', 'fsdp')), may hold values from 0 to 12, as said below
- project_weight: bfloat16 [6, 256, 256], P(None, ('dp', 'fsdp')), may hold values from -0.375 to 0.375
- output_weight: bfloat16 [2, 256, 256], P(None, ('dp', 'fsdp')), may hold values from -1 to 1
- expand_weight: bfloat16 [256, 2048], P(None, ('dp', 'fsdp')), may hold values from -0.375 to 0.375
- shrink_weight: bfloat16 [2048, 256], P(('dp', 'fsdp')), may hold values from -0.125 to 0.125
- box_weight: bfloat16 [2, 256, 256], P(None, ('dp', 'fsdp')), may hold values from -0.375 to 0.375
- class_weight: bfloat16 [256, 92], P(('dp', 'fsdp')), may hold values from -0.375 to 0.375
- box_final: bfloat16 [256, 4], P(('dp', 'fsdp')), may hold values from -0.375 to 0.375
- query_pos: bfloat16 [100, 256], P(None, ('dp', 'fsdp')), may hold values from -6 to 6
- norm_gains: bfloat16 [4, 256], P(None, ('dp', 'fsdp')), may hold values from 0.25 to 1.75
- biases: bfloat16 [13, 256], P(None, ('dp', 'fsdp')), may hold values from -4 to 4
- expand_bias: bfloat16 [2048], P(('dp', 'fsdp')), may hold values from -4 to 4
- head_bias: bfloat16 [96], replicated, may hold values from -6 to 6
- output_cotangent: bfloat16 [64, 1200, 256], P(('dp', 'fsdp')), may hold values from -6 to 6
- logit_cotangent: bfloat16 [64, 1200, 92], P(('dp', 'fsdp')), may hold values from -6 to 6
- box_cotangent: bfloat16 [64, 1200, 4], P(('dp', 'fsdp')), may hold values from -6 to 6
Outputs:
- layer_output: bfloat16 [64, 1200, 256], P(('dp', 'fsdp'))
- target_grad: float32 [64, 1200, 256], P(('dp', 'fsdp'))
- memory_grad: float32 [64, 2048, 256], P(('dp', 'fsdp'))
- project_grad: float32 [6, 256, 256], P(None, ('dp', 'fsdp'))
- output_grad: float32 [2, 256, 256], P(None, ('dp', 'fsdp'))
- expand_grad: float32 [256, 2048], P(None, ('dp', 'fsdp'))
- shrink_grad: float32 [2048, 256], P(('dp', 'fsdp'))
- box_weight_grad: float32 [2, 256, 256], P(None, ('dp', 'fsdp'))
- class_grad: float32 [256, 92], P(('dp', 'fsdp'))
- box_final_grad: float32 [256, 4], P(('dp', 'fsdp'))
- query_pos_grad: float32 [100, 256], P(None, ('dp', 'fsdp'))
- gains_grad: float32 [4, 256], P(None, ('dp', 'fsdp'))
- biases_grad: float32 [13, 256], P(None, ('dp', 'fsdp'))
- expand_bias_grad: float32 [2048], P(('dp', 'fsdp'))
- head_bias_grad: float32 [96], replicated
The draws below stay inside these ranges and needn't reach their ends.
Inputs may be any that keep to these rules, and one draw needn't show every extreme that they name: `segment`: in each pack the images are contiguous non-empty runs of tokens numbered 0, 1, 2 in order, a pack holds 6 to 12 images, its last one or more tokens are padding marked 12, and some pack holds 12 images.
All inputs are finite; a program needn't handle non-finite values.
Results may differ from the reference program's by a relative error of at most 0.018.
The reference program's roundings to bfloat16 on the way count: a program that leaves them out, or rounds other values in their place, can miss the bound.
Values may be sent and summed in bfloat16 or wider, within the bound.
No kernel may reach another device: no remote copies, remote signals or barrier semaphores. Data moves between devices by JAX's collectives and lax.ppermute only.
A program may use at most 576 MiB of HBM per device.

```python
import jax
import jax.numpy as jnp
from jax import lax

D = 256
HEADS = 8
FF = 2048
NQ = 100
CLS = 92
IMG_MAX = 12
PACK = 2048
HEAD_DIM = 32
QCAP = 1200
NPACK = 64


def draw_segment(key, part):
    key = jax.random.fold_in(key, 11)
    keys = jax.random.split(key, 3)
    images = jax.random.randint(keys[0], (NPACK,), IMG_MAX // 2, IMG_MAX + 1)
    images = jnp.where(jnp.arange(NPACK) == 0, IMG_MAX, images)
    padding = jax.random.randint(keys[1], (NPACK,), 1, PACK // 8 + 1)
    used = PACK - padding
    shares = jax.random.randint(keys[2], (NPACK, IMG_MAX), 1, 4)
    shares = jnp.where(jnp.arange(IMG_MAX)[None, :] < images[:, None], shares, 0)
    bounds = jnp.cumsum(shares, axis=1) * used[:, None] // jnp.sum(shares, axis=1, keepdims=True)
    places = jnp.arange(PACK)
    return jnp.sum((bounds[:, None, :] <= places[None, :, None]).astype(jnp.int32), axis=2).astype(jnp.int32)


def levels(own_key, dims, cuts, low, top_value):
    def one(dim, blocks):
        heights = jax.random.uniform(jax.random.fold_in(jax.random.fold_in(own_key, 6), dim), (blocks,), jnp.float32, low / len(cuts), top_value / len(cuts))
        return jnp.repeat(jnp.exp(heights), dims[dim] // blocks).reshape((-1,) + (1,) * (len(dims) - dim - 1))

    loudness = one(*cuts[0])
    for cut in cuts[1:]:
        loudness = loudness * one(*cut)
    return loudness


def scatter_about(key, shape, scale, most, shards=(), held_as=jnp.bfloat16):
    level = levels(key, shape, shards, -0.22, 0.18) if shards else 1.0
    result = jax.random.normal(key, shape, jnp.float32) * scale * level
    return jnp.minimum(jnp.maximum(result, -most), most).astype(held_as)


def setup_inputs(seed: int = 0) -> dict:
    arg_keys = jax.random.split(jax.random.key(seed), 20)
    return {
        "target": scatter_about(arg_keys[0], (NPACK, QCAP, D), 1.0, 6.0, ((0, 32),)),
        "memory": scatter_about(arg_keys[1], (NPACK, PACK, D), 1.0, 6.0, ((0, 32),)),
        "memory_pos": jnp.clip(jax.random.uniform(arg_keys[2], (NPACK, PACK, D), jnp.float32, -1.0, 1.0) * levels(arg_keys[2], (NPACK, PACK, D), ((0, 32),), -0.4, 0.0), -1.0, 1.0).astype(jnp.bfloat16),
        "segment": draw_segment(jax.random.fold_in(arg_keys[19], 71), 0),
        "project_weight": scatter_about(arg_keys[4], (6, D, D), D ** -0.5, 0.375, ((1, 32),)),
        "output_weight": scatter_about(arg_keys[5], (2, D, D), (D // 8) ** -0.5, 1.0, ((1, 32),)),
        "expand_weight": scatter_about(arg_keys[6], (D, FF), D ** -0.5, 0.375, ((1, 32),)),
        "shrink_weight": scatter_about(arg_keys[7], (FF, D), FF ** -0.5, 0.125, ((0, 32),)),
        "box_weight": scatter_about(arg_keys[8], (2, D, D), D ** -0.5, 0.375, ((1, 32),)),
        "class_weight": scatter_about(arg_keys[9], (D, CLS), D ** -0.5, 0.375, ((0, 32),)),
        "box_final": scatter_about(arg_keys[10], (D, 4), D ** -0.5, 0.375, ((0, 32),)),
        "query_pos": scatter_about(arg_keys[11], (NQ, D), 1.0, 6.0, ((1, 32),)),
        "norm_gains": jnp.clip(1.0 + 0.15 * jax.random.normal(arg_keys[12], (4, D), jnp.float32), 0.25, 1.75).astype(jnp.bfloat16),
        "biases": scatter_about(arg_keys[13], (13, D), 0.3, 4.0, ((1, 32),)),
        "expand_bias": scatter_about(arg_keys[14], (FF,), 0.3, 4.0, ((0, 32),)),
        "head_bias": scatter_about(arg_keys[15], (CLS + 4,), 0.5, 6.0),
        "output_cotangent": scatter_about(arg_keys[16], (NPACK, QCAP, D), 1.0, 6.0, ((0, 32),)),
        "logit_cotangent": scatter_about(arg_keys[17], (NPACK, QCAP, CLS), 1.0, 6.0, ((0, 32),)),
        "box_cotangent": scatter_about(arg_keys[18], (NPACK, QCAP, 4), 1.0, 6.0, ((0, 32),)),
    }


@jax.custom_vjp
def low(v):
    return lax.optimization_barrier(v.astype(jnp.bfloat16)).astype(jnp.float32)

@jax.custom_vjp
def low_back(v):
    return v

def low_keep(v):
    return (low(v), None)

def low_pass(kept, grad):
    return (grad,)

def back_keep(v):
    return (v, None)

def back_low(kept, grad):
    return (low(grad),)
low.defvjp(low_keep, low_pass)
low_back.defvjp(back_keep, back_low)
epsilon = 1e-05
masked_score = -1000000000.0
highest = lax.Precision.HIGHEST

def matmul(left, right):
    return jnp.dot(left, right, precision=highest)

def layer_norm(value, gain, shift):
    middle = lax.optimization_barrier(jnp.mean(value, axis=-1, keepdims=True))
    centered = value - middle
    spread = lax.optimization_barrier(jnp.mean(centered * centered, axis=-1, keepdims=True))
    return centered * lax.rsqrt(spread + epsilon) * gain + shift

def softmax_rows(scores):
    maximum = lax.optimization_barrier(jnp.max(scores, axis=-1, keepdims=True))
    raised = jnp.exp(scores - maximum)
    return raised / lax.optimization_barrier(jnp.sum(raised, axis=-1, keepdims=True))

def forward_pack(weights, target, memory, memory_pos, segment):
    project, output, expand, shrink, box_layers, classes, box_final, query_pos, norm_gains, biases, expand_bias, head_bias = weights
    score_scale = HEAD_DIM ** (-0.5)
    images = jnp.max(jnp.where(segment < IMG_MAX, segment + 1, 0))
    image_of = jnp.arange(QCAP) // NQ
    live_rows = (image_of < images).astype(jnp.float32)[:, None]
    position = jnp.tile(query_pos, (IMG_MAX, 1))
    joined = low(target + position)
    query_self = low(low_back(matmul(joined, project[0]) + biases[0]))
    key_self = low(low_back(matmul(joined, project[1])))
    value_self = low(low_back(matmul(target, project[2]) + biases[1]))
    heads_shape = (IMG_MAX, NQ, HEADS, HEAD_DIM)
    scores = jnp.einsum('iqhd,ikhd->ihqk', query_self.reshape(heads_shape), key_self.reshape(heads_shape), precision=highest)
    attend = low(softmax_rows(low_back(scores * score_scale)))
    context = jnp.einsum('ihqk,ikhd->iqhd', attend, value_self.reshape(heads_shape), precision=highest)
    context = low(low_back(context.reshape(QCAP, D)))
    after_self = layer_norm(target + low_back(matmul(context, output[0]) + biases[2]), norm_gains[0], biases[9])
    cross_query = low(low_back(matmul(low(after_self + position), project[3]) + biases[3]))
    cross_key = low(low_back(matmul(low(memory + memory_pos), project[4])))
    cross_value = low(low_back(matmul(memory, project[5]) + biases[4]))
    allowed = image_of[:, None] == segment[None, :]
    split_shape = (-1, HEADS, HEAD_DIM)
    cross = jnp.einsum('qhd,khd->hqk', cross_query.reshape(split_shape), cross_key.reshape(split_shape), precision=highest)
    cross = jnp.where(allowed[None], low_back(cross * score_scale), masked_score)
    attend_cross = low(softmax_rows(cross))
    context_cross = jnp.einsum('hqk,khd->qhd', attend_cross, cross_value.reshape(split_shape), precision=highest)
    context_cross = low(low_back(context_cross.reshape(QCAP, D)))
    after_cross = layer_norm(after_self + low_back(matmul(context_cross, output[1]) + biases[5]), norm_gains[1], biases[10])
    hidden_pre = low_back(matmul(low(after_cross), expand) + expand_bias)
    hidden = low(jax.nn.gelu(hidden_pre))
    after_ffn = layer_norm(after_cross + low_back(matmul(hidden, shrink) + biases[6]), norm_gains[2], biases[11])
    normed = low(layer_norm(after_ffn, norm_gains[3], biases[12]))
    logits = matmul(normed, classes) + head_bias[:CLS]
    box_one = low(jax.nn.gelu(low_back(matmul(normed, box_layers[0]) + biases[7])))
    box_two = low(jax.nn.gelu(low_back(matmul(box_one, box_layers[1]) + biases[8])))
    box_out = jax.nn.sigmoid(low_back(matmul(box_two, box_final) + head_bias[CLS:]))
    return (after_ffn * live_rows, logits * live_rows, box_out * live_rows)

def reference(target, memory, memory_pos, segment, project_weight, output_weight, expand_weight, shrink_weight, box_weight, class_weight, box_final, query_pos, norm_gains, biases, expand_bias, head_bias, output_cotangent, logit_cotangent, box_cotangent):
    weights = tuple((array.astype(jnp.float32) for array in (project_weight, output_weight, expand_weight, shrink_weight, box_weight, class_weight, box_final, query_pos, norm_gains, biases, expand_bias, head_bias)))
    position_all = memory_pos.astype(jnp.float32)

    def whole(weight_set, target_all, memory_all):

        def one_pack(pack):
            return jax.checkpoint(forward_pack)(weight_set, pack[0], pack[1], pack[2], pack[3])
        return lax.map(one_pack, (target_all, memory_all, position_all, segment))
    primal, pullback = jax.vjp(whole, weights, target.astype(jnp.float32), memory.astype(jnp.float32))
    weight_grads, target_grad, memory_grad = pullback((output_cotangent.astype(jnp.float32), logit_cotangent.astype(jnp.float32), box_cotangent.astype(jnp.float32)))
    return (primal[0].astype(jnp.bfloat16), target_grad, memory_grad, weight_grads[0], weight_grads[1], weight_grads[2], weight_grads[3], weight_grads[4], weight_grads[5], weight_grads[6], weight_grads[7], weight_grads[8], weight_grads[9], weight_grads[10], weight_grads[11])
```

```python
import functools

import jax
import jax.numpy as jnp
from jax import lax
from jax.experimental import pallas as pl
from jax.experimental.pallas import tpu as pltpu
from jax.sharding import PartitionSpec as P

D = 256
HEADS = 8
NQ = 100
CLS = 92
IMG_MAX = 12
HEAD_DIM = 32
QP = 128
ROWS = IMG_MAX * QP
PAIRS = HEADS // 2
BLOCK = 256
CHUNK = 512
STEP = 240
FF_BLOCKS = 8
GAIN = 96
BIAS = 100
EXPAND_BIAS = 113
POS = 128
SMALL = 8
SHRINK = 2
EXPAND = 10

epsilon = 1e-05
masked = -1000000000.0
scale = HEAD_DIM ** (-0.5)
log2e = 1.4426950408889634
gelu_a = 0.7978845608028654
gelu_b = gelu_a * 0.044715
AXES = ("dp", "fsdp")
f32 = jnp.float32
bf16 = jnp.bfloat16


def nn(left, right):
    return jnp.dot(left, right, preferred_element_type=f32)


def nt(left, right):
    return lax.dot_general(left, right, (((1,), (1,)), ((), ())), preferred_element_type=f32)


def tn(left, right):
    return lax.dot_general(left, right, (((0,), (0,)), ((), ())), preferred_element_type=f32)


def total(value):
    return jnp.sum(value, axis=0, keepdims=True)


def norm_parts(value):
    middle = jnp.mean(value, axis=-1, keepdims=True)
    centered = value - middle
    spread = jnp.mean(centered * centered, axis=-1, keepdims=True)
    inverse = lax.rsqrt(spread + epsilon)
    return centered * inverse, inverse


def norm_back(unit, inverse, gain, grad):
    scaled = grad * gain
    first = jnp.mean(scaled, axis=-1, keepdims=True)
    second = jnp.mean(scaled * unit, axis=-1, keepdims=True)
    return inverse * (scaled - first - unit * second)


def gelu_parts(value):
    square = value * value
    cdf = 0.5 + 0.5 * jnp.tanh(value * (gelu_a + gelu_b * square))
    result = value * cdf
    slope = cdf + (result - result * cdf) * (2.0 * gelu_a + 6.0 * gelu_b * square)
    return result, slope


def spread_heads(value, spread_ref):
    lane = lax.broadcasted_iota(jnp.int32, (1, D), 1) // HEAD_DIM
    for head in range(HEADS):
        keep = (lane == head).astype(f32).astype(bf16)
        spread_ref[head * QP : (head + 1) * QP, :] = value * keep


def pair_blocks(product):
    half = HEAD_DIM
    return jnp.concatenate([product[:half, :QP], product[half:, QP:]], axis=0)


def pair_rows(ref, pair):
    return ref[2 * QP * pair : 2 * QP * (pair + 1), :]


def attend_block(key, value, spread_ref, valid):
    value_t = value.T
    parts = []
    logs = []
    for pair in range(PAIRS):
        scores = jnp.where(valid, nt(key, pair_rows(spread_ref, pair)), masked)
        top = jnp.max(scores, axis=0, keepdims=True)
        raised = jnp.exp2((scores - top) * (scale * log2e))
        sums = total(raised)
        attend = (raised * (1.0 / sums)).astype(bf16)
        rows = slice(2 * HEAD_DIM * pair, 2 * HEAD_DIM * (pair + 1))
        parts.append(pair_blocks(nn(value_t[rows, :], attend)))
        logs.append(top * (scale * log2e) + jnp.log2(sums))
    return jnp.concatenate(parts, axis=0).T, jnp.concatenate(logs, axis=1)


def early_kernel(
    bounds,
    target_ref,
    memory_ref,
    pos_ref,
    w_ref,
    after_ref,
    qs_ref,
    ks_ref,
    vs_ref,
    cs_ref,
    inner_ref,
    cq_ref,
    ck_ref,
    cv_ref,
    cc_ref,
    log_ref,
    small_ref,
    flat_ref,
    rows_ref,
    spread_ref,
    score_ref,
    top_ref,
    sum_ref,
    out_ref,
):
    pack = pl.program_id(0)
    slots = target_ref.shape[1]
    tokens = memory_ref.shape[1]

    @pl.when(pack == 0)
    def _():
        small_ref[...] = w_ref[SMALL].astype(f32).T

    def bias(index):
        return small_ref[BIAS + index : BIAS + index + 1, :]

    def gain(index):
        return small_ref[GAIN + index : GAIN + index + 1, :]

    inside = lax.broadcasted_iota(jnp.int32, (QP, 1), 0) < NQ
    position = small_ref[POS : POS + QP, :]
    positions = jnp.concatenate([position] * (CHUNK // QP), axis=0)

    value_sum = jnp.zeros((1, D), f32)
    for start in range(0, tokens, CHUNK):
        rows = slice(start, start + CHUNK)
        memory = memory_ref[0, rows, :]
        joined = (memory.astype(f32) + pos_ref[0, rows, :].astype(f32)).astype(bf16)
        ck_ref[0, rows, :] = nn(joined, w_ref[4]).astype(bf16)
        value = (nn(memory, w_ref[5]) + bias(4)).astype(bf16)
        cv_ref[0, rows, :] = value
        value_sum += total(value.astype(f32))
    value_mean = value_sum * (1.0 / tokens)

    flat_ref[0:slots, :] = target_ref[0].astype(f32)
    for image in range(IMG_MAX):
        part = flat_ref[image * NQ : image * NQ + QP, :]
        rows_ref[image * QP : (image + 1) * QP, :] = jnp.where(inside, part, 0.0)

    for start in range(0, ROWS, CHUNK):
        rows = slice(start, start + CHUNK)
        target = rows_ref[rows, :]
        joined = (target + positions).astype(bf16)
        qs_ref[0, rows, :] = (nn(joined, w_ref[0]) + bias(0)).astype(bf16)
        ks_ref[0, rows, :] = nn(joined, w_ref[1]).astype(bf16)
        vs_ref[0, rows, :] = (nn(target.astype(bf16), w_ref[2]) + bias(1)).astype(bf16)

    @pl.loop(0, IMG_MAX)
    def _(image):
        rows = pl.ds(pl.multiple_of(image * QP, QP), QP)
        spread_heads(qs_ref[0, rows, :], spread_ref)
        context, unused = attend_block(ks_ref[0, rows, :], vs_ref[0, rows, :], spread_ref, inside)
        cs_ref[0, rows, :] = context.astype(bf16)

    for start in range(0, ROWS, CHUNK):
        rows = slice(start, start + CHUNK)
        value = rows_ref[rows, :] + nn(cs_ref[0, rows, :], w_ref[6]) + bias(2)
        inner_ref[0, rows, :] = value
        unit, unused = norm_parts(value)
        after = unit * gain(0) + bias(9)
        rows_ref[rows, :] = after
        query = nn((after + positions).astype(bf16), w_ref[3]) + bias(3)
        cq_ref[0, rows, :] = query.astype(bf16)

    @pl.loop(0, IMG_MAX)
    def _(image):
        rows = pl.ds(pl.multiple_of(image * QP, QP), QP)
        first = bounds[pack, image]
        last = bounds[pack, image + 1]
        origin = (first // 16) * 16
        blocks = (last - origin + (BLOCK - 1)) // BLOCK
        spread_heads(cq_ref[0, rows, :], spread_ref)

        def place_at(block):
            wanted = origin + block * BLOCK
            start = pl.multiple_of(jnp.minimum(wanted, tokens - BLOCK), 16)
            token = start + lax.broadcasted_iota(jnp.int32, (BLOCK, 1), 0)
            valid = (token >= jnp.maximum(first, wanted)) & (token < last)
            return pl.ds(start, BLOCK), valid

        @pl.when(last == first)
        def _():
            cc_ref[0, rows, :] = jnp.broadcast_to(value_mean, (QP, D)).astype(bf16)
            log_ref[0, image] = jnp.zeros((1, HEADS * QP), f32)

        @pl.when((last > first) & (blocks == 1))
        def _():
            place, valid = place_at(0)
            context, logs = attend_block(
                ck_ref[0, place, :], cv_ref[0, place, :], spread_ref, valid
            )
            cc_ref[0, rows, :] = context.astype(bf16)
            log_ref[0, image] = logs

        @pl.when((last > first) & (blocks > 1))
        def _():
            top_ref[...] = jnp.full_like(top_ref, masked)
            sum_ref[...] = jnp.zeros_like(sum_ref)
            out_ref[...] = jnp.zeros_like(out_ref)

            @pl.loop(0, blocks)
            def _(block):
                place, valid = place_at(block)
                kept = pl.ds(pl.multiple_of(block * BLOCK, BLOCK), BLOCK)
                key = ck_ref[0, place, :]
                for pair in range(PAIRS):
                    lanes = slice(2 * QP * pair, 2 * QP * (pair + 1))
                    scores = jnp.where(valid, nt(key, pair_rows(spread_ref, pair)), masked)
                    score_ref[kept, lanes] = scores
                    top = jnp.max(scores, axis=0, keepdims=True)
                    top_ref[:, lanes] = jnp.maximum(top_ref[:, lanes], top)

            @pl.loop(0, blocks)
            def _(block):
                kept = pl.ds(pl.multiple_of(block * BLOCK, BLOCK), BLOCK)
                raised = jnp.exp2((score_ref[kept, :] - top_ref[...]) * (scale * log2e))
                score_ref[kept, :] = raised
                sum_ref[...] += total(raised)

            @pl.loop(0, blocks)
            def _(block):
                place, unused = place_at(block)
                kept = pl.ds(pl.multiple_of(block * BLOCK, BLOCK), BLOCK)
                value_t = cv_ref[0, place, :].T
                for pair in range(PAIRS):
                    lanes = slice(2 * QP * pair, 2 * QP * (pair + 1))
                    attend = (score_ref[kept, lanes] * (1.0 / sum_ref[:, lanes])).astype(bf16)
                    side = slice(2 * HEAD_DIM * pair, 2 * HEAD_DIM * (pair + 1))
                    out_ref[side, :] += pair_blocks(nn(value_t[side, :], attend))

            cc_ref[0, rows, :] = out_ref[...].T.astype(bf16)
            log_ref[0, image] = top_ref[...] * (scale * log2e) + jnp.log2(sum_ref[...])

    for start in range(0, ROWS, CHUNK):
        rows = slice(start, start + CHUNK)
        rows_ref[rows, :] = rows_ref[rows, :] + nn(cc_ref[0, rows, :], w_ref[7]) + bias(5)
    for image in range(IMG_MAX):
        after_ref[0, image * NQ : (image + 1) * NQ, :] = rows_ref[image * QP : image * QP + NQ, :]


def middle_kernel(
    bounds,
    x_ref,
    cot_ref,
    head_cot_ref,
    w_ref,
    small_in_ref,
    head_bias_ref,
    layer_ref,
    grad_ref,
    dw_ref,
    dhead_ref,
    drow_ref,
    small_ref,
    hidden_ref,
    slope_ref,
    dhidden_ref,
    dexpand_ref,
    dshrink_ref,
):
    pack = pl.program_id(0)
    step = pl.program_id(1)
    begin = (pack == 0) & (step == 0)
    finish = (pack == pl.num_programs(0) - 1) & (step == pl.num_programs(1) - 1)

    @pl.when(begin)
    def _():
        small_ref[...] = small_in_ref[0].astype(f32).T
        dw_ref[...] = jnp.zeros_like(dw_ref)
        dhead_ref[...] = jnp.zeros_like(dhead_ref)
        drow_ref[...] = jnp.zeros_like(drow_ref)
        dexpand_ref[...] = jnp.zeros_like(dexpand_ref)
        dshrink_ref[...] = jnp.zeros_like(dshrink_ref)

    def bias(index):
        return small_ref[BIAS + index : BIAS + index + 1, :]

    def gain(index):
        return small_ref[GAIN + index : GAIN + index + 1, :]

    def add_row(column, value):
        row = column - GAIN
        drow_ref[row : row + 1, :] += value

    def columns(block):
        return slice(block * D, (block + 1) * D)

    slot = step * STEP + lax.broadcasted_iota(jnp.int32, (STEP, 1), 0)
    live = (slot < bounds[pack, IMG_MAX + 1] * NQ).astype(f32)

    unit_cross, inverse_cross = norm_parts(x_ref[0])
    after_cross = unit_cross * gain(1) + bias(10)
    after_low = after_cross.astype(bf16)
    for block in range(FF_BLOCKS):
        row = EXPAND_BIAS + block
        pre = nt(after_low, w_ref[EXPAND + block]) + small_ref[row : row + 1, :]
        value, slope = gelu_parts(pre)
        hidden_ref[:, columns(block)] = value.astype(bf16)
        slope_ref[:, columns(block)] = slope
    branch = nn(hidden_ref[...], w_ref[SHRINK : SHRINK + FF_BLOCKS].reshape(-1, D))
    unit_ffn, inverse_ffn = norm_parts(after_cross + branch + bias(6))
    after_ffn = unit_ffn * gain(2) + bias(11)
    layer_ref[0] = (after_ffn * live).astype(bf16)
    unit_last, inverse_last = norm_parts(after_ffn)
    normed = (unit_last * gain(3) + bias(12)).astype(bf16)
    one, one_slope = gelu_parts(nn(normed, w_ref[0]) + bias(7))
    box_one = one.astype(bf16)
    two, two_slope = gelu_parts(nn(box_one, w_ref[1]) + bias(8))
    box_two = two.astype(bf16)
    head_weight = small_in_ref[0, :, 0:POS]
    lane = lax.broadcasted_iota(jnp.int32, (1, POS), 1)
    is_box = (lane >= CLS) & (lane < CLS + 4)
    box = jax.nn.sigmoid(nn(box_two, head_weight) + head_bias_ref[0:1, :])

    head_cot = head_cot_ref[0].astype(f32) * live
    grad_box = jnp.where(is_box, head_cot * box * (1.0 - box), 0.0).astype(bf16)
    grad_logit = jnp.where(lane < CLS, head_cot, 0.0).astype(bf16)
    dw_ref[EXPAND + FF_BLOCKS, 0:1, 0:POS] += total(grad_box.astype(f32)) + total(grad_logit.astype(f32))
    normed_t = normed.T
    grad_two = (two_slope * nt(grad_box, head_weight)).astype(bf16)
    grad_one = (one_slope * nt(grad_two, w_ref[1])).astype(bf16)
    dhead_ref[...] += nn(normed_t, grad_logit) + tn(box_two, grad_box)
    dw_ref[1] += tn(box_one, grad_two)
    dw_ref[0] += nn(normed_t, grad_one)
    add_row(BIAS + 8, total(grad_two.astype(f32)))
    add_row(BIAS + 7, total(grad_one.astype(f32)))
    grad_normed = nt(grad_one, w_ref[0]) + nt(grad_logit, head_weight)
    add_row(GAIN + 3, total(grad_normed * unit_last))
    add_row(BIAS + 12, total(grad_normed))
    grad_after = cot_ref[0].astype(f32) * live + norm_back(
        unit_last, inverse_last, gain(3), grad_normed
    )
    add_row(GAIN + 2, total(grad_after * unit_ffn))
    add_row(BIAS + 11, total(grad_after))
    grad_ffn = norm_back(unit_ffn, inverse_ffn, gain(2), grad_after)
    grad_branch = grad_ffn.astype(bf16)
    add_row(BIAS + 6, total(grad_branch.astype(f32)))
    branch_t = grad_branch.T
    after_t = after_low.T
    for block in range(FF_BLOCKS):
        dhidden = nt(grad_branch, w_ref[SHRINK + block]) * slope_ref[:, columns(block)]
        dpre = dhidden.astype(bf16)
        dhidden_ref[:, columns(block)] = dpre
        add_row(EXPAND_BIAS + block, total(dpre.astype(f32)))
        dshrink_ref[:, columns(block)] += nn(branch_t, hidden_ref[:, columns(block)])
        dexpand_ref[:, columns(block)] += nn(after_t, dpre)
    grad_cross = grad_ffn + nn(
        dhidden_ref[...], w_ref[EXPAND : EXPAND + FF_BLOCKS].reshape(-1, D)
    )
    add_row(GAIN + 1, total(grad_cross * unit_cross))
    add_row(BIAS + 10, total(grad_cross))
    grad_ref[0] = norm_back(unit_cross, inverse_cross, gain(1), grad_cross)

    @pl.when(finish)
    def _():
        for block in range(FF_BLOCKS):
            dw_ref[SHRINK + block] = dshrink_ref[:, columns(block)].T
            dw_ref[EXPAND + block] = dexpand_ref[:, columns(block)].T
        row = dw_ref[EXPAND + FF_BLOCKS, 0:1, :]
        dw_ref[EXPAND + FF_BLOCKS] = jnp.broadcast_to(row, (D, D))


def attend_back(key, value, spread_ref, spread_grad_ref, valid, logs, attend_ref, score_ref):
    key_t = key.T
    parts = []
    for pair in range(PAIRS):
        lanes = slice(2 * QP * pair, 2 * QP * (pair + 1))
        scores = nt(key, pair_rows(spread_ref, pair))
        if logs is None:
            scores = jnp.where(valid, scores, masked)
            top = jnp.max(scores, axis=0, keepdims=True)
            raised = jnp.exp2((scores - top) * (scale * log2e))
            attend = raised * (1.0 / total(raised))
        else:
            attend = jnp.exp2(scores * (scale * log2e) - logs[:, lanes])
            attend = jnp.where(valid, attend, 0.0)
        grad_attend = nt(value, pair_rows(spread_grad_ref, pair))
        row_dot = total(attend * grad_attend)
        grad_scores = (attend * (grad_attend - row_dot)).astype(bf16)
        attend_ref[:, lanes] = attend.astype(bf16)
        score_ref[:, lanes] = grad_scores
        side = slice(2 * HEAD_DIM * pair, 2 * HEAD_DIM * (pair + 1))
        parts.append(pair_blocks(nn(key_t[side, :], grad_scores)))
    return jnp.concatenate(parts, axis=0).T * scale


def late_kernel(
    bounds,
    grad_ref,
    target_ref,
    memory_ref,
    pos_ref,
    w_ref,
    qs_ref,
    ks_ref,
    vs_ref,
    cs_ref,
    inner_ref,
    cq_ref,
    ck_ref,
    cv_ref,
    cc_ref,
    log_ref,
    dhead_ref,
    drow_ref,
    dtarget_ref,
    dmemory_ref,
    dw_ref,
    small_ref,
    flat_ref,
    grad_rows_ref,
    place_ref,
    context_ref,
    gq_ref,
    gk_ref,
    gv_ref,
    dv_ref,
    spread_ref,
    spread_grad_ref,
    attend_ref,
    score_ref,
    long_grad_ref,
    sum_ref,
    out_ref,
    drows_ref,
):
    pack = pl.program_id(0)
    slots = target_ref.shape[1]
    tokens = memory_ref.shape[1]

    @pl.when(pack == 0)
    def _():
        small_ref[...] = w_ref[SMALL].astype(f32).T
        dw_ref[...] = jnp.zeros_like(dw_ref)
        drows_ref[...] = jnp.zeros_like(drows_ref)
        drows_ref[GAIN : GAIN + 32, :] = drow_ref[...]

    def bias(index):
        return small_ref[BIAS + index : BIAS + index + 1, :]

    def gain(index):
        return small_ref[GAIN + index : GAIN + index + 1, :]

    def add_row(row, value):
        drows_ref[row : row + 1, :] += value

    inside = lax.broadcasted_iota(jnp.int32, (QP, 1), 0) < NQ
    position = small_ref[POS : POS + QP, :]
    positions = jnp.concatenate([position] * (CHUNK // QP), axis=0)

    flat_ref[0:slots, :] = grad_ref[0]
    for image in range(IMG_MAX):
        part = flat_ref[image * NQ : image * NQ + QP, :]
        grad_rows_ref[image * QP : (image + 1) * QP, :] = jnp.where(inside, part, 0.0)
    flat_ref[0:slots, :] = target_ref[0].astype(f32)

    for start in range(0, ROWS, CHUNK):
        rows = slice(start, start + CHUNK)
        branch = grad_rows_ref[rows, :].astype(bf16)
        add_row(BIAS + 5, total(branch.astype(f32)))
        dw_ref[7] += tn(cc_ref[0, rows, :], branch)
        context_ref[rows, :] = nt(branch, w_ref[7]).astype(bf16)
    dmemory_ref[...] = jnp.zeros_like(dmemory_ref)
    dv_ref[...] = jnp.zeros_like(dv_ref)

    @pl.loop(0, IMG_MAX)
    def _(image):
        rows = pl.ds(pl.multiple_of(image * QP, QP), QP)
        first = bounds[pack, image]
        last = bounds[pack, image + 1]
        origin = (first // 16) * 16
        blocks = (last - origin + (BLOCK - 1)) // BLOCK
        spread_heads(cq_ref[0, rows, :], spread_ref)
        spread_heads(context_ref[rows, :], spread_grad_ref)
        logs = log_ref[0, image]

        def place_at(block):
            wanted = origin + block * BLOCK
            start = pl.multiple_of(jnp.minimum(wanted, tokens - BLOCK), 16)
            token = start + lax.broadcasted_iota(jnp.int32, (BLOCK, 1), 0)
            valid = (token >= jnp.maximum(first, wanted)) & (token < last)
            return pl.ds(start, BLOCK), valid

        @pl.when(last == first)
        def _():
            gq_ref[rows, :] = jnp.zeros((QP, D), bf16)

        @pl.when((last > first) & (blocks == 1))
        def _():
            place, valid = place_at(0)
            grad_query = attend_back(
                ck_ref[0, place, :],
                cv_ref[0, place, :],
                spread_ref,
                spread_grad_ref,
                valid,
                logs,
                attend_ref,
                score_ref,
            )
            gq_ref[rows, :] = grad_query.astype(bf16)
            dv_ref[place, :] += nn(attend_ref[...], spread_grad_ref[...])
            dmemory_ref[0, place, :] += nn(score_ref[...], spread_ref[...])

        @pl.when((last > first) & (blocks > 1))
        def _():
            sum_ref[...] = jnp.zeros_like(sum_ref)
            out_ref[...] = jnp.zeros_like(out_ref)

            @pl.loop(0, blocks)
            def _(block):
                place, valid = place_at(block)
                kept = pl.ds(pl.multiple_of(block * BLOCK, BLOCK), BLOCK)
                for pair in range(PAIRS):
                    lanes = slice(2 * QP * pair, 2 * QP * (pair + 1))
                    scores = nt(ck_ref[0, place, :], pair_rows(spread_ref, pair))
                    attend = jnp.exp2(scores * (scale * log2e) - logs[:, lanes])
                    attend = jnp.where(valid, attend, 0.0)
                    grad_attend = nt(cv_ref[0, place, :], pair_rows(spread_grad_ref, pair))
                    sum_ref[:, lanes] += total(attend * grad_attend)
                    long_grad_ref[kept, lanes] = grad_attend

            @pl.loop(0, blocks)
            def _(block):
                place, valid = place_at(block)
                kept = pl.ds(pl.multiple_of(block * BLOCK, BLOCK), BLOCK)
                key_t = ck_ref[0, place, :].T
                for pair in range(PAIRS):
                    lanes = slice(2 * QP * pair, 2 * QP * (pair + 1))
                    scores = nt(ck_ref[0, place, :], pair_rows(spread_ref, pair))
                    attend = jnp.exp2(scores * (scale * log2e) - logs[:, lanes])
                    attend = jnp.where(valid, attend, 0.0)
                    grad_scores = attend * (long_grad_ref[kept, lanes] - sum_ref[:, lanes])
                    grad_scores = grad_scores.astype(bf16)
                    attend_ref[:, lanes] = attend.astype(bf16)
                    score_ref[:, lanes] = grad_scores
                    side = slice(2 * HEAD_DIM * pair, 2 * HEAD_DIM * (pair + 1))
                    out_ref[side, :] += pair_blocks(nn(key_t[side, :], grad_scores))
                dv_ref[place, :] += nn(attend_ref[...], spread_grad_ref[...])
                dmemory_ref[0, place, :] += nn(score_ref[...], spread_ref[...])

            gq_ref[rows, :] = (out_ref[...].T * scale).astype(bf16)

    for start in range(0, tokens, CHUNK):
        rows = slice(start, start + CHUNK)
        memory = memory_ref[0, rows, :]
        joined = (memory.astype(f32) + pos_ref[0, rows, :].astype(f32)).astype(bf16)
        grad_key = (dmemory_ref[0, rows, :] * scale).astype(bf16)
        grad_value = dv_ref[rows, :].astype(bf16)
        dmemory_ref[0, rows, :] = nt(grad_key, w_ref[4]) + nt(grad_value, w_ref[5])
        add_row(BIAS + 4, total(grad_value.astype(f32)))
        dw_ref[4] += tn(joined, grad_key)
        dw_ref[5] += tn(memory, grad_value)

    for start in range(0, ROWS, CHUNK):
        rows = slice(start, start + CHUNK)
        unit, inverse = norm_parts(inner_ref[0, rows, :])
        cross_in = (unit * gain(0) + bias(9) + positions).astype(bf16)
        grad_query = gq_ref[rows, :]
        add_row(BIAS + 3, total(grad_query.astype(f32)))
        dw_ref[3] += tn(cross_in, grad_query)
        place = nt(grad_query, w_ref[3])
        place_ref[rows, :] = place
        grad = grad_rows_ref[rows, :] + place
        add_row(GAIN, total(grad * unit))
        add_row(BIAS + 9, total(grad))
        grad = norm_back(unit, inverse, gain(0), grad)
        grad_rows_ref[rows, :] = grad
        branch = grad.astype(bf16)
        add_row(BIAS + 2, total(branch.astype(f32)))
        dw_ref[6] += tn(cs_ref[0, rows, :], branch)
        context_ref[rows, :] = nt(branch, w_ref[6]).astype(bf16)

    @pl.loop(0, IMG_MAX)
    def _(image):
        rows = pl.ds(pl.multiple_of(image * QP, QP), QP)
        spread_heads(qs_ref[0, rows, :], spread_ref)
        spread_heads(context_ref[rows, :], spread_grad_ref)
        grad_query = attend_back(
            ks_ref[0, rows, :],
            vs_ref[0, rows, :],
            spread_ref,
            spread_grad_ref,
            inside,
            None,
            attend_ref.at[0:QP],
            score_ref.at[0:QP],
        )
        gq_ref[rows, :] = grad_query.astype(bf16)
        gv_ref[rows, :] = nn(attend_ref[0:QP, :], spread_grad_ref[...]).astype(bf16)
        gk_ref[rows, :] = (nn(score_ref[0:QP, :], spread_ref[...]) * scale).astype(bf16)

    for start in range(0, ROWS, CHUNK):
        rows = slice(start, start + CHUNK)
        images = range(start // QP, (start + CHUNK) // QP)
        parts = [flat_ref[image * NQ : image * NQ + QP, :] for image in images]
        target = jnp.concatenate([jnp.where(inside, part, 0.0) for part in parts], axis=0)
        joined_t = (target + positions).astype(bf16).T
        grad_query = gq_ref[rows, :]
        grad_key = gk_ref[rows, :]
        grad_value = gv_ref[rows, :]
        add_row(BIAS + 0, total(grad_query.astype(f32)))
        add_row(BIAS + 1, total(grad_value.astype(f32)))
        dw_ref[0] += nn(joined_t, grad_query)
        dw_ref[1] += nn(joined_t, grad_key)
        dw_ref[2] += tn(target.astype(bf16), grad_value)
        grad_joined = nt(grad_query, w_ref[0]) + nt(grad_key, w_ref[1])
        grad_rows_ref[rows, :] += grad_joined + nt(grad_value, w_ref[2])
        grad_place = grad_joined + place_ref[rows, :]
        for image in range(CHUNK // QP):
            drows_ref[POS : POS + QP, :] += grad_place[image * QP : (image + 1) * QP, :]
    for image in range(IMG_MAX):
        part = grad_rows_ref[image * QP : image * QP + NQ, :]
        dtarget_ref[0, image * NQ : (image + 1) * NQ, :] = part

    @pl.when(pack == pl.num_programs(0) - 1)
    def _():
        small = drows_ref[...].T
        dw_ref[SMALL, :, POS:] = small[:, POS:]
        dw_ref[SMALL, :, :POS] = small[:, :POS] + dhead_ref[...]


def whole(shape):
    zeros = (0,) * len(shape)
    return pl.BlockSpec(shape, lambda *unused: zeros)


def by_pack(shape):
    zeros = (0,) * (len(shape) - 1)
    return pl.BlockSpec((1,) + tuple(shape[1:]), lambda pack, *unused: (pack,) + zeros)


def by_step(shape):
    return pl.BlockSpec((1, STEP) + tuple(shape[2:]), lambda pack, step, *unused: (pack, step, 0))


LIMIT = 60 * 1024 * 1024


def params(axes):
    return pltpu.CompilerParams(
        dimension_semantics=("arbitrary",) * axes, vmem_limit_bytes=LIMIT
    )


def early(bounds, target, memory, memory_pos, weights):
    packs, slots, unused = target.shape
    tokens = memory.shape[1]
    low_rows = jax.ShapeDtypeStruct((packs, ROWS, D), bf16)
    low_tokens = jax.ShapeDtypeStruct((packs, tokens, D), bf16)
    outs = [
        jax.ShapeDtypeStruct((packs, slots, D), f32),
        low_rows,
        low_rows,
        low_rows,
        low_rows,
        jax.ShapeDtypeStruct((packs, ROWS, D), f32),
        low_rows,
        low_tokens,
        low_tokens,
        low_rows,
        jax.ShapeDtypeStruct((packs, IMG_MAX, 1, HEADS * QP), f32),
    ]
    wide = HEADS * QP
    return pl.pallas_call(
        early_kernel,
        grid_spec=pltpu.PrefetchScalarGridSpec(
            num_scalar_prefetch=1,
            grid=(packs,),
            in_specs=[
                by_pack(target.shape),
                by_pack(memory.shape),
                by_pack(memory_pos.shape),
                whole(weights.shape),
            ],
            out_specs=[by_pack(out.shape) for out in outs],
            scratch_shapes=[
                pltpu.VMEM((D, D), f32),
                pltpu.VMEM((slots + 32, D), f32),
                pltpu.VMEM((ROWS, D), f32),
                pltpu.VMEM((wide, D), bf16),
                pltpu.VMEM((tokens, wide), f32),
                pltpu.VMEM((1, wide), f32),
                pltpu.VMEM((1, wide), f32),
                pltpu.VMEM((D, QP), f32),
            ],
        ),
        out_shape=outs,
        compiler_params=params(1),
        cost_estimate=pl.CostEstimate(
            flops=packs * 12_000_000_000, bytes_accessed=packs * 14_000_000, transcendentals=0
        ),
        name="early",
    )(bounds, target, memory, memory_pos, weights)


def middle(bounds, x, cotangent, head_cotangent, weights, small, head_bias):
    packs, slots, unused = x.shape
    outs = [
        jax.ShapeDtypeStruct(x.shape, bf16),
        jax.ShapeDtypeStruct(x.shape, f32),
        jax.ShapeDtypeStruct((weights.shape[0] + 1, D, D), f32),
        jax.ShapeDtypeStruct((D, POS), f32),
        jax.ShapeDtypeStruct((32, D), f32),
    ]
    ff = FF_BLOCKS * D
    return pl.pallas_call(
        middle_kernel,
        grid_spec=pltpu.PrefetchScalarGridSpec(
            num_scalar_prefetch=1,
            grid=(packs, slots // STEP),
            in_specs=[
                by_step(x.shape),
                by_step(cotangent.shape),
                by_step(head_cotangent.shape),
                whole(weights.shape),
                pl.BlockSpec((1, D, D), lambda *unused: (SMALL, 0, 0)),
                whole(head_bias.shape),
            ],
            out_specs=[by_step(x.shape), by_step(x.shape)] + [whole(out.shape) for out in outs[2:]],
            scratch_shapes=[
                pltpu.VMEM((D, D), f32),
                pltpu.VMEM((STEP, ff), bf16),
                pltpu.VMEM((STEP, ff), f32),
                pltpu.VMEM((STEP, ff), bf16),
                pltpu.VMEM((D, ff), f32),
                pltpu.VMEM((D, ff), f32),
            ],
        ),
        out_shape=outs,
        compiler_params=params(2),
        cost_estimate=pl.CostEstimate(
            flops=packs * 10_000_000_000, bytes_accessed=packs * 9_000_000, transcendentals=0
        ),
        name="middle",
    )(bounds, x, cotangent, head_cotangent, weights, small, head_bias)


def late(bounds, grad, target, memory, memory_pos, weights, saved, dhead, drow):
    packs, slots, unused = target.shape
    tokens = memory.shape[1]
    outs = [
        jax.ShapeDtypeStruct(target.shape, f32),
        jax.ShapeDtypeStruct(memory.shape, f32),
        jax.ShapeDtypeStruct(weights.shape, f32),
    ]
    wide = HEADS * QP
    return pl.pallas_call(
        late_kernel,
        grid_spec=pltpu.PrefetchScalarGridSpec(
            num_scalar_prefetch=1,
            grid=(packs,),
            in_specs=[
                by_pack(grad.shape),
                by_pack(target.shape),
                by_pack(memory.shape),
                by_pack(memory_pos.shape),
                whole(weights.shape),
            ]
            + [by_pack(array.shape) for array in saved]
            + [whole(dhead.shape), whole(drow.shape)],
            out_specs=[by_pack(outs[0].shape), by_pack(outs[1].shape), whole(weights.shape)],
            scratch_shapes=[
                pltpu.VMEM((D, D), f32),
                pltpu.VMEM((slots + 32, D), f32),
                pltpu.VMEM((ROWS, D), f32),
                pltpu.VMEM((ROWS, D), f32),
                pltpu.VMEM((ROWS, D), bf16),
                pltpu.VMEM((ROWS, D), bf16),
                pltpu.VMEM((ROWS, D), bf16),
                pltpu.VMEM((ROWS, D), bf16),
                pltpu.VMEM((tokens, D), f32),
                pltpu.VMEM((wide, D), bf16),
                pltpu.VMEM((wide, D), bf16),
                pltpu.VMEM((BLOCK, wide), bf16),
                pltpu.VMEM((BLOCK, wide), bf16),
                pltpu.VMEM((tokens, wide), f32),
                pltpu.VMEM((1, wide), f32),
                pltpu.VMEM((D, QP), f32),
                pltpu.VMEM((D, D), f32),
            ],
        ),
        out_shape=outs,
        compiler_params=params(1),
        cost_estimate=pl.CostEstimate(
            flops=packs * 20_000_000_000, bytes_accessed=packs * 18_000_000, transcendentals=0
        ),
        name="late",
    )(bounds, grad, target, memory, memory_pos, weights, *saved, dhead, drow)


def run_of_images(segment):
    edge = jnp.arange(16, dtype=jnp.int32)
    below = segment[:, None, :] < edge[None, :, None]
    counts = jnp.sum(below.astype(jnp.int32), axis=-1)
    images = jnp.max(jnp.where(segment < IMG_MAX, segment + 1, 0), axis=-1)
    return jnp.where(edge[None, :] == IMG_MAX + 1, images[:, None], counts)


def pack_early(project, output, classes, box_final, query_pos, gains, biases, expand_bias):
    share = project.shape[1]
    columns = [
        classes,
        box_final,
        gains.T,
        biases.T,
        expand_bias.reshape(share, FF_BLOCKS),
        jnp.zeros((share, POS - EXPAND_BIAS - FF_BLOCKS), bf16),
        query_pos.T,
        jnp.zeros((share, D - POS - NQ), bf16),
    ]
    small = jnp.concatenate(columns, axis=1)[None]
    return jnp.concatenate([project, output, small], axis=0)


def by_block(hidden_rows):
    share = hidden_rows.shape[0] // FF_BLOCKS
    return hidden_rows.reshape(share, FF_BLOCKS, D).swapaxes(0, 1)


def pack_middle(box, shrink, expand):
    return jnp.concatenate([box, by_block(shrink), by_block(expand.T)], axis=0)


def swap_order(devices):
    bits = [1 << k for k in range(devices.bit_length() - 1)]
    return [bit for bit in bits if bit > 2] + bits[1:2] + bits[0:1]


def swap(value, bit, devices):
    return lax.ppermute(value, AXES, [(k, k ^ bit) for k in range(devices)])


def gather(shard, devices):
    units, share, width = shard.shape
    me = lax.axis_index(AXES)
    order = swap_order(devices)
    held = shard.reshape((units,) + (1,) * len(order) + (share, width))
    for bit in order:
        axis = len(order) - (bit.bit_length() - 1)
        other = swap(held, bit, devices)
        upper = (me & bit) != 0
        low = jnp.where(upper, other, held)
        high = jnp.where(upper, held, other)
        held = jnp.concatenate([low, high], axis=axis)
    return held.reshape(units, devices * share, width)


def scatter(partial, devices):
    units, rows, width = partial.shape
    share = rows // devices
    me = lax.axis_index(AXES)
    order = swap_order(devices)[::-1]
    held = partial.reshape((units,) + (2,) * len(order) + (share, width))
    for bit in order:
        axis = len(order) - (bit.bit_length() - 1)
        mine = (me // bit) % 2
        keep = lax.dynamic_slice_in_dim(held, mine, 1, axis)
        send = lax.dynamic_slice_in_dim(held, 1 - mine, 1, axis).astype(bf16)
        held = keep + swap(send, bit, devices).astype(f32)
    return held.reshape(units, share, width)


def core(
    bounds,
    target,
    memory,
    memory_pos,
    cotangent,
    head_cotangent,
    head_row,
    early_weights,
    middle_weights,
):
    after, *saved = early(bounds, target, memory, memory_pos, early_weights)
    layer, grad, dmiddle, dhead, drow = middle(
        bounds, after, cotangent, head_cotangent, middle_weights, early_weights, head_row
    )
    dtarget, dmemory, dearly = late(
        bounds, grad, target, memory, memory_pos, early_weights, saved, dhead, drow
    )
    return layer, dtarget, dmemory, dearly, dmiddle


def unpack(early_share, middle_share):
    share = early_share.shape[1]

    def from_blocks(units):
        return units.swapaxes(0, 1).reshape(share * FF_BLOCKS, D)

    small = early_share[SMALL]
    return (
        early_share[0:6],
        early_share[6:8],
        from_blocks(middle_share[EXPAND : EXPAND + FF_BLOCKS]).T,
        from_blocks(middle_share[SHRINK : SHRINK + FF_BLOCKS]),
        middle_share[0:2],
        small[:, 0:CLS],
        small[:, CLS : CLS + 4],
        small[:, POS : POS + NQ].T,
        small[:, GAIN : GAIN + 4].T,
        small[:, BIAS : BIAS + 13].T,
        small[:, EXPAND_BIAS : EXPAND_BIAS + FF_BLOCKS].reshape(-1),
        middle_share[EXPAND + FF_BLOCKS, 0, 0 : CLS + 4],
    )


def per_device(
    target,
    memory,
    memory_pos,
    segment,
    project_weight,
    output_weight,
    expand_weight,
    shrink_weight,
    box_weight,
    class_weight,
    box_final,
    query_pos,
    norm_gains,
    biases,
    expand_bias,
    head_bias,
    output_cotangent,
    logit_cotangent,
    box_cotangent,
):
    devices = lax.axis_size(AXES)
    bounds = run_of_images(segment)
    early_weights = gather(
        pack_early(
            project_weight,
            output_weight,
            class_weight,
            box_final,
            query_pos,
            norm_gains,
            biases,
            expand_bias,
        ),
        devices,
    )
    middle_weights = gather(pack_middle(box_weight, shrink_weight, expand_weight), devices)
    packs, slots, unused = target.shape
    rest = POS - CLS - 4
    head_cotangent = jnp.concatenate(
        [logit_cotangent, box_cotangent, jnp.zeros((packs, slots, rest), bf16)], axis=-1
    )
    head_row = jnp.broadcast_to(jnp.pad(head_bias.astype(f32), (0, rest))[None], (8, POS))

    layer, dtarget, dmemory, dearly, dmiddle = core(
        bounds,
        target,
        memory,
        memory_pos,
        output_cotangent,
        head_cotangent,
        head_row,
        early_weights,
        middle_weights,
    )
    middle_share = scatter(dmiddle, devices)
    early_share = scatter(dearly, devices)
    return (layer, dtarget, dmemory) + unpack(early_share, middle_share)


def solution(mesh):
    both = ("dp", "fsdp")
    by_rows = P(both, None, None)
    return jax.shard_map(
        per_device,
        mesh=mesh,
        in_specs=(
            by_rows,
            by_rows,
            by_rows,
            P(both, None),
            P(None, both, None),
            P(None, both, None),
            P(None, both),
            P(both, None),
            P(None, both, None),
            P(both, None),
            P(both, None),
            P(None, both),
            P(None, both),
            P(None, both),
            P(both),
            P(),
            by_rows,
            by_rows,
            by_rows,
        ),
        out_specs=(
            by_rows,
            by_rows,
            by_rows,
            P(None, both, None),
            P(None, both, None),
            P(None, both),
            P(both, None),
            P(None, both, None),
            P(both, None),
            P(both, None),
            P(None, both),
            P(None, both),
            P(None, both),
            P(both),
            P(),
        ),
        check_vma=False,
    )
```

```python
import functools

import jax
import jax.numpy as jnp
from jax import lax
from jax.experimental import pallas as pl
from jax.experimental.pallas import tpu as pltpu
from jax.sharding import PartitionSpec as P

D = 256
HEADS = 8
NQ = 100
CLS = 92
IMG_MAX = 12
HEAD_DIM = 32
QP = 128
ROWS = IMG_MAX * QP
PAIRS = HEADS // 2
BLOCK = 256
SIZES = (128, 192, 256, 384, 512)
CHUNK = 512
STEP = 400
FF_BLOCKS = 8
GAIN = 96
BIAS = 100
POS = 128
SMALL = 8
EXTRA = 16

epsilon = 1e-05
masked = -1000000000.0
scale = HEAD_DIM ** (-0.5)
log2e = 1.4426950408889634
gelu_a = 0.7978845608028654
gelu_b = gelu_a * 0.044715
AXES = ("dp", "fsdp")
f32 = jnp.float32
bf16 = jnp.bfloat16


def nn(left, right):
    return jnp.dot(left, right, preferred_element_type=f32)


def nt(left, right):
    return lax.dot_general(left, right, (((1,), (1,)), ((), ())), preferred_element_type=f32)


def tn(left, right):
    return lax.dot_general(left, right, (((0,), (0,)), ((), ())), preferred_element_type=f32)


def total(value):
    return jnp.sum(value, axis=0, keepdims=True)


def norm_parts(value):
    middle = jnp.mean(value, axis=-1, keepdims=True)
    centered = value - middle
    spread = jnp.mean(centered * centered, axis=-1, keepdims=True)
    inverse = lax.rsqrt(spread + epsilon)
    return centered * inverse, inverse


def norm_back(unit, inverse, gain, grad):
    scaled = grad * gain
    first = jnp.mean(scaled, axis=-1, keepdims=True)
    second = jnp.mean(scaled * unit, axis=-1, keepdims=True)
    return inverse * (scaled - first - unit * second)


def gelu_parts(value):
    square = value * value
    cdf = 0.5 + 0.5 * jnp.tanh(value * (gelu_a + gelu_b * square))
    result = value * cdf
    slope = cdf + (result - result * cdf) * (2.0 * gelu_a + 6.0 * gelu_b * square)
    return result, slope


def spread_heads(value, spread_ref):
    lane = lax.broadcasted_iota(jnp.int32, (1, D), 1) // HEAD_DIM
    for head in range(HEADS):
        keep = (lane == head).astype(f32).astype(bf16)
        spread_ref[head * QP : (head + 1) * QP, :] = value * keep


def pair_rows(ref, pair):
    side = pair // 2 * (D // 2)
    return ref[2 * QP * pair : 2 * QP * (pair + 1), side : side + D // 2]


def long_rows(ref, pair):
    return ref[2 * QP * pair : 2 * QP * (pair + 1), :]


def head_lane(lanes):
    return lax.broadcasted_iota(jnp.int32, (1, lanes), 1) // HEAD_DIM


def join_pairs(products):
    lane = head_lane(D)
    result = products[0][:QP]
    for head in range(1, HEADS):
        part = products[head // 2][(head % 2) * QP : (head % 2 + 1) * QP]
        result = jnp.where(lane == head, part, result)
    return result


def join_halves(products):
    lane = head_lane(D // 2)
    halves = []
    for half in range(2):
        low, high = products[2 * half : 2 * half + 2]
        part = jnp.where(lane == 2, high[:QP], high[QP:])
        part = jnp.where(lane == 1, low[QP:], part)
        halves.append(jnp.where(lane == 0, low[:QP], part))
    return jnp.concatenate(halves, axis=1)


def half_lanes(value, pair):
    side = pair // 2 * (D // 2)
    return value[:, side : side + D // 2]


def attend_block(key, value, spread_ref, valid, halves):
    scores = [nt(half_lanes(key, pair), pair_rows(spread_ref, pair)) for pair in range(PAIRS)]
    attends = []
    logs = []
    for pair in range(PAIRS):
        kept = jnp.where(valid, scores[pair], masked)
        top = jnp.max(kept, axis=0, keepdims=True)
        raised = jnp.exp2((kept - top) * (scale * log2e))
        sums = total(raised)
        attends.append((raised * (1.0 / sums)).astype(bf16))
        logs.append(top * (scale * log2e) + jnp.log2(sums))
    if halves:
        products = [tn(attends[pair], half_lanes(value, pair)) for pair in range(PAIRS)]
        context = join_halves(products)
    else:
        context = join_pairs([tn(attends[pair], value) for pair in range(PAIRS)])
    return context, jnp.concatenate(logs, axis=1)


def early_kernel(
    bounds,
    target_ref,
    memory_ref,
    pos_ref,
    w_ref,
    after_ref,
    qs_ref,
    ks_ref,
    vs_ref,
    cs_ref,
    inner_ref,
    cq_ref,
    ck_ref,
    cv_ref,
    cc_ref,
    log_ref,
    small_ref,
    flat_ref,
    rows_ref,
    spread_ref,
    score_ref,
    top_ref,
    sum_ref,
    out_ref,
):
    pack = pl.program_id(0)
    slots = target_ref.shape[1]
    tokens = memory_ref.shape[1]

    @pl.when(pack == 0)
    def _():
        small_ref[...] = w_ref[SMALL].astype(f32).T

    def bias(index):
        return small_ref[BIAS + index : BIAS + index + 1, :]

    def gain(index):
        return small_ref[GAIN + index : GAIN + index + 1, :]

    inside = lax.broadcasted_iota(jnp.int32, (QP, 1), 0) < NQ
    position = small_ref[POS : POS + QP, :]
    positions = jnp.concatenate([position] * (CHUNK // QP), axis=0)

    value_sum = jnp.zeros((1, D), f32)
    for start in range(0, tokens, CHUNK):
        rows = slice(start, start + CHUNK)
        memory = memory_ref[0, rows, :]
        joined = (memory.astype(f32) + pos_ref[0, rows, :].astype(f32)).astype(bf16)
        ck_ref[0, rows, :] = nn(joined, w_ref[4]).astype(bf16)
        value = (nn(memory, w_ref[5]) + bias(4)).astype(bf16)
        cv_ref[0, rows, :] = value
        value_sum += total(value.astype(f32))
    value_mean = value_sum * (1.0 / tokens)

    flat_ref[0:slots, :] = target_ref[0].astype(f32)
    for image in range(IMG_MAX):
        part = flat_ref[image * NQ : image * NQ + QP, :]
        rows_ref[image * QP : (image + 1) * QP, :] = jnp.where(inside, part, 0.0)

    for start in range(0, ROWS, CHUNK):
        rows = slice(start, start + CHUNK)
        target = rows_ref[rows, :]
        joined = (target + positions).astype(bf16)
        qs_ref[0, rows, :] = (nn(joined, w_ref[0]) + bias(0)).astype(bf16)
        ks_ref[0, rows, :] = nn(joined, w_ref[1]).astype(bf16)
        vs_ref[0, rows, :] = (nn(target.astype(bf16), w_ref[2]) + bias(1)).astype(bf16)

    @pl.loop(0, IMG_MAX // 2)
    def _(step):
        for turn in range(2):
            rows = pl.ds(pl.multiple_of((2 * step + turn) * QP, QP), QP)
            spread = spread_ref.at[turn]
            spread_heads(qs_ref[0, rows, :], spread)
            context, unused = attend_block(
                ks_ref[0, rows, :], vs_ref[0, rows, :], spread, inside, True
            )
            cs_ref[0, rows, :] = context.astype(bf16)

    for start in range(0, ROWS, CHUNK):
        rows = slice(start, start + CHUNK)
        value = rows_ref[rows, :] + nn(cs_ref[0, rows, :], w_ref[6]) + bias(2)
        inner_ref[0, rows, :] = value
        unit, unused = norm_parts(value)
        after = unit * gain(0) + bias(9)
        rows_ref[rows, :] = after
        query = nn((after + positions).astype(bf16), w_ref[3]) + bias(3)
        cq_ref[0, rows, :] = query.astype(bf16)

    @pl.loop(0, IMG_MAX)
    def _(image):
        rows = pl.ds(pl.multiple_of(image * QP, QP), QP)
        first = bounds[pack, image]
        last = bounds[pack, image + 1]
        origin = (first // 16) * 16
        blocks = (last - origin + (BLOCK - 1)) // BLOCK
        spread = spread_ref.at[0]
        spread_heads(cq_ref[0, rows, :], spread)

        def place_at(block, size=BLOCK):
            wanted = origin + block * size
            start = pl.multiple_of(jnp.minimum(wanted, tokens - size), 16)
            token = start + lax.broadcasted_iota(jnp.int32, (size, 1), 0)
            valid = (token >= jnp.maximum(first, wanted)) & (token < last)
            return pl.ds(start, size), valid

        def fits(index):
            below = SIZES[index - 1] if index else 0
            return (last > first) & (last - origin > below) & (last - origin <= SIZES[index])

        @pl.when(last == first)
        def _():
            cc_ref[0, rows, :] = jnp.broadcast_to(value_mean, (QP, D)).astype(bf16)
            log_ref[0, image] = jnp.zeros((1, HEADS * QP), f32)

        def in_one(size):
            place, valid = place_at(0, size)
            context, logs = attend_block(
                ck_ref[0, place, :], cv_ref[0, place, :], spread, valid, False
            )
            cc_ref[0, rows, :] = context.astype(bf16)
            log_ref[0, image] = logs

        for index, size in enumerate(SIZES):
            pl.when(fits(index))(functools.partial(in_one, size))

        @pl.when(last - origin > SIZES[-1])
        def _():
            top_ref[...] = jnp.full_like(top_ref, masked)
            sum_ref[...] = jnp.zeros_like(sum_ref)
            out_ref[...] = jnp.zeros_like(out_ref)

            @pl.loop(0, blocks)
            def _(block):
                place, valid = place_at(block)
                kept = pl.ds(pl.multiple_of(block * BLOCK, BLOCK), BLOCK)
                key = ck_ref[0, place, :]
                for pair in range(PAIRS):
                    lanes = slice(2 * QP * pair, 2 * QP * (pair + 1))
                    scores = jnp.where(valid, nt(key, long_rows(spread, pair)), masked)
                    score_ref[kept, lanes] = scores
                    top = jnp.max(scores, axis=0, keepdims=True)
                    top_ref[:, lanes] = jnp.maximum(top_ref[:, lanes], top)

            @pl.loop(0, blocks)
            def _(block):
                kept = pl.ds(pl.multiple_of(block * BLOCK, BLOCK), BLOCK)
                raised = jnp.exp2((score_ref[kept, :] - top_ref[...]) * (scale * log2e))
                score_ref[kept, :] = raised
                sum_ref[...] += total(raised)

            @pl.loop(0, blocks)
            def _(block):
                place, unused = place_at(block)
                kept = pl.ds(pl.multiple_of(block * BLOCK, BLOCK), BLOCK)
                value = cv_ref[0, place, :]
                products = []
                for pair in range(PAIRS):
                    lanes = slice(2 * QP * pair, 2 * QP * (pair + 1))
                    attend = (score_ref[kept, lanes] * (1.0 / sum_ref[:, lanes])).astype(bf16)
                    products.append(tn(attend, value))
                out_ref[...] += join_pairs(products)

            cc_ref[0, rows, :] = out_ref[...].astype(bf16)
            log_ref[0, image] = top_ref[...] * (scale * log2e) + jnp.log2(sum_ref[...])

    for start in range(0, ROWS, CHUNK):
        rows = slice(start, start + CHUNK)
        rows_ref[rows, :] = rows_ref[rows, :] + nn(cc_ref[0, rows, :], w_ref[7]) + bias(5)
    for image in range(IMG_MAX):
        after_ref[0, image * NQ : (image + 1) * NQ, :] = rows_ref[image * QP : image * QP + NQ, :]


def middle_kernel(
    bounds,
    x_ref,
    cot_ref,
    head_cot_ref,
    ff_ref,
    small_in_ref,
    head_bias_ref,
    layer_ref,
    grad_ref,
    dff_ref,
    dhead_ref,
    drow_ref,
    small_ref,
    bias_ref,
    box_ref,
    low_ref,
    cross_ref,
    sum_ref,
    branch_ref,
    hidden_ref,
    slope_ref,
    dpre_ref,
):
    pack = pl.program_id(0)
    slots = x_ref.shape[1]
    parts = ff_ref.shape[0]
    ff = FF_BLOCKS * D // parts
    share = D // parts
    near = D // ff
    boxes = 2 * ff
    extra = 2 * ff + 2 * share

    @pl.when(pack == 0)
    def _():
        small_ref[...] = small_in_ref[0].astype(f32).T
        pair = ff_ref[:, boxes:extra, :].astype(f32)
        box_ref[0] = pair[:, :share].reshape(D, D).astype(bf16)
        box_ref[1] = pair[:, share:].reshape(D, D).astype(bf16)
        for block in range(FF_BLOCKS):
            rows = [ff_ref[block * near + k, extra : extra + 16, :] for k in range(near)]
            rows = [row.astype(f32)[1:2, 0:ff] for row in rows]
            bias_ref[block] = jnp.concatenate(rows, axis=1)
        bias_ref[FF_BLOCKS:] = jnp.zeros((FF_BLOCKS, 1, D), f32)
        dff_ref[...] = jnp.zeros_like(dff_ref)
        dhead_ref[...] = jnp.zeros_like(dhead_ref)
        drow_ref[...] = jnp.zeros_like(drow_ref)

    def bias(index):
        return small_ref[BIAS + index : BIAS + index + 1, :]

    def gain(index):
        return small_ref[GAIN + index : GAIN + index + 1, :]

    def add_row(column, value):
        row = column - GAIN
        drow_ref[row : row + 1, :] += value

    def near_block(block):
        return pl.ds(block * near, near)

    def shrink(block):
        return ff_ref[near_block(block), 0:ff, :].reshape(D, D)

    def expand(block):
        return ff_ref[near_block(block), ff:boxes, :].reshape(D, D)

    for start in range(0, slots, STEP):
        rows = slice(start, start + STEP)
        unit, unused = norm_parts(x_ref[0, rows, :])
        after_cross = unit * gain(1) + bias(10)
        cross_ref[rows, :] = after_cross
        low_ref[rows, :] = after_cross.astype(bf16)

    def hide(block):
        value, slope = gelu_parts(nt(low_ref[...], expand(block)) + bias_ref[block])
        hidden_ref[block] = value.astype(bf16)
        slope_ref[block] = slope

    hide(0)
    sum_ref[...] = cross_ref[...] + bias(6)

    @pl.loop(1, FF_BLOCKS)
    def _(block):
        sum_ref[...] += nn(hidden_ref[block - 1], shrink(block - 1))
        hide(block)

    sum_ref[...] += nn(hidden_ref[FF_BLOCKS - 1], shrink(FF_BLOCKS - 1))

    head_weight = small_in_ref[0, :, 0:POS]
    lane = lax.broadcasted_iota(jnp.int32, (1, POS), 1)
    is_box = (lane >= CLS) & (lane < CLS + 4)
    for start in range(0, slots, STEP):
        rows = slice(start, start + STEP)
        slot = start + lax.broadcasted_iota(jnp.int32, (STEP, 1), 0)
        live = (slot < bounds[pack, IMG_MAX + 1] * NQ).astype(f32)
        unit_ffn, inverse_ffn = norm_parts(sum_ref[rows, :])
        after_ffn = unit_ffn * gain(2) + bias(11)
        layer_ref[0, rows, :] = (after_ffn * live).astype(bf16)
        unit_last, inverse_last = norm_parts(after_ffn)
        normed = (unit_last * gain(3) + bias(12)).astype(bf16)
        one, one_slope = gelu_parts(nn(normed, box_ref[0]) + bias(7))
        box_one = one.astype(bf16)
        two, two_slope = gelu_parts(nn(box_one, box_ref[1]) + bias(8))
        box_two = two.astype(bf16)
        box = jax.nn.sigmoid(nn(box_two, head_weight) + head_bias_ref[0:1, :])

        head_cot = head_cot_ref[0, rows, :].astype(f32) * live
        grad_box = jnp.where(is_box, head_cot * box * (1.0 - box), 0.0).astype(bf16)
        grad_logit = jnp.where(lane < CLS, head_cot, 0.0).astype(bf16)
        drow_ref[31:32, 0:POS] += total(grad_box.astype(f32)) + total(grad_logit.astype(f32))
        normed_t = normed.T
        grad_two = (two_slope * nt(grad_box, head_weight)).astype(bf16)
        grad_one = (one_slope * nt(grad_two, box_ref[1])).astype(bf16)
        dhead_ref[...] += nn(normed_t, grad_logit) + tn(box_two, grad_box)
        dff_ref[:, boxes : boxes + share, :] += nn(normed_t, grad_one).reshape(parts, share, D)
        dff_ref[:, boxes + share : extra, :] += tn(box_one, grad_two).reshape(parts, share, D)
        add_row(BIAS + 8, total(grad_two.astype(f32)))
        add_row(BIAS + 7, total(grad_one.astype(f32)))
        grad_normed = nt(grad_one, box_ref[0]) + nt(grad_logit, head_weight)
        add_row(GAIN + 3, total(grad_normed * unit_last))
        add_row(BIAS + 12, total(grad_normed))
        grad_after = cot_ref[0, rows, :].astype(f32) * live + norm_back(
            unit_last, inverse_last, gain(3), grad_normed
        )
        add_row(GAIN + 2, total(grad_after * unit_ffn))
        add_row(BIAS + 11, total(grad_after))
        grad_ffn = norm_back(unit_ffn, inverse_ffn, gain(2), grad_after)
        grad_branch = grad_ffn.astype(bf16)
        add_row(BIAS + 6, total(grad_branch.astype(f32)))
        sum_ref[rows, :] = grad_ffn
        branch_ref[rows, :] = grad_branch

    @pl.loop(0, FF_BLOCKS)
    def _(block):
        branch = branch_ref[...]
        dpre = (nt(branch, shrink(block)) * slope_ref[block]).astype(bf16)
        dpre_ref[block] = dpre
        bias_ref[FF_BLOCKS + block] += total(dpre.astype(f32))
        dshrink = tn(hidden_ref[block], branch).reshape(near, ff, D)
        dff_ref[near_block(block), 0:ff, :] += dshrink
        dexpand = tn(dpre, low_ref[...]).reshape(near, ff, D)
        dff_ref[near_block(block), ff:boxes, :] += dexpand

    grad_cross = sum_ref[...]
    for block in range(FF_BLOCKS):
        grad_cross += nn(dpre_ref[block], expand(block))
    sum_ref[...] = grad_cross
    for start in range(0, slots, STEP):
        rows = slice(start, start + STEP)
        unit, inverse = norm_parts(x_ref[0, rows, :])
        grad = sum_ref[rows, :]
        add_row(GAIN + 1, total(grad * unit))
        add_row(BIAS + 10, total(grad))
        grad_ref[0, rows, :] = norm_back(unit, inverse, gain(1), grad)

    @pl.when(pack == pl.num_programs(0) - 1)
    def _():
        for part in range(parts):
            dff_ref[part, extra : extra + 1, :] = drow_ref[31:32, :]
            side = part % near * ff
            values = bias_ref[FF_BLOCKS + part // near][:, side : side + ff]
            dff_ref[part, extra + 1 : extra + 2, 0:ff] = values


def attend_back(key, value, spread, spread_grad, valid, logs, attend_ref, score_ref):
    scores = [nt(half_lanes(key, pair), pair_rows(spread, pair)) for pair in range(PAIRS)]
    grads = [nt(half_lanes(value, pair), pair_rows(spread_grad, pair)) for pair in range(PAIRS)]
    lows = []
    for pair in range(PAIRS):
        lanes = slice(2 * QP * pair, 2 * QP * (pair + 1))
        if logs is None:
            kept = jnp.where(valid, scores[pair], masked)
            top = jnp.max(kept, axis=0, keepdims=True)
            raised = jnp.exp2((kept - top) * (scale * log2e))
            attend = raised * (1.0 / total(raised))
        else:
            attend = jnp.exp2(scores[pair] * (scale * log2e) - logs[:, lanes])
            attend = jnp.where(valid, attend, 0.0)
        row_dot = total(attend * grads[pair])
        low = (attend * (grads[pair] - row_dot)).astype(bf16)
        attend_ref[:, lanes] = attend.astype(bf16)
        score_ref[:, lanes] = low
        lows.append(low)
    return join_halves([tn(lows[pair], half_lanes(key, pair)) for pair in range(PAIRS)]) * scale


def late_kernel(
    bounds,
    grad_ref,
    target_ref,
    memory_ref,
    pos_ref,
    w_ref,
    qs_ref,
    ks_ref,
    vs_ref,
    cs_ref,
    inner_ref,
    cq_ref,
    ck_ref,
    cv_ref,
    cc_ref,
    log_ref,
    dhead_ref,
    drow_ref,
    dtarget_ref,
    dmemory_ref,
    dw_ref,
    small_ref,
    flat_ref,
    grad_rows_ref,
    place_ref,
    context_ref,
    gq_ref,
    gk_ref,
    gv_ref,
    dv_ref,
    spread_ref,
    spread_grad_ref,
    attend_ref,
    score_ref,
    sum_ref,
    out_ref,
    drows_ref,
):
    pack = pl.program_id(0)
    slots = target_ref.shape[1]
    tokens = memory_ref.shape[1]

    @pl.when(pack == 0)
    def _():
        small_ref[...] = w_ref[SMALL].astype(f32).T
        dw_ref[...] = jnp.zeros_like(dw_ref)
        drows_ref[...] = jnp.zeros_like(drows_ref)
        drows_ref[GAIN : GAIN + 32, :] = drow_ref[...]

    def bias(index):
        return small_ref[BIAS + index : BIAS + index + 1, :]

    def gain(index):
        return small_ref[GAIN + index : GAIN + index + 1, :]

    def add_row(row, value):
        drows_ref[row : row + 1, :] += value

    inside = lax.broadcasted_iota(jnp.int32, (QP, 1), 0) < NQ
    position = small_ref[POS : POS + QP, :]
    positions = jnp.concatenate([position] * (CHUNK // QP), axis=0)

    flat_ref[0:slots, :] = grad_ref[0]
    for image in range(IMG_MAX):
        part = flat_ref[image * NQ : image * NQ + QP, :]
        grad_rows_ref[image * QP : (image + 1) * QP, :] = jnp.where(inside, part, 0.0)
    flat_ref[0:slots, :] = target_ref[0].astype(f32)

    for start in range(0, ROWS, CHUNK):
        rows = slice(start, start + CHUNK)
        branch = grad_rows_ref[rows, :].astype(bf16)
        add_row(BIAS + 5, total(branch.astype(f32)))
        dw_ref[7] += tn(cc_ref[0, rows, :], branch)
        context_ref[rows, :] = nt(branch, w_ref[7]).astype(bf16)
    dmemory_ref[...] = jnp.zeros_like(dmemory_ref)
    dv_ref[...] = jnp.zeros_like(dv_ref)

    @pl.loop(0, IMG_MAX)
    def _(image):
        rows = pl.ds(pl.multiple_of(image * QP, QP), QP)
        first = bounds[pack, image]
        last = bounds[pack, image + 1]
        origin = (first // 16) * 16
        blocks = (last - origin + (BLOCK - 1)) // BLOCK
        spread = spread_ref.at[0]
        spread_grad = spread_grad_ref.at[0]
        attend_low = attend_ref
        score_low = score_ref
        spread_heads(cq_ref[0, rows, :], spread)
        spread_heads(context_ref[rows, :], spread_grad)
        logs = log_ref[0, image]

        def place_at(block, size=BLOCK):
            wanted = origin + block * size
            start = pl.multiple_of(jnp.minimum(wanted, tokens - size), 16)
            token = start + lax.broadcasted_iota(jnp.int32, (size, 1), 0)
            valid = (token >= jnp.maximum(first, wanted)) & (token < last)
            return pl.ds(start, size), valid

        def fits(index):
            below = SIZES[index - 1] if index else 0
            return (last > first) & (last - origin > below) & (last - origin <= SIZES[index])

        @pl.when(last == first)
        def _():
            gq_ref[rows, :] = jnp.zeros((QP, D), bf16)

        def in_one(size):
            place, valid = place_at(0, size)
            attend_part = attend_low.at[0:size]
            score_part = score_low.at[0:size]
            grad_query = attend_back(
                ck_ref[0, place, :],
                cv_ref[0, place, :],
                spread,
                spread_grad,
                valid,
                logs,
                attend_part,
                score_part,
            )
            gq_ref[rows, :] = grad_query.astype(bf16)
            dv_ref[place, :] += nn(attend_part[...], spread_grad[...])
            dmemory_ref[0, place, :] += nn(score_part[...], spread[...])

        for index, size in enumerate(SIZES):
            pl.when(fits(index))(functools.partial(in_one, size))

        @pl.when(last - origin > SIZES[-1])
        def _():
            sum_ref[...] = jnp.zeros_like(sum_ref)
            out_ref[...] = jnp.zeros_like(out_ref)

            @pl.loop(0, blocks)
            def _(block):
                place, valid = place_at(block)
                for pair in range(PAIRS):
                    lanes = slice(2 * QP * pair, 2 * QP * (pair + 1))
                    scores = nt(ck_ref[0, place, :], long_rows(spread, pair))
                    attend = jnp.exp2(scores * (scale * log2e) - logs[:, lanes])
                    attend = jnp.where(valid, attend, 0.0)
                    grad_attend = nt(cv_ref[0, place, :], long_rows(spread_grad, pair))
                    sum_ref[:, lanes] += total(attend * grad_attend)

            @pl.loop(0, blocks)
            def _(block):
                place, valid = place_at(block)
                key = ck_ref[0, place, :]
                products = []
                for pair in range(PAIRS):
                    lanes = slice(2 * QP * pair, 2 * QP * (pair + 1))
                    scores = nt(ck_ref[0, place, :], long_rows(spread, pair))
                    attend = jnp.exp2(scores * (scale * log2e) - logs[:, lanes])
                    attend = jnp.where(valid, attend, 0.0)
                    grad_attend = nt(cv_ref[0, place, :], long_rows(spread_grad, pair))
                    grad_scores = attend * (grad_attend - sum_ref[:, lanes])
                    grad_scores = grad_scores.astype(bf16)
                    attend_low[0:BLOCK, lanes] = attend.astype(bf16)
                    score_low[0:BLOCK, lanes] = grad_scores
                    products.append(tn(grad_scores, half_lanes(key, pair)))
                out_ref[...] += join_halves(products)
                dv_ref[place, :] += nn(attend_low[0:BLOCK, :], spread_grad[...])
                dmemory_ref[0, place, :] += nn(score_low[0:BLOCK, :], spread[...])

            gq_ref[rows, :] = (out_ref[...] * scale).astype(bf16)

    for start in range(0, tokens, CHUNK):
        rows = slice(start, start + CHUNK)
        memory = memory_ref[0, rows, :]
        joined = (memory.astype(f32) + pos_ref[0, rows, :].astype(f32)).astype(bf16)
        grad_key = (dmemory_ref[0, rows, :] * scale).astype(bf16)
        grad_value = dv_ref[rows, :].astype(bf16)
        dmemory_ref[0, rows, :] = nt(grad_key, w_ref[4]) + nt(grad_value, w_ref[5])
        add_row(BIAS + 4, total(grad_value.astype(f32)))
        dw_ref[4] += tn(joined, grad_key)
        dw_ref[5] += tn(memory, grad_value)

    for start in range(0, ROWS, CHUNK):
        rows = slice(start, start + CHUNK)
        unit, inverse = norm_parts(inner_ref[0, rows, :])
        cross_in = (unit * gain(0) + bias(9) + positions).astype(bf16)
        grad_query = gq_ref[rows, :]
        add_row(BIAS + 3, total(grad_query.astype(f32)))
        dw_ref[3] += tn(cross_in, grad_query)
        place = nt(grad_query, w_ref[3])
        place_ref[rows, :] = place
        grad = grad_rows_ref[rows, :] + place
        add_row(GAIN, total(grad * unit))
        add_row(BIAS + 9, total(grad))
        grad = norm_back(unit, inverse, gain(0), grad)
        grad_rows_ref[rows, :] = grad
        branch = grad.astype(bf16)
        add_row(BIAS + 2, total(branch.astype(f32)))
        dw_ref[6] += tn(cs_ref[0, rows, :], branch)
        context_ref[rows, :] = nt(branch, w_ref[6]).astype(bf16)

    @pl.loop(0, IMG_MAX // 2)
    def _(step):
        for turn in range(2):
            rows = pl.ds(pl.multiple_of((2 * step + turn) * QP, QP), QP)
            spread = spread_ref.at[turn]
            spread_grad = spread_grad_ref.at[turn]
            attend_low = attend_ref.at[turn * QP : (turn + 1) * QP]
            score_low = score_ref.at[turn * QP : (turn + 1) * QP]
            spread_heads(qs_ref[0, rows, :], spread)
            spread_heads(context_ref[rows, :], spread_grad)
            grad_query = attend_back(
                ks_ref[0, rows, :],
                vs_ref[0, rows, :],
                spread,
                spread_grad,
                inside,
                None,
                attend_low,
                score_low,
            )
            gq_ref[rows, :] = grad_query.astype(bf16)
            gv_ref[rows, :] = nn(attend_low[...], spread_grad[...]).astype(bf16)
            gk_ref[rows, :] = (nn(score_low[...], spread[...]) * scale).astype(bf16)

    for start in range(0, ROWS, CHUNK):
        rows = slice(start, start + CHUNK)
        images = range(start // QP, (start + CHUNK) // QP)
        parts = [flat_ref[image * NQ : image * NQ + QP, :] for image in images]
        target = jnp.concatenate([jnp.where(inside, part, 0.0) for part in parts], axis=0)
        joined_t = (target + positions).astype(bf16).T
        grad_query = gq_ref[rows, :]
        grad_key = gk_ref[rows, :]
        grad_value = gv_ref[rows, :]
        add_row(BIAS + 0, total(grad_query.astype(f32)))
        add_row(BIAS + 1, total(grad_value.astype(f32)))
        dw_ref[0] += nn(joined_t, grad_query)
        dw_ref[1] += nn(joined_t, grad_key)
        dw_ref[2] += tn(target.astype(bf16), grad_value)
        grad_joined = nt(grad_query, w_ref[0]) + nt(grad_key, w_ref[1])
        grad_rows_ref[rows, :] += grad_joined + nt(grad_value, w_ref[2])
        grad_place = grad_joined + place_ref[rows, :]
        for image in range(CHUNK // QP):
            drows_ref[POS : POS + QP, :] += grad_place[image * QP : (image + 1) * QP, :]
    for image in range(IMG_MAX):
        part = grad_rows_ref[image * QP : image * QP + NQ, :]
        dtarget_ref[0, image * NQ : (image + 1) * NQ, :] = part

    @pl.when(pack == pl.num_programs(0) - 1)
    def _():
        small = drows_ref[...].T
        dw_ref[SMALL, :, POS:] = small[:, POS:]
        dw_ref[SMALL, :, :POS] = small[:, :POS] + dhead_ref[...]


def whole(shape):
    zeros = (0,) * len(shape)
    return pl.BlockSpec(shape, lambda *unused: zeros)


def by_pack(shape):
    zeros = (0,) * (len(shape) - 1)
    return pl.BlockSpec((1,) + tuple(shape[1:]), lambda pack, *unused: (pack,) + zeros)


LIMIT = 60 * 1024 * 1024


def params(axes):
    return pltpu.CompilerParams(
        dimension_semantics=("arbitrary",) * axes, vmem_limit_bytes=LIMIT
    )


def early(bounds, target, memory, memory_pos, weights):
    packs, slots, unused = target.shape
    tokens = memory.shape[1]
    low_rows = jax.ShapeDtypeStruct((packs, ROWS, D), bf16)
    low_tokens = jax.ShapeDtypeStruct((packs, tokens, D), bf16)
    outs = [
        jax.ShapeDtypeStruct((packs, slots, D), f32),
        low_rows,
        low_rows,
        low_rows,
        low_rows,
        jax.ShapeDtypeStruct((packs, ROWS, D), f32),
        low_rows,
        low_tokens,
        low_tokens,
        low_rows,
        jax.ShapeDtypeStruct((packs, IMG_MAX, 1, HEADS * QP), f32),
    ]
    wide = HEADS * QP
    return pl.pallas_call(
        early_kernel,
        grid_spec=pltpu.PrefetchScalarGridSpec(
            num_scalar_prefetch=1,
            grid=(packs,),
            in_specs=[
                by_pack(target.shape),
                by_pack(memory.shape),
                by_pack(memory_pos.shape),
                whole(weights.shape),
            ],
            out_specs=[by_pack(out.shape) for out in outs],
            scratch_shapes=[
                pltpu.VMEM((D, D), f32),
                pltpu.VMEM((slots + 32, D), f32),
                pltpu.VMEM((ROWS, D), f32),
                pltpu.VMEM((2, wide, D), bf16),
                pltpu.VMEM((tokens, wide), f32),
                pltpu.VMEM((1, wide), f32),
                pltpu.VMEM((1, wide), f32),
                pltpu.VMEM((QP, D), f32),
            ],
        ),
        out_shape=outs,
        compiler_params=params(1),
        cost_estimate=pl.CostEstimate(
            flops=packs * 12_000_000_000, bytes_accessed=packs * 14_000_000, transcendentals=0
        ),
        name="early",
    )(bounds, target, memory, memory_pos, weights)


def middle(bounds, x, cotangent, head_cotangent, ff_weights, small, head_bias):
    packs, slots, unused = x.shape
    outs = [
        jax.ShapeDtypeStruct(x.shape, bf16),
        jax.ShapeDtypeStruct(x.shape, f32),
        jax.ShapeDtypeStruct(ff_weights.shape, f32),
        jax.ShapeDtypeStruct((D, POS), f32),
        jax.ShapeDtypeStruct((32, D), f32),
    ]
    return pl.pallas_call(
        middle_kernel,
        grid_spec=pltpu.PrefetchScalarGridSpec(
            num_scalar_prefetch=1,
            grid=(packs,),
            in_specs=[
                by_pack(x.shape),
                by_pack(cotangent.shape),
                by_pack(head_cotangent.shape),
                whole(ff_weights.shape),
                pl.BlockSpec((1, D, D), lambda *unused: (SMALL, 0, 0)),
                whole(head_bias.shape),
            ],
            out_specs=[by_pack(x.shape), by_pack(x.shape)] + [whole(out.shape) for out in outs[2:]],
            scratch_shapes=[
                pltpu.VMEM((D, D), f32),
                pltpu.VMEM((2 * FF_BLOCKS, 1, D), f32),
                pltpu.VMEM((2, D, D), bf16),
                pltpu.VMEM((slots, D), bf16),
                pltpu.VMEM((slots, D), f32),
                pltpu.VMEM((slots, D), f32),
                pltpu.VMEM((slots, D), bf16),
                pltpu.VMEM((FF_BLOCKS, slots, D), bf16),
                pltpu.VMEM((FF_BLOCKS, slots, D), f32),
                pltpu.VMEM((FF_BLOCKS, slots, D), bf16),
            ],
        ),
        out_shape=outs,
        compiler_params=params(1),
        cost_estimate=pl.CostEstimate(
            flops=packs * 10_000_000_000, bytes_accessed=packs * 9_000_000, transcendentals=0
        ),
        name="middle",
    )(bounds, x, cotangent, head_cotangent, ff_weights, small, head_bias)


def late(bounds, grad, target, memory, memory_pos, weights, saved, dhead, drow):
    packs, slots, unused = target.shape
    tokens = memory.shape[1]
    outs = [
        jax.ShapeDtypeStruct(target.shape, f32),
        jax.ShapeDtypeStruct(memory.shape, f32),
        jax.ShapeDtypeStruct(weights.shape, f32),
    ]
    wide = HEADS * QP
    return pl.pallas_call(
        late_kernel,
        grid_spec=pltpu.PrefetchScalarGridSpec(
            num_scalar_prefetch=1,
            grid=(packs,),
            in_specs=[
                by_pack(grad.shape),
                by_pack(target.shape),
                by_pack(memory.shape),
                by_pack(memory_pos.shape),
                whole(weights.shape),
            ]
            + [by_pack(array.shape) for array in saved]
            + [whole(dhead.shape), whole(drow.shape)],
            out_specs=[by_pack(outs[0].shape), by_pack(outs[1].shape), whole(weights.shape)],
            scratch_shapes=[
                pltpu.VMEM((D, D), f32),
                pltpu.VMEM((slots + 32, D), f32),
                pltpu.VMEM((ROWS, D), f32),
                pltpu.VMEM((ROWS, D), f32),
                pltpu.VMEM((ROWS, D), bf16),
                pltpu.VMEM((ROWS, D), bf16),
                pltpu.VMEM((ROWS, D), bf16),
                pltpu.VMEM((ROWS, D), bf16),
                pltpu.VMEM((tokens, D), f32),
                pltpu.VMEM((2, wide, D), bf16),
                pltpu.VMEM((2, wide, D), bf16),
                pltpu.VMEM((SIZES[-1], wide), bf16),
                pltpu.VMEM((SIZES[-1], wide), bf16),
                pltpu.VMEM((1, wide), f32),
                pltpu.VMEM((QP, D), f32),
                pltpu.VMEM((D, D), f32),
            ],
        ),
        out_shape=outs,
        compiler_params=params(1),
        cost_estimate=pl.CostEstimate(
            flops=packs * 20_000_000_000, bytes_accessed=packs * 18_000_000, transcendentals=0
        ),
        name="late",
    )(bounds, grad, target, memory, memory_pos, weights, *saved, dhead, drow)


def run_of_images(segment):
    edge = jnp.arange(16, dtype=jnp.int32)
    below = segment[:, None, :] < edge[None, :, None]
    counts = jnp.sum(below.astype(jnp.int32), axis=-1)
    images = jnp.max(jnp.where(segment < IMG_MAX, segment + 1, 0), axis=-1)
    return jnp.where(edge[None, :] == IMG_MAX + 1, images[:, None], counts)


def pack_early(project, output, classes, box_final, query_pos, gains, biases):
    share = project.shape[1]
    columns = [
        classes,
        box_final,
        gains.T,
        biases.T,
        jnp.zeros((share, POS - BIAS - 13), bf16),
        query_pos.T,
        jnp.zeros((share, D - POS - NQ), bf16),
    ]
    small = jnp.concatenate(columns, axis=1)[None]
    return jnp.concatenate([project, output, small], axis=0)


def pack_middle(box, shrink, expand, expand_bias):
    extra = jnp.pad(expand_bias[None], ((1, EXTRA - 2), (0, D - expand_bias.shape[0])))
    return jnp.concatenate([shrink, expand.T, box[0], box[1], extra], axis=0)


def block_rows(devices):
    return [FF_BLOCKS * D // devices] * 2 + [D // devices] * 2


def cut(blocks, devices):
    marks = [0]
    for rows in block_rows(devices):
        marks.append(marks[-1] + rows)
    return [blocks[:, low:high] for low, high in zip(marks, marks[1:])], blocks[:, marks[-1] :]


def regroup(blocks, devices, parts):
    pieces, extra = cut(blocks, devices)
    pieces = [piece.reshape(parts, -1, D) for piece in pieces]
    head = jnp.broadcast_to(extra[0:1, 0:1], (parts, 1, D))
    row = extra[:, 1, : FF_BLOCKS * D // devices].reshape(parts, 1, -1)
    row = jnp.pad(row, ((0, 0), (0, EXTRA - 2), (0, D - row.shape[2])))
    return jnp.concatenate(pieces + [head, row], axis=1)


def parts_of(devices):
    return devices if FF_BLOCKS * D // devices % 16 == 0 else FF_BLOCKS


def swap_order(devices):
    bits = [1 << k for k in range(devices.bit_length() - 1)]
    return [bit for bit in bits if bit > 2] + bits[1:2] + bits[0:1]


def swap(value, bit, devices):
    return lax.ppermute(value, AXES, [(k, k ^ bit) for k in range(devices)])


def gather(shard, devices):
    units, share, width = shard.shape
    me = lax.axis_index(AXES)
    order = swap_order(devices)
    held = shard.reshape((units,) + (1,) * len(order) + (share, width))
    for bit in order:
        axis = len(order) - (bit.bit_length() - 1)
        other = swap(held, bit, devices)
        upper = (me & bit) != 0
        low = jnp.where(upper, other, held)
        high = jnp.where(upper, held, other)
        held = jnp.concatenate([low, high], axis=axis)
    return held.reshape(units, devices * share, width)


def scatter(partial, devices):
    units, unused, rows, width = partial.shape
    me = lax.axis_index(AXES)
    order = swap_order(devices)[::-1]
    held = partial.reshape((units,) + (2,) * len(order) + (rows, width))
    for bit in order:
        axis = len(order) - (bit.bit_length() - 1)
        mine = (me // bit) % 2
        keep = lax.dynamic_slice_in_dim(held, mine, 1, axis)
        send = lax.dynamic_slice_in_dim(held, 1 - mine, 1, axis).astype(bf16)
        held = keep + swap(send, bit, devices).astype(f32)
    return held.reshape(units, rows, width)


def core(
    bounds,
    target,
    memory,
    memory_pos,
    cotangent,
    head_cotangent,
    head_row,
    early_weights,
    middle_weights,
):
    after, *saved = early(bounds, target, memory, memory_pos, early_weights)
    layer, grad, dmiddle, dhead, drow = middle(
        bounds, after, cotangent, head_cotangent, middle_weights, early_weights, head_row
    )
    dtarget, dmemory, dearly = late(
        bounds, grad, target, memory, memory_pos, early_weights, saved, dhead, drow
    )
    return layer, dtarget, dmemory, dearly, dmiddle


def unpack(early_share, middle_share, devices):
    pieces, extra = cut(middle_share[None], devices)
    shrink, expand, box_one, box_two = [piece[0] for piece in pieces]
    small = early_share[SMALL]
    return (
        early_share[0:6],
        early_share[6:8],
        expand.T,
        shrink,
        jnp.stack([box_one, box_two]),
        small[:, 0:CLS],
        small[:, CLS : CLS + 4],
        small[:, POS : POS + NQ].T,
        small[:, GAIN : GAIN + 4].T,
        small[:, BIAS : BIAS + 13].T,
        extra[0, 1, 0 : shrink.shape[0]],
        extra[0, 0, 0 : CLS + 4],
    )


def per_device(
    target,
    memory,
    memory_pos,
    segment,
    project_weight,
    output_weight,
    expand_weight,
    shrink_weight,
    box_weight,
    class_weight,
    box_final,
    query_pos,
    norm_gains,
    biases,
    expand_bias,
    head_bias,
    output_cotangent,
    logit_cotangent,
    box_cotangent,
):
    devices = lax.axis_size(AXES)
    bounds = run_of_images(segment)
    early_weights = gather(
        pack_early(
            project_weight,
            output_weight,
            class_weight,
            box_final,
            query_pos,
            norm_gains,
            biases,
        ),
        devices,
    )
    parts = parts_of(devices)
    middle_shard = pack_middle(box_weight, shrink_weight, expand_weight, expand_bias)
    middle_weights = lax.all_gather(middle_shard, AXES, axis=0, tiled=True)
    middle_weights = middle_weights.reshape((devices,) + middle_shard.shape)
    if parts != devices:
        middle_weights = regroup(middle_weights, devices, parts)
    packs, slots, unused = target.shape
    rest = POS - CLS - 4
    head_cotangent = jnp.concatenate(
        [logit_cotangent, box_cotangent, jnp.zeros((packs, slots, rest), bf16)], axis=-1
    )
    head_row = jnp.broadcast_to(jnp.pad(head_bias.astype(f32), (0, rest))[None], (8, POS))

    layer, dtarget, dmemory, dearly, dmiddle = core(
        bounds,
        target,
        memory,
        memory_pos,
        output_cotangent,
        head_cotangent,
        head_row,
        early_weights,
        middle_weights,
    )
    if parts != devices:
        dmiddle = regroup(dmiddle, parts, devices)
    middle_share = scatter(dmiddle[None], devices)[0]
    early_share = scatter(dearly.reshape(dearly.shape[0], devices, -1, D), devices)
    return (layer, dtarget, dmemory) + unpack(early_share, middle_share, devices)


def solution(mesh):
    both = ("dp", "fsdp")
    by_rows = P(both, None, None)
    return jax.shard_map(
        per_device,
        mesh=mesh,
        in_specs=(
            by_rows,
            by_rows,
            by_rows,
            P(both, None),
            P(None, both, None),
            P(None, both, None),
            P(None, both),
            P(both, None),
            P(None, both, None),
            P(both, None),
            P(both, None),
            P(None, both),
            P(None, both),
            P(None, both),
            P(both),
            P(),
            by_rows,
            by_rows,
            by_rows,
        ),
        out_specs=(
            by_rows,
            by_rows,
            by_rows,
            P(None, both, None),
            P(None, both, None),
            P(None, both),
            P(both, None),
            P(None, both, None),
            P(both, None),
            P(both, None),
            P(None, both),
            P(None, both),
            P(None, both),
            P(both),
            P(),
        ),
        check_vma=False,
    )
```

```python
import functools

import jax
import jax.numpy as jnp
from jax import lax
from jax.experimental import pallas as pl
from jax.experimental.pallas import tpu as pltpu
from jax.sharding import PartitionSpec as P

D = 256
HEADS = 8
NQ = 100
CLS = 92
IMG_MAX = 12
HEAD_DIM = 32
QP = 128
ROWS = IMG_MAX * QP
PAIRS = HEADS // 2
BLOCK = 256
SIZES = (128, 192, 256, 384, 512)
CHUNK = 512
STEP = 400
FF_BLOCKS = 8
GAIN = 96
BIAS = 100
POS = 128
SMALL = 8
EXTRA = 16

epsilon = 1e-05
masked = -1000000000.0
scale = HEAD_DIM ** (-0.5)
log2e = 1.4426950408889634
gelu_a = 0.7978845608028654
gelu_b = gelu_a * 0.044715
AXES = ("dp", "fsdp")
f32 = jnp.float32
bf16 = jnp.bfloat16


def nn(left, right):
    return jnp.dot(left, right, preferred_element_type=f32)


def nt(left, right):
    return lax.dot_general(left, right, (((1,), (1,)), ((), ())), preferred_element_type=f32)


def tn(left, right):
    return lax.dot_general(left, right, (((0,), (0,)), ((), ())), preferred_element_type=f32)


def total(value):
    return jnp.sum(value, axis=0, keepdims=True)


def norm_parts(value):
    middle = jnp.mean(value, axis=-1, keepdims=True)
    centered = value - middle
    spread = jnp.mean(centered * centered, axis=-1, keepdims=True)
    inverse = lax.rsqrt(spread + epsilon)
    return centered * inverse, inverse


def norm_back(unit, inverse, gain, grad):
    scaled = grad * gain
    first = jnp.mean(scaled, axis=-1, keepdims=True)
    second = jnp.mean(scaled * unit, axis=-1, keepdims=True)
    return inverse * (scaled - first - unit * second)


def gelu_parts(value):
    square = value * value
    cdf = 0.5 + 0.5 * jnp.tanh(value * (gelu_a + gelu_b * square))
    result = value * cdf
    slope = cdf + (result - result * cdf) * (2.0 * gelu_a + 6.0 * gelu_b * square)
    return result, slope


def spread_heads(value, spread_ref):
    lane = lax.broadcasted_iota(jnp.int32, (1, D), 1) // HEAD_DIM
    for head in range(HEADS):
        keep = (lane == head).astype(f32).astype(bf16)
        spread_ref[head * QP : (head + 1) * QP, :] = value * keep


def pair_rows(ref, pair):
    side = pair // 2 * (D // 2)
    return ref[2 * QP * pair : 2 * QP * (pair + 1), side : side + D // 2]


def long_rows(ref, pair):
    return ref[2 * QP * pair : 2 * QP * (pair + 1), :]


def head_lane(lanes):
    return lax.broadcasted_iota(jnp.int32, (1, lanes), 1) // HEAD_DIM


def join_pairs(products):
    lane = head_lane(D)
    result = products[0][:QP]
    for head in range(1, HEADS):
        part = products[head // 2][(head % 2) * QP : (head % 2 + 1) * QP]
        result = jnp.where(lane == head, part, result)
    return result


def join_halves(products):
    lane = head_lane(D // 2)
    halves = []
    for half in range(2):
        low, high = products[2 * half : 2 * half + 2]
        part = jnp.where(lane == 2, high[:QP], high[QP:])
        part = jnp.where(lane == 1, low[QP:], part)
        halves.append(jnp.where(lane == 0, low[:QP], part))
    return jnp.concatenate(halves, axis=1)


def half_lanes(value, pair):
    side = pair // 2 * (D // 2)
    return value[:, side : side + D // 2]


def chunk_loop(size, step):
    def run(body):
        for start in range(0, size, step):
            body(start, slice(start, start + step))

    return run


def attend_block(key, value, spread_ref, valid, halves):
    scores = [nt(half_lanes(key, pair), pair_rows(spread_ref, pair)) for pair in range(PAIRS)]
    attends = []
    logs = []
    for pair in range(PAIRS):
        kept = jnp.where(valid, scores[pair], masked)
        top = jnp.max(kept, axis=0, keepdims=True)
        raised = jnp.exp2((kept - top) * (scale * log2e))
        sums = total(raised)
        attends.append((raised * (1.0 / sums)).astype(bf16))
        logs.append(top * (scale * log2e) + jnp.log2(sums))
    if halves:
        products = [tn(attends[pair], half_lanes(value, pair)) for pair in range(PAIRS)]
        context = join_halves(products)
    else:
        context = join_pairs([tn(attends[pair], value) for pair in range(PAIRS)])
    return context, jnp.concatenate(logs, axis=1)


def early_kernel(
    bounds,
    target_ref,
    memory_ref,
    pos_ref,
    w_ref,
    after_ref,
    qs_ref,
    ks_ref,
    vs_ref,
    cs_ref,
    inner_ref,
    cq_ref,
    ck_ref,
    cv_ref,
    cc_ref,
    log_ref,
    small_ref,
    flat_ref,
    rows_ref,
    spread_ref,
    score_ref,
    top_ref,
    sum_ref,
    out_ref,
    mean_ref,
):
    pack = pl.program_id(0)
    slots = target_ref.shape[1]
    tokens = memory_ref.shape[1]

    @pl.when(pack == 0)
    def _():
        small_ref[...] = w_ref[SMALL].astype(f32).T

    def bias(index):
        return small_ref[BIAS + index : BIAS + index + 1, :]

    def gain(index):
        return small_ref[GAIN + index : GAIN + index + 1, :]

    inside = lax.broadcasted_iota(jnp.int32, (QP, 1), 0) < NQ
    position = small_ref[POS : POS + QP, :]
    positions = jnp.concatenate([position] * (CHUNK // QP), axis=0)

    mean_ref[...] = jnp.zeros_like(mean_ref)
    @chunk_loop(tokens, CHUNK)
    def _(start, rows):
        memory = memory_ref[0, rows, :]
        joined = (memory.astype(f32) + pos_ref[0, rows, :].astype(f32)).astype(bf16)
        ck_ref[0, rows, :] = nn(joined, w_ref[4]).astype(bf16)
        value = (nn(memory, w_ref[5]) + bias(4)).astype(bf16)
        cv_ref[0, rows, :] = value
        mean_ref[...] += total(value.astype(f32)) * (1.0 / tokens)

    flat_ref[0:slots, :] = target_ref[0].astype(f32)
    for image in range(IMG_MAX):
        part = flat_ref[image * NQ : image * NQ + QP, :]
        rows_ref[image * QP : (image + 1) * QP, :] = jnp.where(inside, part, 0.0)

    @chunk_loop(ROWS, CHUNK)
    def _(start, rows):
        target = rows_ref[rows, :]
        joined = (target + positions).astype(bf16)
        qs_ref[0, rows, :] = (nn(joined, w_ref[0]) + bias(0)).astype(bf16)
        ks_ref[0, rows, :] = nn(joined, w_ref[1]).astype(bf16)
        vs_ref[0, rows, :] = (nn(target.astype(bf16), w_ref[2]) + bias(1)).astype(bf16)

    @pl.loop(0, IMG_MAX // 2)
    def _(step):
        for turn in range(2):
            rows = pl.ds(pl.multiple_of((2 * step + turn) * QP, QP), QP)
            spread = spread_ref.at[turn]
            spread_heads(qs_ref[0, rows, :], spread)
            context, unused = attend_block(
                ks_ref[0, rows, :], vs_ref[0, rows, :], spread, inside, True
            )
            cs_ref[0, rows, :] = context.astype(bf16)

    @chunk_loop(ROWS, CHUNK)
    def _(start, rows):
        value = rows_ref[rows, :] + nn(cs_ref[0, rows, :], w_ref[6]) + bias(2)
        inner_ref[0, rows, :] = value
        unit, unused = norm_parts(value)
        after = unit * gain(0) + bias(9)
        rows_ref[rows, :] = after
        query = nn((after + positions).astype(bf16), w_ref[3]) + bias(3)
        cq_ref[0, rows, :] = query.astype(bf16)

    @pl.loop(0, IMG_MAX)
    def _(image):
        rows = pl.ds(pl.multiple_of(image * QP, QP), QP)
        first = bounds[pack, image]
        last = bounds[pack, image + 1]
        origin = (first // 16) * 16
        blocks = (last - origin + (BLOCK - 1)) // BLOCK
        spread = spread_ref.at[0]
        spread_heads(cq_ref[0, rows, :], spread)

        def place_at(block, size=BLOCK):
            wanted = origin + block * size
            start = pl.multiple_of(jnp.minimum(wanted, tokens - size), 16)
            token = start + lax.broadcasted_iota(jnp.int32, (size, 1), 0)
            valid = (token >= jnp.maximum(first, wanted)) & (token < last)
            return pl.ds(start, size), valid

        def fits(index):
            below = SIZES[index - 1] if index else 0
            return (last > first) & (last - origin > below) & (last - origin <= SIZES[index])

        @pl.when(last == first)
        def _():
            cc_ref[0, rows, :] = jnp.broadcast_to(mean_ref[...], (QP, D)).astype(bf16)
            log_ref[0, image] = jnp.zeros((1, HEADS * QP), f32)

        def in_one(size):
            place, valid = place_at(0, size)
            context, logs = attend_block(
                ck_ref[0, place, :], cv_ref[0, place, :], spread, valid, False
            )
            cc_ref[0, rows, :] = context.astype(bf16)
            log_ref[0, image] = logs

        for index, size in enumerate(SIZES):
            pl.when(fits(index))(functools.partial(in_one, size))

        @pl.when(last - origin > SIZES[-1])
        def _():
            top_ref[...] = jnp.full_like(top_ref, masked)
            sum_ref[...] = jnp.zeros_like(sum_ref)
            out_ref[...] = jnp.zeros_like(out_ref)

            @pl.loop(0, blocks)
            def _(block):
                place, valid = place_at(block)
                kept = pl.ds(pl.multiple_of(block * BLOCK, BLOCK), BLOCK)
                key = ck_ref[0, place, :]
                for pair in range(PAIRS):
                    lanes = slice(2 * QP * pair, 2 * QP * (pair + 1))
                    scores = jnp.where(valid, nt(key, long_rows(spread, pair)), masked)
                    score_ref[kept, lanes] = scores
                    top = jnp.max(scores, axis=0, keepdims=True)
                    top_ref[:, lanes] = jnp.maximum(top_ref[:, lanes], top)

            @pl.loop(0, blocks)
            def _(block):
                kept = pl.ds(pl.multiple_of(block * BLOCK, BLOCK), BLOCK)
                raised = jnp.exp2((score_ref[kept, :] - top_ref[...]) * (scale * log2e))
                score_ref[kept, :] = raised
                sum_ref[...] += total(raised)

            @pl.loop(0, blocks)
            def _(block):
                place, unused = place_at(block)
                kept = pl.ds(pl.multiple_of(block * BLOCK, BLOCK), BLOCK)
                value = cv_ref[0, place, :]
                products = []
                for pair in range(PAIRS):
                    lanes = slice(2 * QP * pair, 2 * QP * (pair + 1))
                    attend = (score_ref[kept, lanes] * (1.0 / sum_ref[:, lanes])).astype(bf16)
                    products.append(tn(attend, value))
                out_ref[...] += join_pairs(products)

            cc_ref[0, rows, :] = out_ref[...].astype(bf16)
            log_ref[0, image] = top_ref[...] * (scale * log2e) + jnp.log2(sum_ref[...])

    @chunk_loop(ROWS, CHUNK)
    def _(start, rows):
        rows_ref[rows, :] = rows_ref[rows, :] + nn(cc_ref[0, rows, :], w_ref[7]) + bias(5)
    for image in range(IMG_MAX):
        after_ref[0, image * NQ : (image + 1) * NQ, :] = rows_ref[image * QP : image * QP + NQ, :]


def middle_kernel(
    bounds,
    x_ref,
    cot_ref,
    head_cot_ref,
    ff_ref,
    small_in_ref,
    head_bias_ref,
    layer_ref,
    grad_ref,
    dff_ref,
    dhead_ref,
    drow_ref,
    small_ref,
    bias_ref,
    box_ref,
    low_ref,
    cross_ref,
    sum_ref,
    branch_ref,
    hidden_ref,
    slope_ref,
    dpre_ref,
):
    pack = pl.program_id(0)
    slots = x_ref.shape[1]
    parts = ff_ref.shape[0]
    ff = FF_BLOCKS * D // parts
    share = D // parts
    near = D // ff
    boxes = 2 * ff
    extra = 2 * ff + 2 * share

    @pl.when(pack == 0)
    def _():
        small_ref[...] = small_in_ref[0].astype(f32).T
        pair = ff_ref[:, boxes:extra, :].astype(f32)
        box_ref[0] = pair[:, :share].reshape(D, D).astype(bf16)
        box_ref[1] = pair[:, share:].reshape(D, D).astype(bf16)
        for block in range(FF_BLOCKS):
            rows = [ff_ref[block * near + k, extra : extra + 16, :] for k in range(near)]
            rows = [row.astype(f32)[1:2, 0:ff] for row in rows]
            bias_ref[block] = jnp.concatenate(rows, axis=1)
        bias_ref[FF_BLOCKS:] = jnp.zeros((FF_BLOCKS, 1, D), f32)
        dff_ref[...] = jnp.zeros_like(dff_ref)
        dhead_ref[...] = jnp.zeros_like(dhead_ref)
        drow_ref[...] = jnp.zeros_like(drow_ref)

    def bias(index):
        return small_ref[BIAS + index : BIAS + index + 1, :]

    def gain(index):
        return small_ref[GAIN + index : GAIN + index + 1, :]

    def add_row(column, value):
        row = column - GAIN
        drow_ref[row : row + 1, :] += value

    def near_block(block):
        return pl.ds(block * near, near)

    def shrink(block):
        return ff_ref[near_block(block), 0:ff, :].reshape(D, D)

    def expand(block):
        return ff_ref[near_block(block), ff:boxes, :].reshape(D, D)

    @chunk_loop(slots, STEP)
    def _(start, rows):
        unit, unused = norm_parts(x_ref[0, rows, :])
        after_cross = unit * gain(1) + bias(10)
        cross_ref[rows, :] = after_cross
        low_ref[rows, :] = after_cross.astype(bf16)

    def hide(block):
        value, slope = gelu_parts(nt(low_ref[...], expand(block)) + bias_ref[block])
        hidden_ref[block] = value.astype(bf16)
        slope_ref[block] = slope

    hide(0)
    sum_ref[...] = cross_ref[...] + bias(6)

    @pl.loop(1, FF_BLOCKS)
    def _(block):
        sum_ref[...] += nn(hidden_ref[block - 1], shrink(block - 1))
        hide(block)

    sum_ref[...] += nn(hidden_ref[FF_BLOCKS - 1], shrink(FF_BLOCKS - 1))

    head_weight = small_in_ref[0, :, 0:POS]
    lane = lax.broadcasted_iota(jnp.int32, (1, POS), 1)
    is_box = (lane >= CLS) & (lane < CLS + 4)
    @chunk_loop(slots, STEP)
    def _(start, rows):
        slot = start + lax.broadcasted_iota(jnp.int32, (STEP, 1), 0)
        live = (slot < bounds[pack, IMG_MAX + 1] * NQ).astype(f32)
        unit_ffn, inverse_ffn = norm_parts(sum_ref[rows, :])
        after_ffn = unit_ffn * gain(2) + bias(11)
        layer_ref[0, rows, :] = (after_ffn * live).astype(bf16)
        unit_last, inverse_last = norm_parts(after_ffn)
        normed = (unit_last * gain(3) + bias(12)).astype(bf16)
        one, one_slope = gelu_parts(nn(normed, box_ref[0]) + bias(7))
        box_one = one.astype(bf16)
        two, two_slope = gelu_parts(nn(box_one, box_ref[1]) + bias(8))
        box_two = two.astype(bf16)
        box = jax.nn.sigmoid(nn(box_two, head_weight) + head_bias_ref[0:1, :])

        head_cot = head_cot_ref[0, rows, :].astype(f32) * live
        grad_box = jnp.where(is_box, head_cot * box * (1.0 - box), 0.0).astype(bf16)
        grad_logit = jnp.where(lane < CLS, head_cot, 0.0).astype(bf16)
        drow_ref[31:32, 0:POS] += total(grad_box.astype(f32)) + total(grad_logit.astype(f32))
        normed_t = normed.T
        grad_two = (two_slope * nt(grad_box, head_weight)).astype(bf16)
        grad_one = (one_slope * nt(grad_two, box_ref[1])).astype(bf16)
        dhead_ref[...] += nn(normed_t, grad_logit) + tn(box_two, grad_box)
        dff_ref[:, boxes : boxes + share, :] += nn(normed_t, grad_one).reshape(parts, share, D)
        dff_ref[:, boxes + share : extra, :] += tn(box_one, grad_two).reshape(parts, share, D)
        add_row(BIAS + 8, total(grad_two.astype(f32)))
        add_row(BIAS + 7, total(grad_one.astype(f32)))
        grad_normed = nt(grad_one, box_ref[0]) + nt(grad_logit, head_weight)
        add_row(GAIN + 3, total(grad_normed * unit_last))
        add_row(BIAS + 12, total(grad_normed))
        grad_after = cot_ref[0, rows, :].astype(f32) * live + norm_back(
            unit_last, inverse_last, gain(3), grad_normed
        )
        add_row(GAIN + 2, total(grad_after * unit_ffn))
        add_row(BIAS + 11, total(grad_after))
        grad_ffn = norm_back(unit_ffn, inverse_ffn, gain(2), grad_after)
        grad_branch = grad_ffn.astype(bf16)
        add_row(BIAS + 6, total(grad_branch.astype(f32)))
        sum_ref[rows, :] = grad_ffn
        branch_ref[rows, :] = grad_branch

    @pl.loop(0, FF_BLOCKS)
    def _(block):
        branch = branch_ref[...]
        dpre = (nt(branch, shrink(block)) * slope_ref[block]).astype(bf16)
        dpre_ref[block] = dpre
        bias_ref[FF_BLOCKS + block] += total(dpre.astype(f32))
        dshrink = tn(hidden_ref[block], branch).reshape(near, ff, D)
        dff_ref[near_block(block), 0:ff, :] += dshrink
        dexpand = tn(dpre, low_ref[...]).reshape(near, ff, D)
        dff_ref[near_block(block), ff:boxes, :] += dexpand

    grad_cross = sum_ref[...]
    for block in range(FF_BLOCKS):
        grad_cross += nn(dpre_ref[block], expand(block))
    sum_ref[...] = grad_cross
    @chunk_loop(slots, STEP)
    def _(start, rows):
        unit, inverse = norm_parts(x_ref[0, rows, :])
        grad = sum_ref[rows, :]
        add_row(GAIN + 1, total(grad * unit))
        add_row(BIAS + 10, total(grad))
        grad_ref[0, rows, :] = norm_back(unit, inverse, gain(1), grad)

    @pl.when(pack == pl.num_programs(0) - 1)
    def _():
        for part in range(parts):
            dff_ref[part, extra : extra + 1, :] = drow_ref[31:32, :]
            side = part % near * ff
            values = bias_ref[FF_BLOCKS + part // near][:, side : side + ff]
            dff_ref[part, extra + 1 : extra + 2, 0:ff] = values


def attend_back(key, value, spread, spread_grad, valid, logs, attend_ref, score_ref):
    scores = [nt(half_lanes(key, pair), pair_rows(spread, pair)) for pair in range(PAIRS)]
    grads = [nt(half_lanes(value, pair), pair_rows(spread_grad, pair)) for pair in range(PAIRS)]
    lows = []
    for pair in range(PAIRS):
        lanes = slice(2 * QP * pair, 2 * QP * (pair + 1))
        if logs is None:
            kept = jnp.where(valid, scores[pair], masked)
            top = jnp.max(kept, axis=0, keepdims=True)
            raised = jnp.exp2((kept - top) * (scale * log2e))
            attend = raised * (1.0 / total(raised))
        else:
            attend = jnp.exp2(scores[pair] * (scale * log2e) - logs[:, lanes])
            attend = jnp.where(valid, attend, 0.0)
        row_dot = total(attend * grads[pair])
        low = (attend * (grads[pair] - row_dot)).astype(bf16)
        attend_ref[:, lanes] = attend.astype(bf16)
        score_ref[:, lanes] = low
        lows.append(low)
    return join_halves([tn(lows[pair], half_lanes(key, pair)) for pair in range(PAIRS)]) * scale


def late_cross_kernel(
    bounds,
    grad_ref,
    memory_ref,
    pos_ref,
    w_ref,
    cq_ref,
    ck_ref,
    cv_ref,
    cc_ref,
    log_ref,
    gq_ref,
    dmemory_ref,
    dw_ref,
    drows_ref,
    flat_ref,
    grad_rows_ref,
    context_ref,
    dv_ref,
    spread_ref,
    spread_grad_ref,
    attend_ref,
    score_ref,
    sum_ref,
    out_ref,
):
    pack = pl.program_id(0)
    slots = grad_ref.shape[1]
    tokens = memory_ref.shape[1]

    @pl.when(pack == 0)
    def _():
        dw_ref[...] = jnp.zeros_like(dw_ref)
        drows_ref[...] = jnp.zeros_like(drows_ref)

    def add_row(row, value):
        drows_ref[row : row + 1, :] += value

    inside = lax.broadcasted_iota(jnp.int32, (QP, 1), 0) < NQ

    flat_ref[0:slots, :] = grad_ref[0]
    for image in range(IMG_MAX):
        part = flat_ref[image * NQ : image * NQ + QP, :]
        grad_rows_ref[image * QP : (image + 1) * QP, :] = jnp.where(inside, part, 0.0)
    @chunk_loop(ROWS, CHUNK)
    def _(start, rows):
        branch = grad_rows_ref[rows, :].astype(bf16)
        add_row(1, total(branch.astype(f32)))
        dw_ref[2] += tn(cc_ref[0, rows, :], branch)
        context_ref[rows, :] = nt(branch, w_ref[7]).astype(bf16)
    dmemory_ref[...] = jnp.zeros_like(dmemory_ref)
    dv_ref[...] = jnp.zeros_like(dv_ref)

    @pl.loop(0, IMG_MAX)
    def _(image):
        rows = pl.ds(pl.multiple_of(image * QP, QP), QP)
        first = bounds[pack, image]
        last = bounds[pack, image + 1]
        origin = (first // 16) * 16
        blocks = (last - origin + (BLOCK - 1)) // BLOCK
        spread = spread_ref
        spread_grad = spread_grad_ref
        attend_low = attend_ref
        score_low = score_ref
        spread_heads(cq_ref[0, rows, :], spread)
        spread_heads(context_ref[rows, :], spread_grad)
        logs = log_ref[0, image]

        def place_at(block, size=BLOCK):
            wanted = origin + block * size
            start = pl.multiple_of(jnp.minimum(wanted, tokens - size), 16)
            token = start + lax.broadcasted_iota(jnp.int32, (size, 1), 0)
            valid = (token >= jnp.maximum(first, wanted)) & (token < last)
            return pl.ds(start, size), valid

        def fits(index):
            below = SIZES[index - 1] if index else 0
            return (last > first) & (last - origin > below) & (last - origin <= SIZES[index])

        @pl.when(last == first)
        def _():
            gq_ref[0, rows, :] = jnp.zeros((QP, D), bf16)

        def in_one(size):
            place, valid = place_at(0, size)
            attend_part = attend_low.at[0:size]
            score_part = score_low.at[0:size]
            grad_query = attend_back(
                ck_ref[0, place, :],
                cv_ref[0, place, :],
                spread,
                spread_grad,
                valid,
                logs,
                attend_part,
                score_part,
            )
            gq_ref[0, rows, :] = grad_query.astype(bf16)
            dv_ref[place, :] += nn(attend_part[...], spread_grad[...])
            dmemory_ref[0, place, :] += nn(score_part[...], spread[...])

        for index, size in enumerate(SIZES):
            pl.when(fits(index))(functools.partial(in_one, size))

        @pl.when(last - origin > SIZES[-1])
        def _():
            sum_ref[...] = jnp.zeros_like(sum_ref)
            out_ref[...] = jnp.zeros_like(out_ref)

            @pl.loop(0, blocks)
            def _(block):
                place, valid = place_at(block)
                for pair in range(PAIRS):
                    lanes = slice(2 * QP * pair, 2 * QP * (pair + 1))
                    scores = nt(ck_ref[0, place, :], long_rows(spread, pair))
                    attend = jnp.exp2(scores * (scale * log2e) - logs[:, lanes])
                    attend = jnp.where(valid, attend, 0.0)
                    grad_attend = nt(cv_ref[0, place, :], long_rows(spread_grad, pair))
                    sum_ref[:, lanes] += total(attend * grad_attend)

            @pl.loop(0, blocks)
            def _(block):
                place, valid = place_at(block)
                key = ck_ref[0, place, :]
                products = []
                for pair in range(PAIRS):
                    lanes = slice(2 * QP * pair, 2 * QP * (pair + 1))
                    scores = nt(ck_ref[0, place, :], long_rows(spread, pair))
                    attend = jnp.exp2(scores * (scale * log2e) - logs[:, lanes])
                    attend = jnp.where(valid, attend, 0.0)
                    grad_attend = nt(cv_ref[0, place, :], long_rows(spread_grad, pair))
                    grad_scores = attend * (grad_attend - sum_ref[:, lanes])
                    grad_scores = grad_scores.astype(bf16)
                    attend_low[0:BLOCK, lanes] = attend.astype(bf16)
                    score_low[0:BLOCK, lanes] = grad_scores
                    products.append(tn(grad_scores, half_lanes(key, pair)))
                out_ref[...] += join_halves(products)
                dv_ref[place, :] += nn(attend_low[0:BLOCK, :], spread_grad[...])
                dmemory_ref[0, place, :] += nn(score_low[0:BLOCK, :], spread[...])

            gq_ref[0, rows, :] = (out_ref[...] * scale).astype(bf16)

    @chunk_loop(tokens, CHUNK)
    def _(start, rows):
        memory = memory_ref[0, rows, :]
        joined = (memory.astype(f32) + pos_ref[0, rows, :].astype(f32)).astype(bf16)
        grad_key = (dmemory_ref[0, rows, :] * scale).astype(bf16)
        grad_value = dv_ref[rows, :].astype(bf16)
        dmemory_ref[0, rows, :] = nt(grad_key, w_ref[4]) + nt(grad_value, w_ref[5])
        add_row(0, total(grad_value.astype(f32)))
        dw_ref[0] += tn(joined, grad_key)
        dw_ref[1] += tn(memory, grad_value)


def late_self_kernel(
    grad_ref,
    gcq_ref,
    target_ref,
    w_ref,
    qs_ref,
    ks_ref,
    vs_ref,
    cs_ref,
    inner_ref,
    dcross_ref,
    dcross_rows_ref,
    dhead_ref,
    drow_ref,
    dtarget_ref,
    dw_ref,
    small_ref,
    flat_ref,
    grad_rows_ref,
    place_ref,
    context_ref,
    gq_ref,
    gk_ref,
    gv_ref,
    spread_ref,
    spread_grad_ref,
    attend_ref,
    score_ref,
    drows_ref,
):
    pack = pl.program_id(0)
    slots = target_ref.shape[1]

    @pl.when(pack == 0)
    def _():
        small_ref[...] = w_ref[SMALL].astype(f32).T
        dw_ref[0:4] = jnp.zeros((4, D, D), f32)
        dw_ref[4:6] = dcross_ref[0:2]
        dw_ref[6] = jnp.zeros((D, D), f32)
        dw_ref[7] = dcross_ref[2]
        drows_ref[...] = jnp.zeros_like(drows_ref)
        drows_ref[GAIN : GAIN + 32, :] = drow_ref[...]
        drows_ref[BIAS + 4 : BIAS + 6, :] += dcross_rows_ref[0:2, :]

    def bias(index):
        return small_ref[BIAS + index : BIAS + index + 1, :]

    def gain(index):
        return small_ref[GAIN + index : GAIN + index + 1, :]

    def add_row(row, value):
        drows_ref[row : row + 1, :] += value

    inside = lax.broadcasted_iota(jnp.int32, (QP, 1), 0) < NQ
    position = small_ref[POS : POS + QP, :]
    positions = jnp.concatenate([position] * (CHUNK // QP), axis=0)

    flat_ref[0:slots, :] = grad_ref[0]
    for image in range(IMG_MAX):
        part = flat_ref[image * NQ : image * NQ + QP, :]
        grad_rows_ref[image * QP : (image + 1) * QP, :] = jnp.where(inside, part, 0.0)
    flat_ref[0:slots, :] = target_ref[0].astype(f32)

    @chunk_loop(ROWS, CHUNK)
    def _(start, rows):
        unit, inverse = norm_parts(inner_ref[0, rows, :])
        cross_in = (unit * gain(0) + bias(9) + positions).astype(bf16)
        grad_query = gcq_ref[0, rows, :]
        add_row(BIAS + 3, total(grad_query.astype(f32)))
        dw_ref[3] += tn(cross_in, grad_query)
        place = nt(grad_query, w_ref[3])
        place_ref[rows, :] = place
        grad = grad_rows_ref[rows, :] + place
        add_row(GAIN, total(grad * unit))
        add_row(BIAS + 9, total(grad))
        grad = norm_back(unit, inverse, gain(0), grad)
        grad_rows_ref[rows, :] = grad
        branch = grad.astype(bf16)
        add_row(BIAS + 2, total(branch.astype(f32)))
        dw_ref[6] += tn(cs_ref[0, rows, :], branch)
        context_ref[rows, :] = nt(branch, w_ref[6]).astype(bf16)

    @pl.loop(0, IMG_MAX // 2)
    def _(step):
        for turn in range(2):
            rows = pl.ds(pl.multiple_of((2 * step + turn) * QP, QP), QP)
            spread = spread_ref.at[turn]
            spread_grad = spread_grad_ref.at[turn]
            attend_low = attend_ref.at[turn * QP : (turn + 1) * QP]
            score_low = score_ref.at[turn * QP : (turn + 1) * QP]
            spread_heads(qs_ref[0, rows, :], spread)
            spread_heads(context_ref[rows, :], spread_grad)
            grad_query = attend_back(
                ks_ref[0, rows, :],
                vs_ref[0, rows, :],
                spread,
                spread_grad,
                inside,
                None,
                attend_low,
                score_low,
            )
            gq_ref[rows, :] = grad_query.astype(bf16)
            gv_ref[rows, :] = nn(attend_low[...], spread_grad[...]).astype(bf16)
            gk_ref[rows, :] = (nn(score_low[...], spread[...]) * scale).astype(bf16)

    for start in range(0, ROWS, CHUNK):
        rows = slice(start, start + CHUNK)
        images = range(start // QP, (start + CHUNK) // QP)
        parts = [flat_ref[image * NQ : image * NQ + QP, :] for image in images]
        target = jnp.concatenate([jnp.where(inside, part, 0.0) for part in parts], axis=0)
        joined_t = (target + positions).astype(bf16).T
        grad_query = gq_ref[rows, :]
        grad_key = gk_ref[rows, :]
        grad_value = gv_ref[rows, :]
        add_row(BIAS + 0, total(grad_query.astype(f32)))
        add_row(BIAS + 1, total(grad_value.astype(f32)))
        dw_ref[0] += nn(joined_t, grad_query)
        dw_ref[1] += nn(joined_t, grad_key)
        dw_ref[2] += tn(target.astype(bf16), grad_value)
        grad_joined = nt(grad_query, w_ref[0]) + nt(grad_key, w_ref[1])
        grad_rows_ref[rows, :] += grad_joined + nt(grad_value, w_ref[2])
        grad_place = grad_joined + place_ref[rows, :]
        for image in range(CHUNK // QP):
            drows_ref[POS : POS + QP, :] += grad_place[image * QP : (image + 1) * QP, :]
    for image in range(IMG_MAX):
        part = grad_rows_ref[image * QP : image * QP + NQ, :]
        dtarget_ref[0, image * NQ : (image + 1) * NQ, :] = part

    @pl.when(pack == pl.num_programs(0) - 1)
    def _():
        small = drows_ref[...].T
        dw_ref[SMALL, :, POS:] = small[:, POS:]
        dw_ref[SMALL, :, :POS] = small[:, :POS] + dhead_ref[...]


def whole(shape):
    zeros = (0,) * len(shape)
    return pl.BlockSpec(shape, lambda *unused: zeros)


def by_pack(shape):
    zeros = (0,) * (len(shape) - 1)
    return pl.BlockSpec((1,) + tuple(shape[1:]), lambda pack, *unused: (pack,) + zeros)


LIMIT = 60 * 1024 * 1024


def params(axes):
    return pltpu.CompilerParams(
        dimension_semantics=("arbitrary",) * axes, vmem_limit_bytes=LIMIT
    )


def early(bounds, target, memory, memory_pos, weights):
    packs, slots, unused = target.shape
    tokens = memory.shape[1]
    low_rows = jax.ShapeDtypeStruct((packs, ROWS, D), bf16)
    low_tokens = jax.ShapeDtypeStruct((packs, tokens, D), bf16)
    outs = [
        jax.ShapeDtypeStruct((packs, slots, D), f32),
        low_rows,
        low_rows,
        low_rows,
        low_rows,
        jax.ShapeDtypeStruct((packs, ROWS, D), f32),
        low_rows,
        low_tokens,
        low_tokens,
        low_rows,
        jax.ShapeDtypeStruct((packs, IMG_MAX, 1, HEADS * QP), f32),
    ]
    wide = HEADS * QP
    return pl.pallas_call(
        early_kernel,
        grid_spec=pltpu.PrefetchScalarGridSpec(
            num_scalar_prefetch=1,
            grid=(packs,),
            in_specs=[
                by_pack(target.shape),
                by_pack(memory.shape),
                by_pack(memory_pos.shape),
                whole(weights.shape),
            ],
            out_specs=[by_pack(out.shape) for out in outs],
            scratch_shapes=[
                pltpu.VMEM((D, D), f32),
                pltpu.VMEM((slots + 32, D), f32),
                pltpu.VMEM((ROWS, D), f32),
                pltpu.VMEM((2, wide, D), bf16),
                pltpu.VMEM((tokens, wide), f32),
                pltpu.VMEM((1, wide), f32),
                pltpu.VMEM((1, wide), f32),
                pltpu.VMEM((QP, D), f32),
                pltpu.VMEM((1, D), f32),
            ],
        ),
        out_shape=outs,
        compiler_params=params(1),
        cost_estimate=pl.CostEstimate(
            flops=packs * 12_000_000_000, bytes_accessed=packs * 14_000_000, transcendentals=0
        ),
        name="early",
    )(bounds, target, memory, memory_pos, weights)


def middle(bounds, x, cotangent, head_cotangent, ff_weights, small, head_bias):
    packs, slots, unused = x.shape
    outs = [
        jax.ShapeDtypeStruct(x.shape, bf16),
        jax.ShapeDtypeStruct(x.shape, f32),
        jax.ShapeDtypeStruct(ff_weights.shape, f32),
        jax.ShapeDtypeStruct((D, POS), f32),
        jax.ShapeDtypeStruct((32, D), f32),
    ]
    return pl.pallas_call(
        middle_kernel,
        grid_spec=pltpu.PrefetchScalarGridSpec(
            num_scalar_prefetch=1,
            grid=(packs,),
            in_specs=[
                by_pack(x.shape),
                by_pack(cotangent.shape),
                by_pack(head_cotangent.shape),
                whole(ff_weights.shape),
                pl.BlockSpec((1, D, D), lambda *unused: (SMALL, 0, 0)),
                whole(head_bias.shape),
            ],
            out_specs=[by_pack(x.shape), by_pack(x.shape)] + [whole(out.shape) for out in outs[2:]],
            scratch_shapes=[
                pltpu.VMEM((D, D), f32),
                pltpu.VMEM((2 * FF_BLOCKS, 1, D), f32),
                pltpu.VMEM((2, D, D), bf16),
                pltpu.VMEM((slots, D), bf16),
                pltpu.VMEM((slots, D), f32),
                pltpu.VMEM((slots, D), f32),
                pltpu.VMEM((slots, D), bf16),
                pltpu.VMEM((FF_BLOCKS, slots, D), bf16),
                pltpu.VMEM((FF_BLOCKS, slots, D), f32),
                pltpu.VMEM((FF_BLOCKS, slots, D), bf16),
            ],
        ),
        out_shape=outs,
        compiler_params=params(1),
        cost_estimate=pl.CostEstimate(
            flops=packs * 10_000_000_000, bytes_accessed=packs * 9_000_000, transcendentals=0
        ),
        name="middle",
    )(bounds, x, cotangent, head_cotangent, ff_weights, small, head_bias)


def late_cross(bounds, grad, memory, memory_pos, weights, saved):
    packs, slots, unused = grad.shape
    tokens = memory.shape[1]
    wide = HEADS * QP
    outs = [
        jax.ShapeDtypeStruct((packs, ROWS, D), bf16),
        jax.ShapeDtypeStruct(memory.shape, f32),
        jax.ShapeDtypeStruct((3, D, D), f32),
        jax.ShapeDtypeStruct((8, D), f32),
    ]
    return pl.pallas_call(
        late_cross_kernel,
        grid_spec=pltpu.PrefetchScalarGridSpec(
            num_scalar_prefetch=1,
            grid=(packs,),
            in_specs=[
                by_pack(grad.shape),
                by_pack(memory.shape),
                by_pack(memory_pos.shape),
                whole(weights.shape),
            ]
            + [by_pack(array.shape) for array in saved],
            out_specs=[by_pack(outs[0].shape), by_pack(outs[1].shape)]
            + [whole(out.shape) for out in outs[2:]],
            scratch_shapes=[
                pltpu.VMEM((slots + 32, D), f32),
                pltpu.VMEM((ROWS, D), f32),
                pltpu.VMEM((ROWS, D), bf16),
                pltpu.VMEM((tokens, D), f32),
                pltpu.VMEM((wide, D), bf16),
                pltpu.VMEM((wide, D), bf16),
                pltpu.VMEM((SIZES[-1], wide), bf16),
                pltpu.VMEM((SIZES[-1], wide), bf16),
                pltpu.VMEM((1, wide), f32),
                pltpu.VMEM((QP, D), f32),
            ],
        ),
        out_shape=outs,
        compiler_params=params(1),
        cost_estimate=pl.CostEstimate(
            flops=packs * 12_000_000_000, bytes_accessed=packs * 9_000_000, transcendentals=0
        ),
        name="late_cross",
    )(bounds, grad, memory, memory_pos, weights, *saved)


def late_self(grad, grad_query, target, weights, saved, dcross, dcross_rows, dhead, drow):
    packs, slots, unused = target.shape
    wide = HEADS * QP
    outs = [
        jax.ShapeDtypeStruct(target.shape, f32),
        jax.ShapeDtypeStruct(weights.shape, f32),
    ]
    sums = [dcross, dcross_rows, dhead, drow]
    return pl.pallas_call(
        late_self_kernel,
        grid=(packs,),
        in_specs=[
            by_pack(grad.shape),
            by_pack(grad_query.shape),
            by_pack(target.shape),
            whole(weights.shape),
        ]
        + [by_pack(array.shape) for array in saved]
        + [whole(array.shape) for array in sums],
        out_specs=[by_pack(target.shape), whole(weights.shape)],
        scratch_shapes=[
            pltpu.VMEM((D, D), f32),
            pltpu.VMEM((slots + 32, D), f32),
            pltpu.VMEM((ROWS, D), f32),
            pltpu.VMEM((ROWS, D), f32),
            pltpu.VMEM((ROWS, D), bf16),
            pltpu.VMEM((ROWS, D), bf16),
            pltpu.VMEM((ROWS, D), bf16),
            pltpu.VMEM((ROWS, D), bf16),
            pltpu.VMEM((2, wide, D), bf16),
            pltpu.VMEM((2, wide, D), bf16),
            pltpu.VMEM((2 * QP, wide), bf16),
            pltpu.VMEM((2 * QP, wide), bf16),
            pltpu.VMEM((D, D), f32),
        ],
        out_shape=outs,
        compiler_params=params(1),
        cost_estimate=pl.CostEstimate(
            flops=packs * 10_000_000_000, bytes_accessed=packs * 7_000_000, transcendentals=0
        ),
        name="late_self",
    )(grad, grad_query, target, weights, *saved, *sums)


def run_of_images(segment):
    edge = jnp.arange(16, dtype=jnp.int32)
    below = segment[:, None, :] < edge[None, :, None]
    counts = jnp.sum(below.astype(jnp.int32), axis=-1)
    images = jnp.max(jnp.where(segment < IMG_MAX, segment + 1, 0), axis=-1)
    return jnp.where(edge[None, :] == IMG_MAX + 1, images[:, None], counts)


def pack_early(project, output, classes, box_final, query_pos, gains, biases):
    share = project.shape[1]
    columns = [
        classes,
        box_final,
        gains.T,
        biases.T,
        jnp.zeros((share, POS - BIAS - 13), bf16),
        query_pos.T,
        jnp.zeros((share, D - POS - NQ), bf16),
    ]
    small = jnp.concatenate(columns, axis=1)[None]
    return jnp.concatenate([project, output, small], axis=0)


def pack_middle(box, shrink, expand, expand_bias):
    extra = jnp.pad(expand_bias[None], ((1, EXTRA - 2), (0, D - expand_bias.shape[0])))
    return jnp.concatenate([shrink, expand.T, box[0], box[1], extra], axis=0)


def block_rows(devices):
    return [FF_BLOCKS * D // devices] * 2 + [D // devices] * 2


def cut(blocks, devices):
    marks = [0]
    for rows in block_rows(devices):
        marks.append(marks[-1] + rows)
    return [blocks[:, low:high] for low, high in zip(marks, marks[1:])], blocks[:, marks[-1] :]


def regroup(blocks, devices, parts):
    pieces, extra = cut(blocks, devices)
    pieces = [piece.reshape(parts, -1, D) for piece in pieces]
    head = jnp.broadcast_to(extra[0:1, 0:1], (parts, 1, D))
    row = extra[:, 1, : FF_BLOCKS * D // devices].reshape(parts, 1, -1)
    row = jnp.pad(row, ((0, 0), (0, EXTRA - 2), (0, D - row.shape[2])))
    return jnp.concatenate(pieces + [head, row], axis=1)


def parts_of(devices):
    return devices if FF_BLOCKS * D // devices % 16 == 0 else FF_BLOCKS


def bit_groups(devices):
    bits = [1 << k for k in range(1, devices.bit_length() - 1)]
    groups = [(1,)]
    while bits:
        groups.append((bits[0], bits[-1]) if len(bits) > 1 else (bits[0],))
        bits = bits[1:-1]
    return groups


def mixes(bits):
    result = [0]
    for bit in bits:
        result += [mix | bit for mix in result]
    return result


def swap(value, bits, devices):
    return lax.ppermute(value, AXES, [(k, k ^ bits) for k in range(devices)])


def bit_axis(bit, devices):
    return devices.bit_length() - bit.bit_length()


def gather(shard, devices):
    units, share, width = shard.shape
    me = lax.axis_index(AXES)
    bits_all = devices.bit_length() - 1
    held = shard.reshape((units,) + (1,) * bits_all + (share, width))
    for bits in bit_groups(devices)[::-1]:
        parts = [swap(held, mix, devices) if mix else held for mix in mixes(bits)]
        for bit in bits:
            upper = (me & bit) != 0
            joined = []
            for mine, other in zip(parts[0::2], parts[1::2]):
                low = jnp.where(upper, other, mine)
                high = jnp.where(upper, mine, other)
                joined.append(jnp.concatenate([low, high], axis=bit_axis(bit, devices)))
            parts = joined
        held = parts[0]
    return held.reshape(units, devices * share, width)


def by_bits(partial, devices):
    units, unused, rows, width = partial.shape
    return partial.reshape((units,) + (2,) * (devices.bit_length() - 1) + (rows, width))


def divide(held, bits, devices):
    me = lax.axis_index(AXES)
    parts = []
    for mix in mixes(bits):
        part = held
        for bit in bits:
            place = ((me ^ mix) // bit) % 2
            part = lax.dynamic_slice_in_dim(part, place, 1, bit_axis(bit, devices))
        parts.append(part if mix == 0 else part.astype(bf16))
    return parts[0], parts[1:]


def collect(keep, sends, bits, devices):
    for mix, send in zip(mixes(bits)[1:], sends):
        keep = keep + swap(send, mix, devices).astype(f32)
    return keep


def scatter(held, groups, devices):
    for bits in groups:
        held = collect(*divide(held, bits, devices), bits, devices)
    return held


def unpack(early_share, middle_share, devices):
    pieces, extra = cut(middle_share[None], devices)
    shrink, expand, box_one, box_two = [piece[0] for piece in pieces]
    small = early_share[SMALL]
    return (
        early_share[0:6],
        early_share[6:8],
        expand.T,
        shrink,
        jnp.stack([box_one, box_two]),
        small[:, 0:CLS],
        small[:, CLS : CLS + 4],
        small[:, POS : POS + NQ].T,
        small[:, GAIN : GAIN + 4].T,
        small[:, BIAS : BIAS + 13].T,
        extra[0, 1, 0 : shrink.shape[0]],
        extra[0, 0, 0 : CLS + 4],
    )


def per_device(
    target,
    memory,
    memory_pos,
    segment,
    project_weight,
    output_weight,
    expand_weight,
    shrink_weight,
    box_weight,
    class_weight,
    box_final,
    query_pos,
    norm_gains,
    biases,
    expand_bias,
    head_bias,
    output_cotangent,
    logit_cotangent,
    box_cotangent,
):
    devices = lax.axis_size(AXES)
    bounds = run_of_images(segment)
    early_weights = gather(
        pack_early(
            project_weight,
            output_weight,
            class_weight,
            box_final,
            query_pos,
            norm_gains,
            biases,
        ),
        devices,
    )
    parts = parts_of(devices)
    middle_shard = pack_middle(box_weight, shrink_weight, expand_weight, expand_bias)
    middle_weights = lax.all_gather(middle_shard, AXES, axis=0, tiled=True)
    middle_weights = middle_weights.reshape((devices,) + middle_shard.shape)
    if parts != devices:
        middle_weights = regroup(middle_weights, devices, parts)
    packs, slots, unused = target.shape
    rest = POS - CLS - 4
    head_cotangent = jnp.concatenate(
        [logit_cotangent, box_cotangent, jnp.zeros((packs, slots, rest), bf16)], axis=-1
    )
    head_row = jnp.broadcast_to(jnp.pad(head_bias.astype(f32), (0, rest))[None], (8, POS))

    groups = bit_groups(devices)
    after, *saved = early(bounds, target, memory, memory_pos, early_weights)
    layer, grad, dmiddle, dhead, drow = middle(
        bounds,
        after,
        output_cotangent,
        head_cotangent,
        middle_weights,
        early_weights,
        head_row,
    )
    if parts != devices:
        dmiddle = regroup(dmiddle, parts, devices)
    held = scatter(by_bits(dmiddle[None], devices), groups[:1], devices)
    keep, sends = divide(held, groups[1], devices)
    grad, keep, sends = lax.optimization_barrier((grad, keep, sends))
    held = collect(keep, sends, groups[1], devices)
    grad_query, dmemory, dcross, dcross_rows = late_cross(
        bounds, grad, memory, memory_pos, early_weights, saved[5:]
    )
    keep, sends = divide(held, groups[2], devices)
    grad_query, keep, sends = lax.optimization_barrier((grad_query, keep, sends))
    held = collect(keep, sends, groups[2], devices)
    dtarget, dearly = late_self(
        grad,
        grad_query,
        target,
        early_weights,
        saved[:5],
        dcross,
        dcross_rows,
        dhead,
        drow,
    )
    middle_share = scatter(held, groups[3:], devices).reshape(-1, D)
    units = dearly.shape[0]
    early_held = by_bits(dearly.reshape(units, devices, -1, D), devices)
    early_share = scatter(early_held, groups, devices).reshape(units, -1, D)
    return (layer, dtarget, dmemory) + unpack(early_share, middle_share, devices)


def solution(mesh):
    both = ("dp", "fsdp")
    by_rows = P(both, None, None)
    return jax.shard_map(
        per_device,
        mesh=mesh,
        in_specs=(
            by_rows,
            by_rows,
            by_rows,
            P(both, None),
            P(None, both, None),
            P(None, both, None),
            P(None, both),
            P(both, None),
            P(None, both, None),
            P(both, None),
            P(both, None),
            P(None, both),
            P(None, both),
            P(None, both),
            P(both),
            P(),
            by_rows,
            by_rows,
            by_rows,
        ),
        out_specs=(
            by_rows,
            by_rows,
            by_rows,
            P(None, both, None),
            P(None, both, None),
            P(None, both),
            P(both, None),
            P(None, both, None),
            P(both, None),
            P(both, None),
            P(None, both),
            P(None, both),
            P(None, both),
            P(both),
            P(),
        ),
        check_vma=False,
    )
```

```python
import functools

import jax
import jax.numpy as jnp
from jax import lax
from jax.experimental import pallas as pl
from jax.experimental.pallas import tpu as pltpu
from jax.sharding import PartitionSpec as P

D = 256
HEADS = 8
NQ = 100
CLS = 92
IMG_MAX = 12
HEAD_DIM = 32
QP = 128
ROWS = IMG_MAX * QP
PAIRS = HEADS // 2
BLOCK = 256
SIZES = (128, 192, 256, 384, 512)
CHUNK = 512
STEP = 400
FF_BLOCKS = 8
GAIN = 96
BIAS = 100
POS = 128
SMALL = 8
EXTRA = 16
ME = 14

epsilon = 1e-05
masked = -1000000000.0
scale = HEAD_DIM ** (-0.5)
log2e = 1.4426950408889634
gelu_a = 0.7978845608028654
gelu_b = gelu_a * 0.044715
AXES = ("dp", "fsdp")
f32 = jnp.float32
bf16 = jnp.bfloat16


def nn(left, right):
    return jnp.dot(left, right, preferred_element_type=f32)


def nt(left, right):
    return lax.dot_general(left, right, (((1,), (1,)), ((), ())), preferred_element_type=f32)


def tn(left, right):
    return lax.dot_general(left, right, (((0,), (0,)), ((), ())), preferred_element_type=f32)


def total(value):
    return jnp.sum(value, axis=0, keepdims=True)


def norm_parts(value):
    middle = jnp.mean(value, axis=-1, keepdims=True)
    centered = value - middle
    spread = jnp.mean(centered * centered, axis=-1, keepdims=True)
    inverse = lax.rsqrt(spread + epsilon)
    return centered * inverse, inverse


def norm_back(unit, inverse, gain, grad):
    scaled = grad * gain
    first = jnp.mean(scaled, axis=-1, keepdims=True)
    second = jnp.mean(scaled * unit, axis=-1, keepdims=True)
    return inverse * (scaled - first - unit * second)


def gelu_parts(value):
    square = value * value
    cdf = 0.5 + 0.5 * jnp.tanh(value * (gelu_a + gelu_b * square))
    result = value * cdf
    slope = cdf + (result - result * cdf) * (2.0 * gelu_a + 6.0 * gelu_b * square)
    return result, slope


def spread_heads(value, spread_ref):
    lane = lax.broadcasted_iota(jnp.int32, (1, D), 1) // HEAD_DIM
    for head in range(HEADS):
        keep = (lane == head).astype(f32).astype(bf16)
        spread_ref[head * QP : (head + 1) * QP, :] = value * keep


def pair_rows(ref, pair):
    side = pair // 2 * (D // 2)
    return ref[2 * QP * pair : 2 * QP * (pair + 1), side : side + D // 2]


def long_rows(ref, pair):
    return ref[2 * QP * pair : 2 * QP * (pair + 1), :]


def head_lane(lanes):
    return lax.broadcasted_iota(jnp.int32, (1, lanes), 1) // HEAD_DIM


def join_pairs(products):
    lane = head_lane(D)
    result = products[0][:QP]
    for head in range(1, HEADS):
        part = products[head // 2][(head % 2) * QP : (head % 2 + 1) * QP]
        result = jnp.where(lane == head, part, result)
    return result


def join_halves(products):
    lane = head_lane(D // 2)
    halves = []
    for half in range(2):
        low, high = products[2 * half : 2 * half + 2]
        part = jnp.where(lane == 2, high[:QP], high[QP:])
        part = jnp.where(lane == 1, low[QP:], part)
        halves.append(jnp.where(lane == 0, low[:QP], part))
    return jnp.concatenate(halves, axis=1)


def half_lanes(value, pair):
    side = pair // 2 * (D // 2)
    return value[:, side : side + D // 2]


def chunk_loop(size, step):
    def run(body):
        for start in range(0, size, step):
            body(start, slice(start, start + step))

    return run


def attend_block(key, value, spread_ref, valid, halves):
    scores = [nt(half_lanes(key, pair), pair_rows(spread_ref, pair)) for pair in range(PAIRS)]
    attends = []
    logs = []
    for pair in range(PAIRS):
        kept = jnp.where(valid, scores[pair], masked)
        top = jnp.max(kept, axis=0, keepdims=True)
        raised = jnp.exp2((kept - top) * (scale * log2e))
        sums = total(raised)
        attends.append((raised * (1.0 / sums)).astype(bf16))
        logs.append(top * (scale * log2e) + jnp.log2(sums))
    if halves:
        products = [tn(attends[pair], half_lanes(value, pair)) for pair in range(PAIRS)]
        context = join_halves(products)
    else:
        context = join_pairs([tn(attends[pair], value) for pair in range(PAIRS)])
    return context, jnp.concatenate(logs, axis=1)


def place_of(device, bounds, ordered, parts):
    return order_of(device ^ bounds[0, ME], parts) if ordered else device


def early_self_kernel(
    ordered,
    bounds,
    target_ref,
    memory_ref,
    pos_ref,
    mine_ref,
    other_ref,
    after_ref,
    qs_ref,
    ks_ref,
    vs_ref,
    cs_ref,
    inner_ref,
    cq_ref,
    ck_ref,
    cv_ref,
    mean_ref,
    w_ref,
    small_ref,
    flat_ref,
    rows_ref,
    spread_ref,
    block_ref,
    unit_ref,
):
    pack = pl.program_id(0)
    slots = target_ref.shape[1]
    tokens = memory_ref.shape[1]
    near = mine_ref.shape[0]
    parts = 2 * near
    share = D // parts

    @pl.when(pack == 0)
    def _():
        block_ref[0:near] = mine_ref[...]
        block_ref[near:] = other_ref[...]
        for device in range(parts):
            block = block_ref[place_of(device, bounds, ordered, parts)].astype(f32)
            for unit in range(SMALL + 1):
                rows = slice(device * share, (device + 1) * share)
                unit_ref[unit, rows, :] = block[unit * share : (unit + 1) * share]
        w_ref[...] = unit_ref[...].astype(bf16)
        small_ref[...] = unit_ref[SMALL].T

    def bias(index):
        return small_ref[BIAS + index : BIAS + index + 1, :]

    def gain(index):
        return small_ref[GAIN + index : GAIN + index + 1, :]

    inside = lax.broadcasted_iota(jnp.int32, (QP, 1), 0) < NQ
    position = small_ref[POS : POS + QP, :]
    positions = jnp.concatenate([position] * (CHUNK // QP), axis=0)

    mean_ref[0] = jnp.zeros((1, D), f32)
    @chunk_loop(tokens, CHUNK)
    def _(start, rows):
        memory = memory_ref[0, rows, :]
        joined = (memory.astype(f32) + pos_ref[0, rows, :].astype(f32)).astype(bf16)
        ck_ref[0, rows, :] = nn(joined, w_ref[4]).astype(bf16)
        value = (nn(memory, w_ref[5]) + bias(4)).astype(bf16)
        cv_ref[0, rows, :] = value
        mean_ref[0] += total(value.astype(f32)) * (1.0 / tokens)

    flat_ref[0:slots, :] = target_ref[0].astype(f32)
    for image in range(IMG_MAX):
        part = flat_ref[image * NQ : image * NQ + QP, :]
        rows_ref[image * QP : (image + 1) * QP, :] = jnp.where(inside, part, 0.0)

    @chunk_loop(ROWS, CHUNK)
    def _(start, rows):
        target = rows_ref[rows, :]
        joined = (target + positions).astype(bf16)
        qs_ref[0, rows, :] = (nn(joined, w_ref[0]) + bias(0)).astype(bf16)
        ks_ref[0, rows, :] = nn(joined, w_ref[1]).astype(bf16)
        vs_ref[0, rows, :] = (nn(target.astype(bf16), w_ref[2]) + bias(1)).astype(bf16)

    @pl.loop(0, IMG_MAX // 2)
    def _(step):
        for turn in range(2):
            rows = pl.ds(pl.multiple_of((2 * step + turn) * QP, QP), QP)
            spread = spread_ref.at[turn]
            spread_heads(qs_ref[0, rows, :], spread)
            context, unused = attend_block(
                ks_ref[0, rows, :], vs_ref[0, rows, :], spread, inside, True
            )
            cs_ref[0, rows, :] = context.astype(bf16)

    @chunk_loop(ROWS, CHUNK)
    def _(start, rows):
        value = rows_ref[rows, :] + nn(cs_ref[0, rows, :], w_ref[6]) + bias(2)
        inner_ref[0, rows, :] = value
        unit, unused = norm_parts(value)
        after = unit * gain(0) + bias(9)
        after_ref[0, rows, :] = after
        query = nn((after + positions).astype(bf16), w_ref[3]) + bias(3)
        cq_ref[0, rows, :] = query.astype(bf16)


def early_cross_kernel(
    bounds,
    rows_in_ref,
    cq_ref,
    ck_ref,
    cv_ref,
    mean_ref,
    w_ref,
    small_in_ref,
    after_ref,
    cc_ref,
    log_ref,
    rows_ref,
    spread_ref,
    score_ref,
    top_ref,
    sum_ref,
    out_ref,
    bias_ref,
):
    pack = pl.program_id(0)
    tokens = ck_ref.shape[1]

    @pl.when(pack == 0)
    def _():
        bias_ref[...] = small_in_ref[0].astype(f32).T[BIAS + 5 : BIAS + 6]

    @pl.loop(0, IMG_MAX)
    def _(image):
        rows = pl.ds(pl.multiple_of(image * QP, QP), QP)
        first = bounds[pack, image]
        last = bounds[pack, image + 1]
        origin = (first // 16) * 16
        blocks = (last - origin + (BLOCK - 1)) // BLOCK
        spread = spread_ref
        spread_heads(cq_ref[0, rows, :], spread)

        def place_at(block, size=BLOCK):
            wanted = origin + block * size
            start = pl.multiple_of(jnp.minimum(wanted, tokens - size), 16)
            token = start + lax.broadcasted_iota(jnp.int32, (size, 1), 0)
            valid = (token >= jnp.maximum(first, wanted)) & (token < last)
            return pl.ds(start, size), valid

        def fits(index):
            below = SIZES[index - 1] if index else 0
            return (last > first) & (last - origin > below) & (last - origin <= SIZES[index])

        @pl.when(last == first)
        def _():
            cc_ref[0, rows, :] = jnp.broadcast_to(mean_ref[0], (QP, D)).astype(bf16)
            log_ref[0, image] = jnp.zeros((1, HEADS * QP), f32)

        def in_one(size):
            place, valid = place_at(0, size)
            context, logs = attend_block(
                ck_ref[0, place, :], cv_ref[0, place, :], spread, valid, False
            )
            cc_ref[0, rows, :] = context.astype(bf16)
            log_ref[0, image] = logs

        for index, size in enumerate(SIZES):
            pl.when(fits(index))(functools.partial(in_one, size))

        @pl.when(last - origin > SIZES[-1])
        def _():
            top_ref[...] = jnp.full_like(top_ref, masked)
            sum_ref[...] = jnp.zeros_like(sum_ref)
            out_ref[...] = jnp.zeros_like(out_ref)

            @pl.loop(0, blocks)
            def _(block):
                place, valid = place_at(block)
                kept = pl.ds(pl.multiple_of(block * BLOCK, BLOCK), BLOCK)
                key = ck_ref[0, place, :]
                for pair in range(PAIRS):
                    lanes = slice(2 * QP * pair, 2 * QP * (pair + 1))
                    scores = jnp.where(valid, nt(key, long_rows(spread, pair)), masked)
                    score_ref[kept, lanes] = scores
                    top = jnp.max(scores, axis=0, keepdims=True)
                    top_ref[:, lanes] = jnp.maximum(top_ref[:, lanes], top)

            @pl.loop(0, blocks)
            def _(block):
                kept = pl.ds(pl.multiple_of(block * BLOCK, BLOCK), BLOCK)
                raised = jnp.exp2((score_ref[kept, :] - top_ref[...]) * (scale * log2e))
                score_ref[kept, :] = raised
                sum_ref[...] += total(raised)

            @pl.loop(0, blocks)
            def _(block):
                place, unused = place_at(block)
                kept = pl.ds(pl.multiple_of(block * BLOCK, BLOCK), BLOCK)
                value = cv_ref[0, place, :]
                products = []
                for pair in range(PAIRS):
                    lanes = slice(2 * QP * pair, 2 * QP * (pair + 1))
                    attend = (score_ref[kept, lanes] * (1.0 / sum_ref[:, lanes])).astype(bf16)
                    products.append(tn(attend, value))
                out_ref[...] += join_pairs(products)

            cc_ref[0, rows, :] = out_ref[...].astype(bf16)
            log_ref[0, image] = top_ref[...] * (scale * log2e) + jnp.log2(sum_ref[...])

    @chunk_loop(ROWS, CHUNK)
    def _(start, rows):
        rows_ref[rows, :] = rows_in_ref[0, rows, :] + nn(cc_ref[0, rows, :], w_ref[0]) + bias_ref[...]
    for image in range(IMG_MAX):
        after_ref[0, image * NQ : (image + 1) * NQ, :] = rows_ref[image * QP : image * QP + NQ, :]


def lanes_of(count, first, lanes=POS):
    row = lax.broadcasted_iota(jnp.int32, (count, lanes), 0)
    lane = lax.broadcasted_iota(jnp.int32, (count, lanes), 1)
    return (row + first == lane).astype(f32).astype(bf16)


def middle_kernel(
    ordered,
    bounds,
    x_ref,
    cot_ref,
    logit_cot_ref,
    box_cot_ref,
    mine_ref,
    other_ref,
    small_in_ref,
    head_bias_ref,
    layer_ref,
    grad_ref,
    keep_ref,
    send_ref,
    dhead_ref,
    drow_ref,
    small_ref,
    bias_ref,
    box_ref,
    low_ref,
    cross_ref,
    sum_ref,
    branch_ref,
    hidden_ref,
    slope_ref,
    dpre_ref,
    ff_ref,
    dff_ref,
    unit_ref,
):
    pack = pl.program_id(0)
    slots = x_ref.shape[1]
    half = mine_ref.shape[0]
    parts = 2 * half
    ff = FF_BLOCKS * D // parts
    share = D // parts
    near = D // ff
    boxes = 2 * ff
    extra = 2 * ff + 2 * share

    @pl.when(pack == 0)
    def _():
        small_ref[...] = small_in_ref[0].astype(f32).T
        ff_ref[0:half] = mine_ref[...]
        ff_ref[half:] = other_ref[...]
        for device in range(parts):
            place = place_of(device, bounds, ordered, parts)
            pair = ff_ref[place, boxes:extra, :].astype(f32)
            rows = slice(device * share, (device + 1) * share)
            unit_ref[0, rows, :] = pair[:share]
            unit_ref[1, rows, :] = pair[share:]
        box_ref[...] = unit_ref[...].astype(bf16)
        unit_ref[...] = jnp.zeros_like(unit_ref)
        for block in range(FF_BLOCKS):
            rows = [ff_ref[block * near + k, extra : extra + 16, :] for k in range(near)]
            rows = [row.astype(f32)[1:2, 0:ff] for row in rows]
            bias_ref[block] = jnp.concatenate(rows, axis=1)
        bias_ref[FF_BLOCKS:] = jnp.zeros((FF_BLOCKS, 1, D), f32)
        dff_ref[...] = jnp.zeros_like(dff_ref)
        dhead_ref[...] = jnp.zeros_like(dhead_ref)
        drow_ref[...] = jnp.zeros_like(drow_ref)

    def bias(index):
        return small_ref[BIAS + index : BIAS + index + 1, :]

    def gain(index):
        return small_ref[GAIN + index : GAIN + index + 1, :]

    def add_row(column, value):
        row = column - GAIN
        drow_ref[row : row + 1, :] += value

    def near_block(block):
        return pl.ds(block * near, near)

    def shrink(block):
        return ff_ref[near_block(block), 0:ff, :].reshape(D, D)

    def expand(block):
        return ff_ref[near_block(block), ff:boxes, :].reshape(D, D)

    @chunk_loop(slots, STEP)
    def _(start, rows):
        unit, unused = norm_parts(x_ref[0, rows, :])
        after_cross = unit * gain(1) + bias(10)
        cross_ref[rows, :] = after_cross
        low_ref[rows, :] = after_cross.astype(bf16)

    def hide(block):
        value, slope = gelu_parts(nt(low_ref[...], expand(block)) + bias_ref[block])
        hidden_ref[block] = value.astype(bf16)
        slope_ref[block] = slope

    hide(0)
    sum_ref[...] = cross_ref[...] + bias(6)

    @pl.loop(1, FF_BLOCKS)
    def _(block):
        sum_ref[...] += nn(hidden_ref[block - 1], shrink(block - 1))
        hide(block)

    sum_ref[...] += nn(hidden_ref[FF_BLOCKS - 1], shrink(FF_BLOCKS - 1))

    head_weight = small_in_ref[0, :, 0:POS]
    lane = lax.broadcasted_iota(jnp.int32, (1, POS), 1)
    is_box = (lane >= CLS) & (lane < CLS + 4)
    @chunk_loop(slots, STEP)
    def _(start, rows):
        slot = start + lax.broadcasted_iota(jnp.int32, (STEP, 1), 0)
        live = (slot < bounds[pack, IMG_MAX + 1] * NQ).astype(f32)
        unit_ffn, inverse_ffn = norm_parts(sum_ref[rows, :])
        after_ffn = unit_ffn * gain(2) + bias(11)
        layer_ref[0, rows, :] = (after_ffn * live).astype(bf16)
        unit_last, inverse_last = norm_parts(after_ffn)
        normed = (unit_last * gain(3) + bias(12)).astype(bf16)
        one, one_slope = gelu_parts(nn(normed, box_ref[0]) + bias(7))
        box_one = one.astype(bf16)
        two, two_slope = gelu_parts(nn(box_one, box_ref[1]) + bias(8))
        box_two = two.astype(bf16)
        box = jax.nn.sigmoid(nn(box_two, head_weight) + head_bias_ref[0:1, :])

        head_cot = nn(logit_cot_ref[0, rows, :], lanes_of(CLS, 0))
        head_cot = (head_cot + nn(box_cot_ref[0, rows, :], lanes_of(4, CLS))) * live
        grad_box = jnp.where(is_box, head_cot * box * (1.0 - box), 0.0).astype(bf16)
        grad_logit = jnp.where(lane < CLS, head_cot, 0.0).astype(bf16)
        drow_ref[31:32, 0:POS] += total(grad_box.astype(f32)) + total(grad_logit.astype(f32))
        normed_t = normed.T
        grad_two = (two_slope * nt(grad_box, head_weight)).astype(bf16)
        grad_one = (one_slope * nt(grad_two, box_ref[1])).astype(bf16)
        dhead_ref[...] += nn(normed_t, grad_logit) + tn(box_two, grad_box)
        unit_ref[0] += nn(normed_t, grad_one)
        unit_ref[1] += tn(box_one, grad_two)
        add_row(BIAS + 8, total(grad_two.astype(f32)))
        add_row(BIAS + 7, total(grad_one.astype(f32)))
        grad_normed = nt(grad_one, box_ref[0]) + nt(grad_logit, head_weight)
        add_row(GAIN + 3, total(grad_normed * unit_last))
        add_row(BIAS + 12, total(grad_normed))
        grad_after = cot_ref[0, rows, :].astype(f32) * live + norm_back(
            unit_last, inverse_last, gain(3), grad_normed
        )
        add_row(GAIN + 2, total(grad_after * unit_ffn))
        add_row(BIAS + 11, total(grad_after))
        grad_ffn = norm_back(unit_ffn, inverse_ffn, gain(2), grad_after)
        grad_branch = grad_ffn.astype(bf16)
        add_row(BIAS + 6, total(grad_branch.astype(f32)))
        sum_ref[rows, :] = grad_ffn
        branch_ref[rows, :] = grad_branch

    @pl.loop(0, FF_BLOCKS)
    def _(block):
        branch = branch_ref[...]
        dpre = (nt(branch, shrink(block)) * slope_ref[block]).astype(bf16)
        dpre_ref[block] = dpre
        bias_ref[FF_BLOCKS + block] += total(dpre.astype(f32))
        dshrink = tn(hidden_ref[block], branch).reshape(near, ff, D)
        dff_ref[near_block(block), 0:ff, :] += dshrink
        dexpand = tn(dpre, low_ref[...]).reshape(near, ff, D)
        dff_ref[near_block(block), ff:boxes, :] += dexpand

    grad_cross = sum_ref[...]
    for block in range(FF_BLOCKS):
        grad_cross += nn(dpre_ref[block], expand(block))
    sum_ref[...] = grad_cross
    @chunk_loop(slots, STEP)
    def _(start, rows):
        unit, inverse = norm_parts(x_ref[0, rows, :])
        grad = sum_ref[rows, :]
        add_row(GAIN + 1, total(grad * unit))
        add_row(BIAS + 10, total(grad))
        grad_ref[0, rows, :] = norm_back(unit, inverse, gain(1), grad)

    @pl.when(pack == pl.num_programs(0) - 1)
    def _():
        for device in range(parts):
            place = place_of(device, bounds, ordered, parts)
            rows = slice(device * share, (device + 1) * share)
            dff_ref[place, boxes : boxes + share, :] = unit_ref[0, rows, :]
            dff_ref[place, boxes + share : extra, :] = unit_ref[1, rows, :]
        for part in range(parts):
            dff_ref[part, extra : extra + 1, :] = drow_ref[31:32, :]
            side = part % near * ff
            values = bias_ref[FF_BLOCKS + part // near][:, side : side + ff]
            dff_ref[part, extra + 1 : extra + 2, 0:ff] = values
        keep_ref[...] = dff_ref[0:half]
        send_ref[...] = dff_ref[half:].astype(bf16)


def attend_back(key, value, spread, spread_grad, valid, logs, attend_ref, score_ref):
    scores = [nt(half_lanes(key, pair), pair_rows(spread, pair)) for pair in range(PAIRS)]
    grads = [nt(half_lanes(value, pair), pair_rows(spread_grad, pair)) for pair in range(PAIRS)]
    lows = []
    for pair in range(PAIRS):
        lanes = slice(2 * QP * pair, 2 * QP * (pair + 1))
        if logs is None:
            kept = jnp.where(valid, scores[pair], masked)
            top = jnp.max(kept, axis=0, keepdims=True)
            raised = jnp.exp2((kept - top) * (scale * log2e))
            attend = raised * (1.0 / total(raised))
        else:
            attend = jnp.exp2(scores[pair] * (scale * log2e) - logs[:, lanes])
            attend = jnp.where(valid, attend, 0.0)
        row_dot = total(attend * grads[pair])
        low = (attend * (grads[pair] - row_dot)).astype(bf16)
        attend_ref[:, lanes] = attend.astype(bf16)
        score_ref[:, lanes] = low
        lows.append(low)
    return join_halves([tn(lows[pair], half_lanes(key, pair)) for pair in range(PAIRS)]) * scale


def late_cross_kernel(
    bounds,
    grad_ref,
    memory_ref,
    pos_ref,
    w_ref,
    cq_ref,
    ck_ref,
    cv_ref,
    cc_ref,
    log_ref,
    gq_ref,
    dmemory_ref,
    dw_ref,
    drows_ref,
    flat_ref,
    grad_rows_ref,
    context_ref,
    dv_ref,
    spread_ref,
    spread_grad_ref,
    attend_ref,
    score_ref,
    sum_ref,
    out_ref,
):
    pack = pl.program_id(0)
    slots = grad_ref.shape[1]
    tokens = memory_ref.shape[1]

    @pl.when(pack == 0)
    def _():
        dw_ref[...] = jnp.zeros_like(dw_ref)
        drows_ref[...] = jnp.zeros_like(drows_ref)

    def add_row(row, value):
        drows_ref[row : row + 1, :] += value

    inside = lax.broadcasted_iota(jnp.int32, (QP, 1), 0) < NQ

    flat_ref[0:slots, :] = grad_ref[0]
    for image in range(IMG_MAX):
        part = flat_ref[image * NQ : image * NQ + QP, :]
        grad_rows_ref[image * QP : (image + 1) * QP, :] = jnp.where(inside, part, 0.0)
    @chunk_loop(ROWS, CHUNK)
    def _(start, rows):
        branch = grad_rows_ref[rows, :].astype(bf16)
        add_row(1, total(branch.astype(f32)))
        dw_ref[2] += tn(cc_ref[0, rows, :], branch)
        context_ref[rows, :] = nt(branch, w_ref[7]).astype(bf16)
    dmemory_ref[...] = jnp.zeros_like(dmemory_ref)
    dv_ref[...] = jnp.zeros_like(dv_ref)

    @pl.loop(0, IMG_MAX)
    def _(image):
        rows = pl.ds(pl.multiple_of(image * QP, QP), QP)
        first = bounds[pack, image]
        last = bounds[pack, image + 1]
        origin = (first // 16) * 16
        blocks = (last - origin + (BLOCK - 1)) // BLOCK
        spread = spread_ref
        spread_grad = spread_grad_ref
        attend_low = attend_ref
        score_low = score_ref
        spread_heads(cq_ref[0, rows, :], spread)
        spread_heads(context_ref[rows, :], spread_grad)
        logs = log_ref[0, image]

        def place_at(block, size=BLOCK):
            wanted = origin + block * size
            start = pl.multiple_of(jnp.minimum(wanted, tokens - size), 16)
            token = start + lax.broadcasted_iota(jnp.int32, (size, 1), 0)
            valid = (token >= jnp.maximum(first, wanted)) & (token < last)
            return pl.ds(start, size), valid

        def fits(index):
            below = SIZES[index - 1] if index else 0
            return (last > first) & (last - origin > below) & (last - origin <= SIZES[index])

        @pl.when(last == first)
        def _():
            gq_ref[0, rows, :] = jnp.zeros((QP, D), bf16)

        def in_one(size):
            place, valid = place_at(0, size)
            attend_part = attend_low.at[0:size]
            score_part = score_low.at[0:size]
            grad_query = attend_back(
                ck_ref[0, place, :],
                cv_ref[0, place, :],
                spread,
                spread_grad,
                valid,
                logs,
                attend_part,
                score_part,
            )
            gq_ref[0, rows, :] = grad_query.astype(bf16)
            dv_ref[place, :] += nn(attend_part[...], spread_grad[...])
            dmemory_ref[0, place, :] += nn(score_part[...], spread[...])

        for index, size in enumerate(SIZES):
            pl.when(fits(index))(functools.partial(in_one, size))

        @pl.when(last - origin > SIZES[-1])
        def _():
            sum_ref[...] = jnp.zeros_like(sum_ref)
            out_ref[...] = jnp.zeros_like(out_ref)

            @pl.loop(0, blocks)
            def _(block):
                place, valid = place_at(block)
                for pair in range(PAIRS):
                    lanes = slice(2 * QP * pair, 2 * QP * (pair + 1))
                    scores = nt(ck_ref[0, place, :], long_rows(spread, pair))
                    attend = jnp.exp2(scores * (scale * log2e) - logs[:, lanes])
                    attend = jnp.where(valid, attend, 0.0)
                    grad_attend = nt(cv_ref[0, place, :], long_rows(spread_grad, pair))
                    sum_ref[:, lanes] += total(attend * grad_attend)

            @pl.loop(0, blocks)
            def _(block):
                place, valid = place_at(block)
                key = ck_ref[0, place, :]
                products = []
                for pair in range(PAIRS):
                    lanes = slice(2 * QP * pair, 2 * QP * (pair + 1))
                    scores = nt(ck_ref[0, place, :], long_rows(spread, pair))
                    attend = jnp.exp2(scores * (scale * log2e) - logs[:, lanes])
                    attend = jnp.where(valid, attend, 0.0)
                    grad_attend = nt(cv_ref[0, place, :], long_rows(spread_grad, pair))
                    grad_scores = attend * (grad_attend - sum_ref[:, lanes])
                    grad_scores = grad_scores.astype(bf16)
                    attend_low[0:BLOCK, lanes] = attend.astype(bf16)
                    score_low[0:BLOCK, lanes] = grad_scores
                    products.append(tn(grad_scores, half_lanes(key, pair)))
                out_ref[...] += join_halves(products)
                dv_ref[place, :] += nn(attend_low[0:BLOCK, :], spread_grad[...])
                dmemory_ref[0, place, :] += nn(score_low[0:BLOCK, :], spread[...])

            gq_ref[0, rows, :] = (out_ref[...] * scale).astype(bf16)

    @chunk_loop(tokens, CHUNK)
    def _(start, rows):
        memory = memory_ref[0, rows, :]
        joined = (memory.astype(f32) + pos_ref[0, rows, :].astype(f32)).astype(bf16)
        grad_key = (dmemory_ref[0, rows, :] * scale).astype(bf16)
        grad_value = dv_ref[rows, :].astype(bf16)
        dmemory_ref[0, rows, :] = nt(grad_key, w_ref[4]) + nt(grad_value, w_ref[5])
        add_row(0, total(grad_value.astype(f32)))
        dw_ref[0] += tn(joined, grad_key)
        dw_ref[1] += tn(memory, grad_value)


def late_self_kernel(
    ordered,
    bounds,
    grad_ref,
    gcq_ref,
    target_ref,
    w_ref,
    qs_ref,
    ks_ref,
    vs_ref,
    cs_ref,
    inner_ref,
    dcross_ref,
    dcross_rows_ref,
    dhead_ref,
    drow_ref,
    dtarget_ref,
    keep_ref,
    send_ref,
    small_ref,
    flat_ref,
    grad_rows_ref,
    place_ref,
    context_ref,
    gq_ref,
    gk_ref,
    gv_ref,
    spread_ref,
    spread_grad_ref,
    attend_ref,
    score_ref,
    drows_ref,
    dw_ref,
    block_ref,
):
    pack = pl.program_id(0)
    slots = target_ref.shape[1]

    @pl.when(pack == 0)
    def _():
        small_ref[...] = w_ref[SMALL].astype(f32).T
        dw_ref[0:4] = jnp.zeros((4, D, D), f32)
        dw_ref[4:6] = dcross_ref[0:2]
        dw_ref[6] = jnp.zeros((D, D), f32)
        dw_ref[7] = dcross_ref[2]
        drows_ref[...] = jnp.zeros_like(drows_ref)
        drows_ref[GAIN : GAIN + 32, :] = drow_ref[...]
        drows_ref[BIAS + 4 : BIAS + 6, :] += dcross_rows_ref[0:2, :]

    def bias(index):
        return small_ref[BIAS + index : BIAS + index + 1, :]

    def gain(index):
        return small_ref[GAIN + index : GAIN + index + 1, :]

    def add_row(row, value):
        drows_ref[row : row + 1, :] += value

    inside = lax.broadcasted_iota(jnp.int32, (QP, 1), 0) < NQ
    position = small_ref[POS : POS + QP, :]
    positions = jnp.concatenate([position] * (CHUNK // QP), axis=0)

    flat_ref[0:slots, :] = grad_ref[0]
    for image in range(IMG_MAX):
        part = flat_ref[image * NQ : image * NQ + QP, :]
        grad_rows_ref[image * QP : (image + 1) * QP, :] = jnp.where(inside, part, 0.0)
    flat_ref[0:slots, :] = target_ref[0].astype(f32)

    @chunk_loop(ROWS, CHUNK)
    def _(start, rows):
        unit, inverse = norm_parts(inner_ref[0, rows, :])
        cross_in = (unit * gain(0) + bias(9) + positions).astype(bf16)
        grad_query = gcq_ref[0, rows, :]
        add_row(BIAS + 3, total(grad_query.astype(f32)))
        dw_ref[3] += tn(cross_in, grad_query)
        place = nt(grad_query, w_ref[3])
        place_ref[rows, :] = place
        grad = grad_rows_ref[rows, :] + place
        add_row(GAIN, total(grad * unit))
        add_row(BIAS + 9, total(grad))
        grad = norm_back(unit, inverse, gain(0), grad)
        grad_rows_ref[rows, :] = grad
        branch = grad.astype(bf16)
        add_row(BIAS + 2, total(branch.astype(f32)))
        dw_ref[6] += tn(cs_ref[0, rows, :], branch)
        context_ref[rows, :] = nt(branch, w_ref[6]).astype(bf16)

    @pl.loop(0, IMG_MAX // 2)
    def _(step):
        for turn in range(2):
            rows = pl.ds(pl.multiple_of((2 * step + turn) * QP, QP), QP)
            spread = spread_ref.at[turn]
            spread_grad = spread_grad_ref.at[turn]
            attend_low = attend_ref.at[turn * QP : (turn + 1) * QP]
            score_low = score_ref.at[turn * QP : (turn + 1) * QP]
            spread_heads(qs_ref[0, rows, :], spread)
            spread_heads(context_ref[rows, :], spread_grad)
            grad_query = attend_back(
                ks_ref[0, rows, :],
                vs_ref[0, rows, :],
                spread,
                spread_grad,
                inside,
                None,
                attend_low,
                score_low,
            )
            gq_ref[rows, :] = grad_query.astype(bf16)
            gv_ref[rows, :] = nn(attend_low[...], spread_grad[...]).astype(bf16)
            gk_ref[rows, :] = (nn(score_low[...], spread[...]) * scale).astype(bf16)

    for start in range(0, ROWS, CHUNK):
        rows = slice(start, start + CHUNK)
        images = range(start // QP, (start + CHUNK) // QP)
        parts = [flat_ref[image * NQ : image * NQ + QP, :] for image in images]
        target = jnp.concatenate([jnp.where(inside, part, 0.0) for part in parts], axis=0)
        joined_t = (target + positions).astype(bf16).T
        grad_query = gq_ref[rows, :]
        grad_key = gk_ref[rows, :]
        grad_value = gv_ref[rows, :]
        add_row(BIAS + 0, total(grad_query.astype(f32)))
        add_row(BIAS + 1, total(grad_value.astype(f32)))
        dw_ref[0] += nn(joined_t, grad_query)
        dw_ref[1] += nn(joined_t, grad_key)
        dw_ref[2] += tn(target.astype(bf16), grad_value)
        grad_joined = nt(grad_query, w_ref[0]) + nt(grad_key, w_ref[1])
        grad_rows_ref[rows, :] += grad_joined + nt(grad_value, w_ref[2])
        grad_place = grad_joined + place_ref[rows, :]
        for image in range(CHUNK // QP):
            drows_ref[POS : POS + QP, :] += grad_place[image * QP : (image + 1) * QP, :]
    for image in range(IMG_MAX):
        part = grad_rows_ref[image * QP : image * QP + NQ, :]
        dtarget_ref[0, image * NQ : (image + 1) * NQ, :] = part

    @pl.when(pack == pl.num_programs(0) - 1)
    def _():
        small = drows_ref[...].T
        dw_ref[SMALL, :, POS:] = small[:, POS:]
        dw_ref[SMALL, :, :POS] = small[:, :POS] + dhead_ref[...]
        half, height, unused = keep_ref.shape
        parts = 2 * half
        share = D // parts
        used = (SMALL + 1) * share
        if height > used:
            block_ref[:, used:, :] = jnp.zeros((parts, height - used, D), f32)
        for device in range(parts):
            place = place_of(device, bounds, ordered, parts)
            rows = slice(device * share, (device + 1) * share)
            for unit in range(SMALL + 1):
                block_ref[place, unit * share : (unit + 1) * share, :] = dw_ref[unit, rows, :]
        keep_ref[...] = block_ref[0:half]
        send_ref[...] = block_ref[half:].astype(bf16)


def whole(shape):
    zeros = (0,) * len(shape)
    return pl.BlockSpec(shape, lambda *unused: zeros)


def by_pack(shape):
    zeros = (0,) * (len(shape) - 1)
    return pl.BlockSpec((1,) + tuple(shape[1:]), lambda pack, *unused: (pack,) + zeros)


LIMIT = 60 * 1024 * 1024


def params(axes):
    return pltpu.CompilerParams(
        dimension_semantics=("arbitrary",) * axes, vmem_limit_bytes=LIMIT
    )


def early_self(bounds, target, memory, memory_pos, mine, other, ordered):
    packs, slots, unused = target.shape
    tokens = memory.shape[1]
    height = mine.shape[1]
    wide = HEADS * QP
    low_rows = jax.ShapeDtypeStruct((packs, ROWS, D), bf16)
    rows = jax.ShapeDtypeStruct((packs, ROWS, D), f32)
    low_tokens = jax.ShapeDtypeStruct((packs, tokens, D), bf16)
    mean = jax.ShapeDtypeStruct((packs, 1, D), f32)
    outs = [rows] + [low_rows] * 4 + [rows, low_rows, low_tokens, low_tokens, mean]
    units = jax.ShapeDtypeStruct((SMALL + 1, D, D), bf16)
    return pl.pallas_call(
        functools.partial(early_self_kernel, ordered),
        grid_spec=pltpu.PrefetchScalarGridSpec(
            num_scalar_prefetch=1,
            grid=(packs,),
            in_specs=[
                by_pack(target.shape),
                by_pack(memory.shape),
                by_pack(memory_pos.shape),
                whole(mine.shape),
                whole(other.shape),
            ],
            out_specs=[by_pack(out.shape) for out in outs] + [whole(units.shape)],
            scratch_shapes=[
                pltpu.VMEM((D, D), f32),
                pltpu.VMEM((slots + 32, D), f32),
                pltpu.VMEM((ROWS, D), f32),
                pltpu.VMEM((2, wide, D), bf16),
                pltpu.VMEM((2 * mine.shape[0], height, D), bf16),
                pltpu.VMEM((SMALL + 1, D, D), f32),
            ],
        ),
        out_shape=outs + [units],
        compiler_params=params(1),
        cost_estimate=pl.CostEstimate(
            flops=packs * 8_000_000_000, bytes_accessed=packs * 9_000_000, transcendentals=0
        ),
        name="early_self",
    )(bounds, target, memory, memory_pos, mine, other)


def early_cross(bounds, rows, query, key, value, mean, weights, slots):
    packs = rows.shape[0]
    tokens = key.shape[1]
    wide = HEADS * QP
    outs = [
        jax.ShapeDtypeStruct((packs, slots, D), f32),
        jax.ShapeDtypeStruct(query.shape, bf16),
        jax.ShapeDtypeStruct((packs, IMG_MAX, 1, wide), f32),
    ]
    arrays = [rows, query, key, value, mean]
    return pl.pallas_call(
        early_cross_kernel,
        grid_spec=pltpu.PrefetchScalarGridSpec(
            num_scalar_prefetch=1,
            grid=(packs,),
            in_specs=[by_pack(array.shape) for array in arrays]
            + [
                pl.BlockSpec((1, D, D), lambda *unused: (7, 0, 0)),
                pl.BlockSpec((1, D, D), lambda *unused: (SMALL, 0, 0)),
            ],
            out_specs=[by_pack(out.shape) for out in outs],
            scratch_shapes=[
                pltpu.VMEM((ROWS, D), f32),
                pltpu.VMEM((wide, D), bf16),
                pltpu.VMEM((tokens, wide), f32),
                pltpu.VMEM((1, wide), f32),
                pltpu.VMEM((1, wide), f32),
                pltpu.VMEM((QP, D), f32),
                pltpu.VMEM((1, D), f32),
            ],
        ),
        out_shape=outs,
        compiler_params=params(1),
        cost_estimate=pl.CostEstimate(
            flops=packs * 8_000_000_000, bytes_accessed=packs * 7_000_000, transcendentals=0
        ),
        name="early_cross",
    )(bounds, *arrays, weights, weights)


def middle(bounds, x, cotangents, mine, other, small, head_bias, ordered):
    packs, slots, unused = x.shape
    half, height, unused = mine.shape
    outs = [
        jax.ShapeDtypeStruct(x.shape, bf16),
        jax.ShapeDtypeStruct(x.shape, f32),
        jax.ShapeDtypeStruct(mine.shape, f32),
        jax.ShapeDtypeStruct(mine.shape, bf16),
        jax.ShapeDtypeStruct((D, POS), f32),
        jax.ShapeDtypeStruct((32, D), f32),
    ]
    return pl.pallas_call(
        functools.partial(middle_kernel, ordered),
        grid_spec=pltpu.PrefetchScalarGridSpec(
            num_scalar_prefetch=1,
            grid=(packs,),
            in_specs=[
                by_pack(x.shape),
                *[by_pack(array.shape) for array in cotangents],
                whole(mine.shape),
                whole(other.shape),
                pl.BlockSpec((1, D, D), lambda *unused: (SMALL, 0, 0)),
                whole(head_bias.shape),
            ],
            out_specs=[by_pack(x.shape), by_pack(x.shape)] + [whole(out.shape) for out in outs[2:]],
            scratch_shapes=[
                pltpu.VMEM((D, D), f32),
                pltpu.VMEM((2 * FF_BLOCKS, 1, D), f32),
                pltpu.VMEM((2, D, D), bf16),
                pltpu.VMEM((slots, D), bf16),
                pltpu.VMEM((slots, D), f32),
                pltpu.VMEM((slots, D), f32),
                pltpu.VMEM((slots, D), bf16),
                pltpu.VMEM((FF_BLOCKS, slots, D), bf16),
                pltpu.VMEM((FF_BLOCKS, slots, D), f32),
                pltpu.VMEM((FF_BLOCKS, slots, D), bf16),
                pltpu.VMEM((2 * half, height, D), bf16),
                pltpu.VMEM((2 * half, height, D), f32),
                pltpu.VMEM((2, D, D), f32),
            ],
        ),
        out_shape=outs,
        compiler_params=params(1),
        cost_estimate=pl.CostEstimate(
            flops=packs * 10_000_000_000, bytes_accessed=packs * 9_000_000, transcendentals=0
        ),
        name="middle",
    )(bounds, x, *cotangents, mine, other, small, head_bias)


def late_cross(bounds, grad, memory, memory_pos, weights, saved):
    packs, slots, unused = grad.shape
    tokens = memory.shape[1]
    wide = HEADS * QP
    outs = [
        jax.ShapeDtypeStruct((packs, ROWS, D), bf16),
        jax.ShapeDtypeStruct(memory.shape, f32),
        jax.ShapeDtypeStruct((3, D, D), f32),
        jax.ShapeDtypeStruct((8, D), f32),
    ]
    return pl.pallas_call(
        late_cross_kernel,
        grid_spec=pltpu.PrefetchScalarGridSpec(
            num_scalar_prefetch=1,
            grid=(packs,),
            in_specs=[
                by_pack(grad.shape),
                by_pack(memory.shape),
                by_pack(memory_pos.shape),
                whole(weights.shape),
            ]
            + [by_pack(array.shape) for array in saved],
            out_specs=[by_pack(outs[0].shape), by_pack(outs[1].shape)]
            + [whole(out.shape) for out in outs[2:]],
            scratch_shapes=[
                pltpu.VMEM((slots + 32, D), f32),
                pltpu.VMEM((ROWS, D), f32),
                pltpu.VMEM((ROWS, D), bf16),
                pltpu.VMEM((tokens, D), f32),
                pltpu.VMEM((wide, D), bf16),
                pltpu.VMEM((wide, D), bf16),
                pltpu.VMEM((SIZES[-1], wide), bf16),
                pltpu.VMEM((SIZES[-1], wide), bf16),
                pltpu.VMEM((1, wide), f32),
                pltpu.VMEM((QP, D), f32),
            ],
        ),
        out_shape=outs,
        compiler_params=params(1),
        cost_estimate=pl.CostEstimate(
            flops=packs * 12_000_000_000, bytes_accessed=packs * 9_000_000, transcendentals=0
        ),
        name="late_cross",
    )(bounds, grad, memory, memory_pos, weights, *saved)


def late_self(bounds, grad, grad_query, target, weights, saved, sums, block, ordered):
    packs, slots, unused = target.shape
    wide = HEADS * QP
    half, height, unused = block
    outs = [
        jax.ShapeDtypeStruct(target.shape, f32),
        jax.ShapeDtypeStruct(block, f32),
        jax.ShapeDtypeStruct(block, bf16),
    ]
    return pl.pallas_call(
        functools.partial(late_self_kernel, ordered),
        grid_spec=pltpu.PrefetchScalarGridSpec(
            num_scalar_prefetch=1,
            grid=(packs,),
            in_specs=[
                by_pack(grad.shape),
                by_pack(grad_query.shape),
                by_pack(target.shape),
                whole(weights.shape),
            ]
            + [by_pack(array.shape) for array in saved]
            + [whole(array.shape) for array in sums],
            out_specs=[by_pack(target.shape), whole(block), whole(block)],
            scratch_shapes=[
                pltpu.VMEM((D, D), f32),
                pltpu.VMEM((slots + 32, D), f32),
                pltpu.VMEM((ROWS, D), f32),
                pltpu.VMEM((ROWS, D), f32),
                pltpu.VMEM((ROWS, D), bf16),
                pltpu.VMEM((ROWS, D), bf16),
                pltpu.VMEM((ROWS, D), bf16),
                pltpu.VMEM((ROWS, D), bf16),
                pltpu.VMEM((2, wide, D), bf16),
                pltpu.VMEM((2, wide, D), bf16),
                pltpu.VMEM((2 * QP, wide), bf16),
                pltpu.VMEM((2 * QP, wide), bf16),
                pltpu.VMEM((D, D), f32),
                pltpu.VMEM(weights.shape, f32),
                pltpu.VMEM((2 * half, height, D), f32),
            ],
        ),
        out_shape=outs,
        compiler_params=params(1),
        cost_estimate=pl.CostEstimate(
            flops=packs * 10_000_000_000, bytes_accessed=packs * 7_000_000, transcendentals=0
        ),
        name="late_self",
    )(bounds, grad, grad_query, target, weights, *saved, *sums)


def stack(parts):
    return jnp.concatenate(parts, axis=0)


def fold(keep, received, count):
    for part in received:
        keep = keep + part.astype(f32)
    size = keep.shape[0] // count
    pieces = [keep[index * size : (index + 1) * size] for index in range(count)]
    return pieces[:1] + [piece.astype(bf16) for piece in pieces[1:]]


def run_of_images(segment, me):
    edge = jnp.arange(16, dtype=jnp.int32)
    below = segment[:, None, :] < edge[None, :, None]
    counts = jnp.sum(below.astype(jnp.int32), axis=-1)
    images = jnp.max(jnp.where(segment < IMG_MAX, segment + 1, 0), axis=-1)
    result = jnp.where(edge[None, :] == IMG_MAX + 1, images[:, None], counts)
    return jnp.where(edge[None, :] == ME, me, result)


def taller(rows):
    return jnp.pad(rows, ((0, -rows.shape[0] % 16), (0, 0)))


def pack_early(project, output, classes, box_final, query_pos, gains, biases):
    share = project.shape[1]
    columns = [
        classes,
        box_final,
        gains.T,
        biases.T,
        jnp.zeros((share, POS - BIAS - 13), bf16),
        query_pos.T,
        jnp.zeros((share, D - POS - NQ), bf16),
    ]
    small = jnp.concatenate(columns, axis=1)
    return taller(jnp.concatenate([project.reshape(-1, D), output.reshape(-1, D), small], axis=0))


def pack_middle(box, shrink, expand, expand_bias):
    extra = jnp.pad(expand_bias[None], ((1, EXTRA - 2), (0, D - expand_bias.shape[0])))
    return taller(jnp.concatenate([shrink, expand.T, box[0], box[1], extra], axis=0))


def pack_kernel(
    project,
    output,
    classes,
    final_t,
    gains,
    shifts_t,
    places_t,
    shrink,
    expand_t,
    box,
    row,
    out,
):
    share = project.shape[1]
    small = nn(classes[...], lanes_of(CLS, 0, D)) + tn(final_t[...], lanes_of(4, CLS, D))
    small += tn(gains[...], lanes_of(4, GAIN, D)) + nn(shifts_t[...], lanes_of(13, BIAS, D))
    small += nn(places_t[...], lanes_of(NQ, POS, D))
    first = [project[...].astype(f32).reshape(-1, D), output[...].astype(f32).reshape(-1, D), small]
    first = jnp.concatenate(first, axis=0)
    rest = -first.shape[0] % 16
    count = row.shape[1]
    vector = nn(row[...], lanes_of(count, 0, D))
    index = lax.broadcasted_iota(jnp.int32, (EXTRA, 1), 0)
    extra = jnp.where(index == 1, vector, 0.0)
    blocks = [first, jnp.zeros((rest, D), f32), shrink[...].astype(f32), expand_t[...].astype(f32)]
    blocks += [box[...].astype(f32).reshape(2 * share, D), extra]
    out[...] = jnp.concatenate(blocks, axis=0).astype(bf16)


def pack_both(project, output, classes, final, places, gains, shifts, box, shrink, expand, row):
    share = project.shape[1]
    early_rows = (SMALL + 1) * share
    early_rows += -early_rows % 16
    if share % 8:
        first = pack_early(project, output, classes, final, places, gains, shifts)
        return jnp.concatenate([first, pack_middle(box, shrink, expand, row)]), early_rows
    rows = early_rows + 2 * shrink.shape[0] + 2 * share + EXTRA
    block = pl.pallas_call(
        pack_kernel,
        out_shape=jax.ShapeDtypeStruct((rows, D), bf16),
        name="pack",
    )(
        project,
        output,
        classes,
        final.T,
        gains,
        shifts.T,
        places.T,
        shrink,
        expand.T,
        box,
        row[None],
    )
    return block, early_rows


def block_rows(devices):
    return [FF_BLOCKS * D // devices] * 2 + [D // devices] * 2


def cut(blocks, devices):
    marks = [0]
    for rows in block_rows(devices):
        marks.append(marks[-1] + rows)
    return [blocks[:, low:high] for low, high in zip(marks, marks[1:])], blocks[:, marks[-1] :]


def regroup(blocks, devices, parts):
    pieces, extra = cut(blocks, devices)
    pieces = [piece.reshape(parts, -1, D) for piece in pieces]
    head = jnp.broadcast_to(extra[0:1, 0:1], (parts, 1, D))
    row = extra[:, 1, : FF_BLOCKS * D // devices].reshape(parts, 1, -1)
    row = jnp.pad(row, ((0, 0), (0, EXTRA - 2), (0, D - row.shape[2])))
    result = jnp.concatenate(pieces + [head, row], axis=1)
    return jnp.pad(result, ((0, 0), (0, -result.shape[1] % 16), (0, 0)))


def regroup_units(blocks, devices, parts):
    units = SMALL + 1
    share = D // devices
    result = blocks[:, : units * share].reshape(devices, units, share, D).swapaxes(0, 1)
    result = result.reshape(units, parts, D // parts, D).swapaxes(0, 1).reshape(parts, -1, D)
    return jnp.pad(result, ((0, 0), (0, -result.shape[1] % 16), (0, 0)))


def parts_of(devices):
    return devices if FF_BLOCKS * D // devices % 16 == 0 else FF_BLOCKS


def bit_groups(devices):
    bits = [1 << k for k in range(1, devices.bit_length() - 1)]
    groups = [(1,)]
    while bits:
        groups.append((bits[0], bits[-1]) if len(bits) > 1 else (bits[0],))
        bits = bits[1:-1]
    return groups


def order_of(distance, devices):
    place = 0
    for bits in bit_groups(devices):
        for bit in bits[::-1]:
            place = 2 * place + distance // bit % 2
    return place


def mixes(bits):
    result = [0]
    for bit in bits:
        result += [mix | bit for mix in result]
    return result


def swap(value, bits, devices):
    return lax.ppermute(value, AXES, [(k, k ^ bits) for k in range(devices)])


def trade(held, bits, devices):
    return [swap(held, mix, devices) if mix else held for mix in mixes(bits)]


def deliver(sends, bits, devices):
    return [swap(send, mix, devices) for mix, send in zip(mixes(bits)[1:], sends)]


def counted(blocks, devices, me):
    places = [order_of(device, devices) for device in range(devices)]
    order = jnp.array(places)[jnp.arange(devices) ^ me]
    return jnp.take(blocks, order, axis=0)


def stepped(blocks, devices, me):
    distances = [0] * devices
    for device in range(devices):
        distances[order_of(device, devices)] = device
    return jnp.take(blocks, jnp.array(distances) ^ me, axis=0)


def unpack_middle(block, devices):
    pieces, extra = cut(block[None], devices)
    shrink, expand, box_one, box_two = [piece[0] for piece in pieces]
    row = extra[0, 1, 0 : shrink.shape[0]]
    return shrink, expand.T, jnp.stack([box_one, box_two]), row, extra[0, 0, 0 : CLS + 4]


def finish_kernel(count, keep, *refs):
    total_block = keep[0]
    for ref in refs[:count]:
        total_block += ref[0].astype(f32)
    project, output, classes, final_t, places_t, gains, shifts_t = refs[count:]
    share = project.shape[1]
    project[...] = total_block[: 6 * share].reshape(6, share, D)
    output[...] = total_block[6 * share : 8 * share].reshape(2, share, D)
    small = total_block[8 * share : 9 * share]
    classes[...] = small[:, 0:CLS]
    places_t[...] = small[:, POS : POS + NQ]
    shifts_t[...] = small[:, BIAS : BIAS + 13]
    turned = small[:, 0:POS].T
    final_t[...] = turned[CLS : CLS + 4]
    gains[...] = turned[GAIN : GAIN + 4]


def finish_early(keep, received, devices):
    share = D // devices
    if share % 8:
        return unpack_early(fold(keep, received, 1)[0][0], devices)
    shapes = [(6, share, D), (2, share, D), (share, CLS), (4, share), (share, NQ), (4, share)]
    shapes.append((share, 13))
    project, output, classes, final_t, places_t, gains, shifts_t = pl.pallas_call(
        functools.partial(finish_kernel, len(received)),
        out_shape=[jax.ShapeDtypeStruct(shape, f32) for shape in shapes],
        name="finish",
    )(keep, *received)
    return project, output, classes, final_t.T, places_t.T, gains, shifts_t.T


def unpack_early(block, devices):
    units = SMALL + 1
    share = D // devices
    block = block[: units * share].reshape(units, share, D)
    small = block[SMALL]
    return (
        block[0:6],
        block[6:8],
        small[:, 0:CLS],
        small[:, CLS : CLS + 4],
        small[:, POS : POS + NQ].T,
        small[:, GAIN : GAIN + 4].T,
        small[:, BIAS : BIAS + 13].T,
    )


def per_device(
    target,
    memory,
    memory_pos,
    segment,
    project_weight,
    output_weight,
    expand_weight,
    shrink_weight,
    box_weight,
    class_weight,
    box_final,
    query_pos,
    norm_gains,
    biases,
    expand_bias,
    head_bias,
    output_cotangent,
    logit_cotangent,
    box_cotangent,
):
    devices = lax.axis_size(AXES)
    me = lax.axis_index(AXES)
    groups = bit_groups(devices)
    parts = parts_of(devices)
    ordered = parts == devices
    slots = target.shape[1]

    both, height = pack_both(
        project_weight,
        output_weight,
        class_weight,
        box_final,
        query_pos,
        norm_gains,
        biases,
        box_weight,
        shrink_weight,
        expand_weight,
        expand_bias,
    )
    both = both[None]
    both_parts = trade(both, groups[-1], devices)
    early_held = stack([part[:, :height] for part in both_parts])
    middle_held = stack([part[:, height:] for part in both_parts])
    for bits in groups[-2:1:-1]:
        early_held = stack(trade(early_held, bits, devices))
    early_parts = trade(early_held, groups[1], devices)
    bounds = run_of_images(segment, me)
    head_row = jnp.pad(head_bias.astype(f32), (0, POS - CLS - 4))
    head_row = jnp.broadcast_to(head_row[None], (8, POS))
    early_parts, bounds, head_row, middle_held = lax.optimization_barrier(
        (early_parts, bounds, head_row, middle_held)
    )
    early_mine = stack(early_parts)
    early_other = swap(early_mine, 1, devices)
    if not ordered:
        blocks = counted(jnp.concatenate([early_mine, early_other]), devices, me)
        blocks = regroup_units(blocks, devices, parts)
        early_mine, early_other = blocks[: parts // 2], blocks[parts // 2 :]
    middle_parts = trade(middle_held, groups[-2], devices)
    rows, *saved = early_self(
        bounds, target, memory, memory_pos, early_mine, early_other, ordered
    )
    query, key, value, mean, weights = saved[5:]
    middle_parts, query = lax.optimization_barrier((middle_parts, query))
    for bits in groups[-3:0:-1]:
        middle_parts = trade(stack(middle_parts), bits, devices)
    middle_mine = stack(middle_parts)
    middle_mine, query = lax.optimization_barrier((middle_mine, query))
    middle_other = swap(middle_mine, 1, devices)
    after, context, logs = early_cross(bounds, rows, query, key, value, mean, weights, slots)
    if not ordered:
        blocks = counted(jnp.concatenate([middle_mine, middle_other]), devices, me)
        blocks = regroup(blocks, devices, parts)
        middle_mine, middle_other = blocks[: parts // 2], blocks[parts // 2 :]
    layer, grad, keep, send, dhead, drow = middle(
        bounds,
        after,
        [output_cotangent, logit_cotangent, box_cotangent],
        middle_mine,
        middle_other,
        weights,
        head_row,
        ordered,
    )

    def real_blocks(keep, send, change):
        if ordered:
            return keep, send
        blocks = jnp.concatenate([keep, send.astype(f32)])
        blocks = stepped(change(blocks, parts, devices), devices, me)
        return blocks[: devices // 2], blocks[devices // 2 :].astype(bf16)

    def counts(index):
        return 1 << len(groups[index]) if index < len(groups) else 1

    keep, send = real_blocks(keep, send, regroup)
    keep, *sends = fold(keep, deliver([send], groups[0], devices), counts(1))
    grad, keep, sends = lax.optimization_barrier((grad, keep, sends))
    received = deliver(sends, groups[1], devices)
    grad_query, dmemory, dcross, dcross_rows = late_cross(
        bounds, grad, memory, memory_pos, weights, [query, key, value, context, logs]
    )
    keep, *sends = fold(keep, received, counts(2))
    grad_query, keep, sends = lax.optimization_barrier((grad_query, keep, sends))
    received = deliver(sends, groups[2], devices)
    sums = [dcross, dcross_rows, dhead, drow]
    block = early_mine.shape
    dtarget, early_keep, early_send = late_self(
        bounds, grad, grad_query, target, weights, saved[:5], sums, block, ordered
    )
    early_keep, early_send, received = lax.optimization_barrier(
        (early_keep, early_send, received)
    )
    for index in range(3, len(groups)):
        keep, *sends = fold(keep, received, counts(index))
        received = deliver(sends, groups[index], devices)
    early_keep, early_send = real_blocks(early_keep, early_send, regroup_units)
    early_received = deliver([early_send], groups[0], devices)
    early_keep, *sends = fold(early_keep, early_received, counts(1))
    middle_sum = fold(keep, received, 1)[0]
    sends, middle_sum = lax.optimization_barrier((sends, middle_sum))
    early_received = deliver(sends, groups[1], devices)
    middle_grads = unpack_middle(middle_sum[0], devices)
    early_received, middle_grads = lax.optimization_barrier((early_received, middle_grads))
    for index in range(2, len(groups)):
        early_keep, *sends = fold(early_keep, early_received, counts(index))
        early_received = deliver(sends, groups[index], devices)
    shrink, expand, box, expand_row, head = middle_grads
    project, output, classes, final, places, gains, shifts = finish_early(
        early_keep, early_received, devices
    )
    return (
        layer,
        dtarget,
        dmemory,
        project,
        output,
        expand,
        shrink,
        box,
        classes,
        final,
        places,
        gains,
        shifts,
        expand_row,
        head,
    )


def solution(mesh):
    both = ("dp", "fsdp")
    by_rows = P(both, None, None)
    return jax.shard_map(
        per_device,
        mesh=mesh,
        in_specs=(
            by_rows,
            by_rows,
            by_rows,
            P(both, None),
            P(None, both, None),
            P(None, both, None),
            P(None, both),
            P(both, None),
            P(None, both, None),
            P(both, None),
            P(both, None),
            P(None, both),
            P(None, both),
            P(None, both),
            P(both),
            P(),
            by_rows,
            by_rows,
            by_rows,
        ),
        out_specs=(
            by_rows,
            by_rows,
            by_rows,
            P(None, both, None),
            P(None, both, None),
            P(None, both),
            P(both, None),
            P(None, both, None),
            P(both, None),
            P(both, None),
            P(None, both),
            P(None, both),
            P(None, both),
            P(both),
            P(),
        ),
        check_vma=False,
    )
```

```python
import functools

import jax
import jax.numpy as jnp
from jax import lax
from jax.experimental import pallas as pl
from jax.experimental.pallas import tpu as pltpu
from jax.sharding import PartitionSpec as P

D = 256
HEADS = 8
NQ = 100
CLS = 92
IMG_MAX = 12
HEAD_DIM = 32
QP = 128
ROWS = IMG_MAX * QP
PAIRS = HEADS // 2
BLOCK = 256
SIZES = (128, 192, 256, 384, 512)
SHORT = (128, 192, 256, 512)
CHUNK = 512
STEP = 400
FF_BLOCKS = 8
GAIN = 96
BIAS = 100
POS = 128
SMALL = 8
EXTRA = 16
ME = 14

epsilon = 1e-05
masked = -1000000000.0
scale = HEAD_DIM ** (-0.5)
log2e = 1.4426950408889634
gelu_a = 0.7978845608028654
gelu_b = gelu_a * 0.044715
AXES = ("dp", "fsdp")
f32 = jnp.float32
bf16 = jnp.bfloat16


def nn(left, right):
    return jnp.dot(left, right, preferred_element_type=f32)


def nt(left, right):
    return lax.dot_general(left, right, (((1,), (1,)), ((), ())), preferred_element_type=f32)


def tn(left, right):
    return lax.dot_general(left, right, (((0,), (0,)), ((), ())), preferred_element_type=f32)


def total(value):
    return jnp.sum(value, axis=0, keepdims=True)


def norm_parts(value):
    middle = jnp.mean(value, axis=-1, keepdims=True)
    centered = value - middle
    spread = jnp.mean(centered * centered, axis=-1, keepdims=True)
    inverse = lax.rsqrt(spread + epsilon)
    return centered * inverse, inverse


def norm_back(unit, inverse, gain, grad):
    scaled = grad * gain
    first = jnp.mean(scaled, axis=-1, keepdims=True)
    second = jnp.mean(scaled * unit, axis=-1, keepdims=True)
    return inverse * (scaled - first - unit * second)


def gelu_parts(value):
    square = value * value
    cdf = 0.5 + 0.5 * jnp.tanh(value * (gelu_a + gelu_b * square))
    result = value * cdf
    slope = cdf + (result - result * cdf) * (2.0 * gelu_a + 6.0 * gelu_b * square)
    return result, slope


def spread_heads(value, spread_ref):
    lane = lax.broadcasted_iota(jnp.int32, (1, D), 1) // HEAD_DIM
    for head in range(HEADS):
        keep = (lane == head).astype(f32).astype(bf16)
        spread_ref[head * QP : (head + 1) * QP, :] = value * keep


def pair_rows(ref, pair):
    side = pair // 2 * (D // 2)
    return ref[2 * QP * pair : 2 * QP * (pair + 1), side : side + D // 2]


def long_rows(ref, pair):
    return ref[2 * QP * pair : 2 * QP * (pair + 1), :]


def head_lane(lanes):
    return lax.broadcasted_iota(jnp.int32, (1, lanes), 1) // HEAD_DIM


def join_pairs(products):
    lane = head_lane(D)
    result = products[0][:QP]
    for head in range(1, HEADS):
        part = products[head // 2][(head % 2) * QP : (head % 2 + 1) * QP]
        result = jnp.where(lane == head, part, result)
    return result


def join_halves(products):
    lane = head_lane(D // 2)
    halves = []
    for half in range(2):
        low, high = products[2 * half : 2 * half + 2]
        part = jnp.where(lane == 2, high[:QP], high[QP:])
        part = jnp.where(lane == 1, low[QP:], part)
        halves.append(jnp.where(lane == 0, low[:QP], part))
    return jnp.concatenate(halves, axis=1)


def half_lanes(value, pair):
    side = pair // 2 * (D // 2)
    return value[:, side : side + D // 2]


def row_loop(size, step):
    def run(body):
        @pl.loop(0, size // step)
        def _(index):
            start = pl.multiple_of(index * step, step)
            body(start, pl.ds(start, step))

    return run


def chunk_loop(size, step):
    def run(body):
        for start in range(0, size, step):
            body(start, slice(start, start + step))

    return run


def attend_block(key, value, spread_ref, valid, halves):
    scores = [nt(half_lanes(key, pair), pair_rows(spread_ref, pair)) for pair in range(PAIRS)]
    attends = []
    logs = []
    for pair in range(PAIRS):
        kept = jnp.where(valid, scores[pair], masked)
        top = jnp.max(kept, axis=0, keepdims=True)
        raised = jnp.exp2((kept - top) * (scale * log2e))
        sums = total(raised)
        attends.append((raised * (1.0 / sums)).astype(bf16))
        logs.append(top * (scale * log2e) + jnp.log2(sums))
    if halves:
        products = [tn(attends[pair], half_lanes(value, pair)) for pair in range(PAIRS)]
        context = join_halves(products)
    else:
        context = join_pairs([tn(attends[pair], value) for pair in range(PAIRS)])
    return context, jnp.concatenate(logs, axis=1)


def place_of(device, bounds, ordered, parts):
    return order_of(device ^ bounds[0, ME], parts) if ordered else device


def early_self_kernel(
    ordered,
    bounds,
    target_ref,
    memory_ref,
    pos_ref,
    mine_ref,
    other_ref,
    after_ref,
    qs_ref,
    ks_ref,
    vs_ref,
    cs_ref,
    inner_ref,
    cq_ref,
    ck_ref,
    cv_ref,
    mean_ref,
    w_ref,
    small_ref,
    flat_ref,
    rows_ref,
    spread_ref,
    block_ref,
    unit_ref,
):
    pack = pl.program_id(0)
    slots = target_ref.shape[1]
    tokens = memory_ref.shape[1]
    near = mine_ref.shape[0]
    parts = 2 * near
    share = D // parts

    @pl.when(pack == 0)
    def _():
        block_ref[0:near] = mine_ref[...]
        block_ref[near:] = other_ref[...]

        @pl.loop(0, parts)
        def _(device):
            block = block_ref[place_of(device, bounds, ordered, parts)].astype(f32)
            rows = pl.ds(pl.multiple_of(device * share, share), share)
            for unit in range(SMALL + 1):
                unit_ref[unit, rows, :] = block[unit * share : (unit + 1) * share]

        w_ref[...] = unit_ref[...].astype(bf16)
        small_ref[...] = unit_ref[SMALL].T

    def bias(index):
        return small_ref[BIAS + index : BIAS + index + 1, :]

    def gain(index):
        return small_ref[GAIN + index : GAIN + index + 1, :]

    inside = lax.broadcasted_iota(jnp.int32, (QP, 1), 0) < NQ
    position = small_ref[POS : POS + QP, :]
    positions = jnp.concatenate([position] * (CHUNK // QP), axis=0)

    mean_ref[0] = jnp.zeros((1, D), f32)
    @chunk_loop(tokens, CHUNK)
    def _(start, rows):
        memory = memory_ref[0, rows, :]
        joined = (memory.astype(f32) + pos_ref[0, rows, :].astype(f32)).astype(bf16)
        ck_ref[0, rows, :] = nn(joined, w_ref[4]).astype(bf16)
        value = (nn(memory, w_ref[5]) + bias(4)).astype(bf16)
        cv_ref[0, rows, :] = value
        mean_ref[0] += total(value.astype(f32)) * (1.0 / tokens)

    flat_ref[0:slots, :] = target_ref[0].astype(f32)
    for image in range(IMG_MAX):
        part = flat_ref[image * NQ : image * NQ + QP, :]
        rows_ref[image * QP : (image + 1) * QP, :] = jnp.where(inside, part, 0.0)

    @chunk_loop(ROWS, CHUNK)
    def _(start, rows):
        target = rows_ref[rows, :]
        joined = (target + positions).astype(bf16)
        qs_ref[0, rows, :] = (nn(joined, w_ref[0]) + bias(0)).astype(bf16)
        ks_ref[0, rows, :] = nn(joined, w_ref[1]).astype(bf16)
        vs_ref[0, rows, :] = (nn(target.astype(bf16), w_ref[2]) + bias(1)).astype(bf16)

    @pl.loop(0, IMG_MAX // 2)
    def _(step):
        for turn in range(2):
            rows = pl.ds(pl.multiple_of((2 * step + turn) * QP, QP), QP)
            spread = spread_ref.at[turn]
            spread_heads(qs_ref[0, rows, :], spread)
            context, unused = attend_block(
                ks_ref[0, rows, :], vs_ref[0, rows, :], spread, inside, True
            )
            cs_ref[0, rows, :] = context.astype(bf16)

    @chunk_loop(ROWS, CHUNK)
    def _(start, rows):
        value = rows_ref[rows, :] + nn(cs_ref[0, rows, :], w_ref[6]) + bias(2)
        inner_ref[0, rows, :] = value
        unit, unused = norm_parts(value)
        after = unit * gain(0) + bias(9)
        after_ref[0, rows, :] = after
        query = nn((after + positions).astype(bf16), w_ref[3]) + bias(3)
        cq_ref[0, rows, :] = query.astype(bf16)


def early_cross_kernel(
    bounds,
    rows_in_ref,
    cq_ref,
    ck_ref,
    cv_ref,
    mean_ref,
    w_ref,
    small_in_ref,
    after_ref,
    cc_ref,
    log_ref,
    rows_ref,
    spread_ref,
    score_ref,
    top_ref,
    sum_ref,
    out_ref,
    bias_ref,
):
    pack = pl.program_id(0)
    tokens = ck_ref.shape[1]

    @pl.when(pack == 0)
    def _():
        bias_ref[...] = small_in_ref[0].astype(f32).T[BIAS + 5 : BIAS + 6]

    @pl.loop(0, IMG_MAX)
    def _(image):
        rows = pl.ds(pl.multiple_of(image * QP, QP), QP)
        first = bounds[pack, image]
        last = bounds[pack, image + 1]
        origin = (first // 16) * 16
        blocks = (last - origin + (BLOCK - 1)) // BLOCK
        spread = spread_ref
        spread_heads(cq_ref[0, rows, :], spread)

        def place_at(block, size=BLOCK):
            wanted = origin + block * size
            start = pl.multiple_of(jnp.minimum(wanted, tokens - size), 16)
            token = start + lax.broadcasted_iota(jnp.int32, (size, 1), 0)
            valid = (token >= jnp.maximum(first, wanted)) & (token < last)
            return pl.ds(start, size), valid

        def fits(index):
            below = SHORT[index - 1] if index else 0
            return (last > first) & (last - origin > below) & (last - origin <= SHORT[index])

        @pl.when(last == first)
        def _():
            cc_ref[0, rows, :] = jnp.broadcast_to(mean_ref[0], (QP, D)).astype(bf16)
            log_ref[0, image] = jnp.zeros((1, HEADS * QP), f32)

        def in_one(size):
            place, valid = place_at(0, size)
            context, logs = attend_block(
                ck_ref[0, place, :], cv_ref[0, place, :], spread, valid, False
            )
            cc_ref[0, rows, :] = context.astype(bf16)
            log_ref[0, image] = logs

        for index, size in enumerate(SHORT):
            pl.when(fits(index))(functools.partial(in_one, size))

        @pl.when(last - origin > SHORT[-1])
        def _():
            top_ref[...] = jnp.full_like(top_ref, masked)
            sum_ref[...] = jnp.zeros_like(sum_ref)
            out_ref[...] = jnp.zeros_like(out_ref)

            @pl.loop(0, blocks)
            def _(block):
                place, valid = place_at(block)
                kept = pl.ds(pl.multiple_of(block * BLOCK, BLOCK), BLOCK)
                key = ck_ref[0, place, :]
                for pair in range(PAIRS):
                    lanes = slice(2 * QP * pair, 2 * QP * (pair + 1))
                    scores = jnp.where(valid, nt(key, long_rows(spread, pair)), masked)
                    score_ref[kept, lanes] = scores
                    top = jnp.max(scores, axis=0, keepdims=True)
                    top_ref[:, lanes] = jnp.maximum(top_ref[:, lanes], top)

            @pl.loop(0, blocks)
            def _(block):
                kept = pl.ds(pl.multiple_of(block * BLOCK, BLOCK), BLOCK)
                raised = jnp.exp2((score_ref[kept, :] - top_ref[...]) * (scale * log2e))
                score_ref[kept, :] = raised
                sum_ref[...] += total(raised)

            @pl.loop(0, blocks)
            def _(block):
                place, unused = place_at(block)
                kept = pl.ds(pl.multiple_of(block * BLOCK, BLOCK), BLOCK)
                value = cv_ref[0, place, :]
                products = []
                for pair in range(PAIRS):
                    lanes = slice(2 * QP * pair, 2 * QP * (pair + 1))
                    attend = (score_ref[kept, lanes] * (1.0 / sum_ref[:, lanes])).astype(bf16)
                    products.append(tn(attend, value))
                out_ref[...] += join_pairs(products)

            cc_ref[0, rows, :] = out_ref[...].astype(bf16)
            log_ref[0, image] = top_ref[...] * (scale * log2e) + jnp.log2(sum_ref[...])

    @chunk_loop(ROWS, CHUNK)
    def _(start, rows):
        rows_ref[rows, :] = rows_in_ref[0, rows, :] + nn(cc_ref[0, rows, :], w_ref[0]) + bias_ref[...]
    for image in range(IMG_MAX):
        after_ref[0, image * NQ : (image + 1) * NQ, :] = rows_ref[image * QP : image * QP + NQ, :]


def lanes_of(count, first, lanes=POS):
    row = lax.broadcasted_iota(jnp.int32, (count, lanes), 0)
    lane = lax.broadcasted_iota(jnp.int32, (count, lanes), 1)
    return (row + first == lane).astype(f32).astype(bf16)


def middle_kernel(
    ordered,
    bounds,
    x_ref,
    cot_ref,
    head_cot_ref,
    mine_ref,
    other_ref,
    small_in_ref,
    head_bias_ref,
    layer_ref,
    grad_ref,
    keep_ref,
    send_ref,
    dhead_ref,
    drow_ref,
    small_ref,
    bias_ref,
    box_ref,
    low_ref,
    cross_ref,
    sum_ref,
    branch_ref,
    hidden_ref,
    slope_ref,
    ff_ref,
    dff_ref,
    unit_ref,
):
    pack = pl.program_id(0)
    slots = x_ref.shape[1]
    half = mine_ref.shape[0]
    parts = 2 * half
    ff = FF_BLOCKS * D // parts
    share = D // parts
    near = D // ff
    boxes = 2 * ff
    extra = 2 * ff + 2 * share

    @pl.when(pack == 0)
    def _():
        small_ref[...] = small_in_ref[0].astype(f32).T
        ff_ref[0:half] = mine_ref[...]
        ff_ref[half:] = other_ref[...]

        @pl.loop(0, parts)
        def _(device):
            place = place_of(device, bounds, ordered, parts)
            pair = ff_ref[place, boxes:extra, :].astype(f32)
            rows = pl.ds(pl.multiple_of(device * share, share), share)
            unit_ref[0, rows, :] = pair[:share]
            unit_ref[1, rows, :] = pair[share:]

        box_ref[...] = unit_ref[...].astype(bf16)
        unit_ref[...] = jnp.zeros_like(unit_ref)
        for block in range(FF_BLOCKS):
            rows = [ff_ref[block * near + k, extra : extra + 16, :] for k in range(near)]
            rows = [row.astype(f32)[1:2, 0:ff] for row in rows]
            bias_ref[block] = jnp.concatenate(rows, axis=1)
        bias_ref[FF_BLOCKS:] = jnp.zeros((FF_BLOCKS, 1, D), f32)
        dff_ref[...] = jnp.zeros_like(dff_ref)
        dhead_ref[...] = jnp.zeros_like(dhead_ref)
        drow_ref[...] = jnp.zeros_like(drow_ref)

    def bias(index):
        return small_ref[BIAS + index : BIAS + index + 1, :]

    def gain(index):
        return small_ref[GAIN + index : GAIN + index + 1, :]

    def add_row(column, value):
        row = column - GAIN
        drow_ref[row : row + 1, :] += value

    def near_block(block):
        return pl.ds(block * near, near)

    def shrink(block):
        return ff_ref[near_block(block), 0:ff, :].reshape(D, D)

    def expand(block):
        return ff_ref[near_block(block), ff:boxes, :].reshape(D, D)

    @row_loop(slots, STEP)
    def _(start, rows):
        unit, unused = norm_parts(x_ref[0, rows, :])
        after_cross = unit * gain(1) + bias(10)
        cross_ref[rows, :] = after_cross
        low_ref[rows, :] = after_cross.astype(bf16)

    sum_ref[...] = cross_ref[...] + bias(6)
    hidden_ref[FF_BLOCKS - 1] = jnp.zeros((slots, D), bf16)

    @pl.loop(0, FF_BLOCKS)
    def _(block):
        before = (block + FF_BLOCKS - 1) % FF_BLOCKS
        sum_ref[...] += nn(hidden_ref[before], shrink(before))
        value, slope = gelu_parts(nt(low_ref[...], expand(block)) + bias_ref[block])
        hidden_ref[block] = value.astype(bf16)
        slope_ref[block] = slope

    sum_ref[...] += nn(hidden_ref[FF_BLOCKS - 1], shrink(FF_BLOCKS - 1))

    head_weight = small_in_ref[0, :, 0:POS]
    lane = lax.broadcasted_iota(jnp.int32, (1, POS), 1)
    is_box = (lane >= CLS) & (lane < CLS + 4)
    @chunk_loop(slots, STEP)
    def _(start, rows):
        slot = start + lax.broadcasted_iota(jnp.int32, (STEP, 1), 0)
        live = (slot < bounds[pack, IMG_MAX + 1] * NQ).astype(f32)
        unit_ffn, inverse_ffn = norm_parts(sum_ref[rows, :])
        after_ffn = unit_ffn * gain(2) + bias(11)
        layer_ref[0, rows, :] = (after_ffn * live).astype(bf16)
        unit_last, inverse_last = norm_parts(after_ffn)
        normed = (unit_last * gain(3) + bias(12)).astype(bf16)
        one, one_slope = gelu_parts(nn(normed, box_ref[0]) + bias(7))
        box_one = one.astype(bf16)
        two, two_slope = gelu_parts(nn(box_one, box_ref[1]) + bias(8))
        box_two = two.astype(bf16)
        box = jax.nn.sigmoid(nn(box_two, head_weight) + head_bias_ref[0:1, :])

        head_cot = head_cot_ref[0, rows, :].astype(f32) * live
        grad_box = jnp.where(is_box, head_cot * box * (1.0 - box), 0.0).astype(bf16)
        grad_logit = jnp.where(lane < CLS, head_cot, 0.0).astype(bf16)
        drow_ref[31:32, 0:POS] += total(grad_box.astype(f32)) + total(grad_logit.astype(f32))
        normed_t = normed.T
        grad_two = (two_slope * nt(grad_box, head_weight)).astype(bf16)
        grad_one = (one_slope * nt(grad_two, box_ref[1])).astype(bf16)
        dhead_ref[...] += nn(normed_t, grad_logit) + tn(box_two, grad_box)
        unit_ref[0] += nn(normed_t, grad_one)
        unit_ref[1] += tn(box_one, grad_two)
        add_row(BIAS + 8, total(grad_two.astype(f32)))
        add_row(BIAS + 7, total(grad_one.astype(f32)))
        grad_normed = nt(grad_one, box_ref[0]) + nt(grad_logit, head_weight)
        add_row(GAIN + 3, total(grad_normed * unit_last))
        add_row(BIAS + 12, total(grad_normed))
        grad_after = cot_ref[0, rows, :].astype(f32) * live + norm_back(
            unit_last, inverse_last, gain(3), grad_normed
        )
        add_row(GAIN + 2, total(grad_after * unit_ffn))
        add_row(BIAS + 11, total(grad_after))
        grad_ffn = norm_back(unit_ffn, inverse_ffn, gain(2), grad_after)
        grad_branch = grad_ffn.astype(bf16)
        add_row(BIAS + 6, total(grad_branch.astype(f32)))
        sum_ref[rows, :] = grad_ffn
        branch_ref[rows, :] = grad_branch

    @pl.loop(0, FF_BLOCKS)
    def _(block):
        branch = branch_ref[...]
        dpre = (nt(branch, shrink(block)) * slope_ref[block]).astype(bf16)
        bias_ref[FF_BLOCKS + block] += total(dpre.astype(f32))
        dshrink = tn(hidden_ref[block], branch).reshape(near, ff, D)
        dff_ref[near_block(block), 0:ff, :] += dshrink
        dexpand = tn(dpre, low_ref[...]).reshape(near, ff, D)
        dff_ref[near_block(block), ff:boxes, :] += dexpand
        sum_ref[...] += nn(dpre, expand(block))

    @row_loop(slots, STEP)
    def _(start, rows):
        unit, inverse = norm_parts(x_ref[0, rows, :])
        grad = sum_ref[rows, :]
        add_row(GAIN + 1, total(grad * unit))
        add_row(BIAS + 10, total(grad))
        grad_ref[0, rows, :] = norm_back(unit, inverse, gain(1), grad)

    @pl.when(pack == pl.num_programs(0) - 1)
    def _():
        @pl.loop(0, parts)
        def _(device):
            place = place_of(device, bounds, ordered, parts)
            rows = pl.ds(pl.multiple_of(device * share, share), share)
            dff_ref[place, boxes : boxes + share, :] = unit_ref[0, rows, :]
            dff_ref[place, boxes + share : extra, :] = unit_ref[1, rows, :]

        for part in range(parts):
            dff_ref[part, extra : extra + 1, :] = drow_ref[31:32, :]
            side = part % near * ff
            values = bias_ref[FF_BLOCKS + part // near][:, side : side + ff]
            dff_ref[part, extra + 1 : extra + 2, 0:ff] = values
        keep_ref[...] = dff_ref[0:half]
        send_ref[...] = dff_ref[half:].astype(bf16)


def attend_back(key, value, spread, spread_grad, valid, logs, attend_ref, score_ref):
    scores = [nt(half_lanes(key, pair), pair_rows(spread, pair)) for pair in range(PAIRS)]
    grads = [nt(half_lanes(value, pair), pair_rows(spread_grad, pair)) for pair in range(PAIRS)]
    lows = []
    for pair in range(PAIRS):
        lanes = slice(2 * QP * pair, 2 * QP * (pair + 1))
        if logs is None:
            kept = jnp.where(valid, scores[pair], masked)
            top = jnp.max(kept, axis=0, keepdims=True)
            raised = jnp.exp2((kept - top) * (scale * log2e))
            attend = raised * (1.0 / total(raised))
        else:
            attend = jnp.exp2(scores[pair] * (scale * log2e) - logs[:, lanes])
            attend = jnp.where(valid, attend, 0.0)
        row_dot = total(attend * grads[pair])
        low = (attend * (grads[pair] - row_dot)).astype(bf16)
        attend_ref[:, lanes] = attend.astype(bf16)
        score_ref[:, lanes] = low
        lows.append(low)
    return join_halves([tn(lows[pair], half_lanes(key, pair)) for pair in range(PAIRS)]) * scale


def late_cross_kernel(
    bounds,
    grad_ref,
    memory_ref,
    pos_ref,
    w_ref,
    cq_ref,
    ck_ref,
    cv_ref,
    cc_ref,
    log_ref,
    gq_ref,
    dmemory_ref,
    dw_ref,
    drows_ref,
    flat_ref,
    grad_rows_ref,
    context_ref,
    dv_ref,
    spread_ref,
    spread_grad_ref,
    attend_ref,
    score_ref,
    sum_ref,
    out_ref,
):
    pack = pl.program_id(0)
    slots = grad_ref.shape[1]
    tokens = memory_ref.shape[1]

    @pl.when(pack == 0)
    def _():
        dw_ref[...] = jnp.zeros_like(dw_ref)
        drows_ref[...] = jnp.zeros_like(drows_ref)

    def add_row(row, value):
        drows_ref[row : row + 1, :] += value

    inside = lax.broadcasted_iota(jnp.int32, (QP, 1), 0) < NQ

    flat_ref[0:slots, :] = grad_ref[0]
    for image in range(IMG_MAX):
        part = flat_ref[image * NQ : image * NQ + QP, :]
        grad_rows_ref[image * QP : (image + 1) * QP, :] = jnp.where(inside, part, 0.0)
    @chunk_loop(ROWS, CHUNK)
    def _(start, rows):
        branch = grad_rows_ref[rows, :].astype(bf16)
        add_row(1, total(branch.astype(f32)))
        dw_ref[2] += tn(cc_ref[0, rows, :], branch)
        context_ref[rows, :] = nt(branch, w_ref[7]).astype(bf16)
    dmemory_ref[...] = jnp.zeros_like(dmemory_ref)
    dv_ref[...] = jnp.zeros_like(dv_ref)

    @pl.loop(0, IMG_MAX)
    def _(image):
        rows = pl.ds(pl.multiple_of(image * QP, QP), QP)
        first = bounds[pack, image]
        last = bounds[pack, image + 1]
        origin = (first // 16) * 16
        blocks = (last - origin + (BLOCK - 1)) // BLOCK
        spread = spread_ref
        spread_grad = spread_grad_ref
        attend_low = attend_ref
        score_low = score_ref
        spread_heads(cq_ref[0, rows, :], spread)
        spread_heads(context_ref[rows, :], spread_grad)
        logs = log_ref[0, image]

        def place_at(block, size=BLOCK):
            wanted = origin + block * size
            start = pl.multiple_of(jnp.minimum(wanted, tokens - size), 16)
            token = start + lax.broadcasted_iota(jnp.int32, (size, 1), 0)
            valid = (token >= jnp.maximum(first, wanted)) & (token < last)
            return pl.ds(start, size), valid

        def fits(index):
            below = SIZES[index - 1] if index else 0
            return (last > first) & (last - origin > below) & (last - origin <= SIZES[index])

        @pl.when(last == first)
        def _():
            gq_ref[0, rows, :] = jnp.zeros((QP, D), bf16)

        def in_one(size):
            place, valid = place_at(0, size)
            attend_part = attend_low.at[0:size]
            score_part = score_low.at[0:size]
            grad_query = attend_back(
                ck_ref[0, place, :],
                cv_ref[0, place, :],
                spread,
                spread_grad,
                valid,
                logs,
                attend_part,
                score_part,
            )
            gq_ref[0, rows, :] = grad_query.astype(bf16)
            dv_ref[place, :] += nn(attend_part[...], spread_grad[...])
            dmemory_ref[0, place, :] += nn(score_part[...], spread[...])

        for index, size in enumerate(SIZES):
            pl.when(fits(index))(functools.partial(in_one, size))

        @pl.when(last - origin > SIZES[-1])
        def _():
            sum_ref[...] = jnp.zeros_like(sum_ref)
            out_ref[...] = jnp.zeros_like(out_ref)

            @pl.loop(0, blocks)
            def _(block):
                place, valid = place_at(block)
                for pair in range(PAIRS):
                    lanes = slice(2 * QP * pair, 2 * QP * (pair + 1))
                    scores = nt(ck_ref[0, place, :], long_rows(spread, pair))
                    attend = jnp.exp2(scores * (scale * log2e) - logs[:, lanes])
                    attend = jnp.where(valid, attend, 0.0)
                    grad_attend = nt(cv_ref[0, place, :], long_rows(spread_grad, pair))
                    sum_ref[:, lanes] += total(attend * grad_attend)

            @pl.loop(0, blocks)
            def _(block):
                place, valid = place_at(block)
                key = ck_ref[0, place, :]
                products = []
                for pair in range(PAIRS):
                    lanes = slice(2 * QP * pair, 2 * QP * (pair + 1))
                    scores = nt(ck_ref[0, place, :], long_rows(spread, pair))
                    attend = jnp.exp2(scores * (scale * log2e) - logs[:, lanes])
                    attend = jnp.where(valid, attend, 0.0)
                    grad_attend = nt(cv_ref[0, place, :], long_rows(spread_grad, pair))
                    grad_scores = attend * (grad_attend - sum_ref[:, lanes])
                    grad_scores = grad_scores.astype(bf16)
                    attend_low[0:BLOCK, lanes] = attend.astype(bf16)
                    score_low[0:BLOCK, lanes] = grad_scores
                    products.append(tn(grad_scores, half_lanes(key, pair)))
                out_ref[...] += join_halves(products)
                dv_ref[place, :] += nn(attend_low[0:BLOCK, :], spread_grad[...])
                dmemory_ref[0, place, :] += nn(score_low[0:BLOCK, :], spread[...])

            gq_ref[0, rows, :] = (out_ref[...] * scale).astype(bf16)

    @chunk_loop(tokens, CHUNK)
    def _(start, rows):
        memory = memory_ref[0, rows, :]
        joined = (memory.astype(f32) + pos_ref[0, rows, :].astype(f32)).astype(bf16)
        grad_key = (dmemory_ref[0, rows, :] * scale).astype(bf16)
        grad_value = dv_ref[rows, :].astype(bf16)
        dmemory_ref[0, rows, :] = nt(grad_key, w_ref[4]) + nt(grad_value, w_ref[5])
        add_row(0, total(grad_value.astype(f32)))
        dw_ref[0] += tn(joined, grad_key)
        dw_ref[1] += tn(memory, grad_value)


def late_self_kernel(
    ordered,
    bounds,
    grad_ref,
    gcq_ref,
    target_ref,
    w_ref,
    qs_ref,
    ks_ref,
    vs_ref,
    cs_ref,
    inner_ref,
    dcross_ref,
    dcross_rows_ref,
    dhead_ref,
    drow_ref,
    dtarget_ref,
    keep_ref,
    send_ref,
    small_ref,
    flat_ref,
    grad_rows_ref,
    place_ref,
    context_ref,
    gq_ref,
    gk_ref,
    gv_ref,
    spread_ref,
    spread_grad_ref,
    attend_ref,
    score_ref,
    drows_ref,
    dw_ref,
    block_ref,
):
    pack = pl.program_id(0)
    slots = target_ref.shape[1]

    @pl.when(pack == 0)
    def _():
        small_ref[...] = w_ref[SMALL].astype(f32).T
        dw_ref[0:4] = jnp.zeros((4, D, D), f32)
        dw_ref[4:6] = dcross_ref[0:2]
        dw_ref[6] = jnp.zeros((D, D), f32)
        dw_ref[7] = dcross_ref[2]
        drows_ref[...] = jnp.zeros_like(drows_ref)
        drows_ref[GAIN : GAIN + 32, :] = drow_ref[...]
        drows_ref[BIAS + 4 : BIAS + 6, :] += dcross_rows_ref[0:2, :]

    def bias(index):
        return small_ref[BIAS + index : BIAS + index + 1, :]

    def gain(index):
        return small_ref[GAIN + index : GAIN + index + 1, :]

    def add_row(row, value):
        drows_ref[row : row + 1, :] += value

    inside = lax.broadcasted_iota(jnp.int32, (QP, 1), 0) < NQ
    position = small_ref[POS : POS + QP, :]
    positions = jnp.concatenate([position] * (CHUNK // QP), axis=0)

    flat_ref[0:slots, :] = grad_ref[0]
    for image in range(IMG_MAX):
        part = flat_ref[image * NQ : image * NQ + QP, :]
        grad_rows_ref[image * QP : (image + 1) * QP, :] = jnp.where(inside, part, 0.0)
    flat_ref[0:slots, :] = target_ref[0].astype(f32)

    @chunk_loop(ROWS, CHUNK)
    def _(start, rows):
        unit, inverse = norm_parts(inner_ref[0, rows, :])
        cross_in = (unit * gain(0) + bias(9) + positions).astype(bf16)
        grad_query = gcq_ref[0, rows, :]
        add_row(BIAS + 3, total(grad_query.astype(f32)))
        dw_ref[3] += tn(cross_in, grad_query)
        place = nt(grad_query, w_ref[3])
        place_ref[rows, :] = place
        grad = grad_rows_ref[rows, :] + place
        add_row(GAIN, total(grad * unit))
        add_row(BIAS + 9, total(grad))
        grad = norm_back(unit, inverse, gain(0), grad)
        grad_rows_ref[rows, :] = grad
        branch = grad.astype(bf16)
        add_row(BIAS + 2, total(branch.astype(f32)))
        dw_ref[6] += tn(cs_ref[0, rows, :], branch)
        context_ref[rows, :] = nt(branch, w_ref[6]).astype(bf16)

    @pl.loop(0, IMG_MAX // 2)
    def _(step):
        for turn in range(2):
            rows = pl.ds(pl.multiple_of((2 * step + turn) * QP, QP), QP)
            spread = spread_ref.at[turn]
            spread_grad = spread_grad_ref.at[turn]
            attend_low = attend_ref.at[turn * QP : (turn + 1) * QP]
            score_low = score_ref.at[turn * QP : (turn + 1) * QP]
            spread_heads(qs_ref[0, rows, :], spread)
            spread_heads(context_ref[rows, :], spread_grad)
            grad_query = attend_back(
                ks_ref[0, rows, :],
                vs_ref[0, rows, :],
                spread,
                spread_grad,
                inside,
                None,
                attend_low,
                score_low,
            )
            gq_ref[rows, :] = grad_query.astype(bf16)
            gv_ref[rows, :] = nn(attend_low[...], spread_grad[...]).astype(bf16)
            gk_ref[rows, :] = (nn(score_low[...], spread[...]) * scale).astype(bf16)

    for start in range(0, ROWS, CHUNK):
        rows = slice(start, start + CHUNK)
        images = range(start // QP, (start + CHUNK) // QP)
        parts = [flat_ref[image * NQ : image * NQ + QP, :] for image in images]
        target = jnp.concatenate([jnp.where(inside, part, 0.0) for part in parts], axis=0)
        joined_t = (target + positions).astype(bf16).T
        grad_query = gq_ref[rows, :]
        grad_key = gk_ref[rows, :]
        grad_value = gv_ref[rows, :]
        add_row(BIAS + 0, total(grad_query.astype(f32)))
        add_row(BIAS + 1, total(grad_value.astype(f32)))
        dw_ref[0] += nn(joined_t, grad_query)
        dw_ref[1] += nn(joined_t, grad_key)
        dw_ref[2] += tn(target.astype(bf16), grad_value)
        grad_joined = nt(grad_query, w_ref[0]) + nt(grad_key, w_ref[1])
        grad_rows_ref[rows, :] += grad_joined + nt(grad_value, w_ref[2])
        grad_place = grad_joined + place_ref[rows, :]
        for image in range(CHUNK // QP):
            drows_ref[POS : POS + QP, :] += grad_place[image * QP : (image + 1) * QP, :]
    for image in range(IMG_MAX):
        part = grad_rows_ref[image * QP : image * QP + NQ, :]
        dtarget_ref[0, image * NQ : (image + 1) * NQ, :] = part

    @pl.when(pack == pl.num_programs(0) - 1)
    def _():
        small = drows_ref[...].T
        dw_ref[SMALL, :, POS:] = small[:, POS:]
        dw_ref[SMALL, :, :POS] = small[:, :POS] + dhead_ref[...]
        half, height, unused = keep_ref.shape
        parts = 2 * half
        share = D // parts
        used = (SMALL + 1) * share
        if height > used:
            block_ref[:, used:, :] = jnp.zeros((parts, height - used, D), f32)

        @pl.loop(0, parts)
        def _(device):
            place = place_of(device, bounds, ordered, parts)
            rows = pl.ds(pl.multiple_of(device * share, share), share)
            for unit in range(SMALL + 1):
                block_ref[place, unit * share : (unit + 1) * share, :] = dw_ref[unit, rows, :]

        keep_ref[...] = block_ref[0:half]
        send_ref[...] = block_ref[half:].astype(bf16)


def whole(shape):
    zeros = (0,) * len(shape)
    return pl.BlockSpec(shape, lambda *unused: zeros)


def by_pack(shape):
    zeros = (0,) * (len(shape) - 1)
    return pl.BlockSpec((1,) + tuple(shape[1:]), lambda pack, *unused: (pack,) + zeros)


LIMIT = 60 * 1024 * 1024


def params(axes):
    return pltpu.CompilerParams(
        dimension_semantics=("arbitrary",) * axes, vmem_limit_bytes=LIMIT
    )


def early_self(bounds, target, memory, memory_pos, mine, other, ordered):
    packs, slots, unused = target.shape
    tokens = memory.shape[1]
    height = mine.shape[1]
    wide = HEADS * QP
    low_rows = jax.ShapeDtypeStruct((packs, ROWS, D), bf16)
    rows = jax.ShapeDtypeStruct((packs, ROWS, D), f32)
    low_tokens = jax.ShapeDtypeStruct((packs, tokens, D), bf16)
    mean = jax.ShapeDtypeStruct((packs, 1, D), f32)
    outs = [rows] + [low_rows] * 4 + [rows, low_rows, low_tokens, low_tokens, mean]
    units = jax.ShapeDtypeStruct((SMALL + 1, D, D), bf16)
    return pl.pallas_call(
        functools.partial(early_self_kernel, ordered),
        grid_spec=pltpu.PrefetchScalarGridSpec(
            num_scalar_prefetch=1,
            grid=(packs,),
            in_specs=[
                by_pack(target.shape),
                by_pack(memory.shape),
                by_pack(memory_pos.shape),
                whole(mine.shape),
                whole(other.shape),
            ],
            out_specs=[by_pack(out.shape) for out in outs] + [whole(units.shape)],
            scratch_shapes=[
                pltpu.VMEM((D, D), f32),
                pltpu.VMEM((slots + 32, D), f32),
                pltpu.VMEM((ROWS, D), f32),
                pltpu.VMEM((2, wide, D), bf16),
                pltpu.VMEM((2 * mine.shape[0], height, D), bf16),
                pltpu.VMEM((SMALL + 1, D, D), f32),
            ],
        ),
        out_shape=outs + [units],
        compiler_params=params(1),
        cost_estimate=pl.CostEstimate(
            flops=packs * 8_000_000_000, bytes_accessed=packs * 9_000_000, transcendentals=0
        ),
        name="early_self",
    )(bounds, target, memory, memory_pos, mine, other)


def early_cross(bounds, rows, query, key, value, mean, weights, slots):
    packs = rows.shape[0]
    tokens = key.shape[1]
    wide = HEADS * QP
    outs = [
        jax.ShapeDtypeStruct((packs, slots, D), f32),
        jax.ShapeDtypeStruct(query.shape, bf16),
        jax.ShapeDtypeStruct((packs, IMG_MAX, 1, wide), f32),
    ]
    arrays = [rows, query, key, value, mean]
    return pl.pallas_call(
        early_cross_kernel,
        grid_spec=pltpu.PrefetchScalarGridSpec(
            num_scalar_prefetch=1,
            grid=(packs,),
            in_specs=[by_pack(array.shape) for array in arrays]
            + [
                pl.BlockSpec((1, D, D), lambda *unused: (7, 0, 0)),
                pl.BlockSpec((1, D, D), lambda *unused: (SMALL, 0, 0)),
            ],
            out_specs=[by_pack(out.shape) for out in outs],
            scratch_shapes=[
                pltpu.VMEM((ROWS, D), f32),
                pltpu.VMEM((wide, D), bf16),
                pltpu.VMEM((tokens, wide), f32),
                pltpu.VMEM((1, wide), f32),
                pltpu.VMEM((1, wide), f32),
                pltpu.VMEM((QP, D), f32),
                pltpu.VMEM((1, D), f32),
            ],
        ),
        out_shape=outs,
        compiler_params=params(1),
        cost_estimate=pl.CostEstimate(
            flops=packs * 8_000_000_000, bytes_accessed=packs * 7_000_000, transcendentals=0
        ),
        name="early_cross",
    )(bounds, *arrays, weights, weights)


def middle(bounds, x, cotangents, mine, other, small, head_bias, ordered):
    packs, slots, unused = x.shape
    half, height, unused = mine.shape
    outs = [
        jax.ShapeDtypeStruct(x.shape, bf16),
        jax.ShapeDtypeStruct(x.shape, f32),
        jax.ShapeDtypeStruct(mine.shape, f32),
        jax.ShapeDtypeStruct(mine.shape, bf16),
        jax.ShapeDtypeStruct((D, POS), f32),
        jax.ShapeDtypeStruct((32, D), f32),
    ]
    return pl.pallas_call(
        functools.partial(middle_kernel, ordered),
        grid_spec=pltpu.PrefetchScalarGridSpec(
            num_scalar_prefetch=1,
            grid=(packs,),
            in_specs=[
                by_pack(x.shape),
                *[by_pack(array.shape) for array in cotangents],
                whole(mine.shape),
                whole(other.shape),
                pl.BlockSpec((1, D, D), lambda *unused: (SMALL, 0, 0)),
                whole(head_bias.shape),
            ],
            out_specs=[by_pack(x.shape), by_pack(x.shape)] + [whole(out.shape) for out in outs[2:]],
            scratch_shapes=[
                pltpu.VMEM((D, D), f32),
                pltpu.VMEM((2 * FF_BLOCKS, 1, D), f32),
                pltpu.VMEM((2, D, D), bf16),
                pltpu.VMEM((slots, D), bf16),
                pltpu.VMEM((slots, D), f32),
                pltpu.VMEM((slots, D), f32),
                pltpu.VMEM((slots, D), bf16),
                pltpu.VMEM((FF_BLOCKS, slots, D), bf16),
                pltpu.VMEM((FF_BLOCKS, slots, D), f32),
                pltpu.VMEM((2 * half, height, D), bf16),
                pltpu.VMEM((2 * half, height, D), f32),
                pltpu.VMEM((2, D, D), f32),
            ],
        ),
        out_shape=outs,
        compiler_params=params(1),
        cost_estimate=pl.CostEstimate(
            flops=packs * 10_000_000_000, bytes_accessed=packs * 9_000_000, transcendentals=0
        ),
        name="middle",
    )(bounds, x, *cotangents, mine, other, small, head_bias)


def late_cross(bounds, grad, memory, memory_pos, weights, saved):
    packs, slots, unused = grad.shape
    tokens = memory.shape[1]
    wide = HEADS * QP
    outs = [
        jax.ShapeDtypeStruct((packs, ROWS, D), bf16),
        jax.ShapeDtypeStruct(memory.shape, f32),
        jax.ShapeDtypeStruct((3, D, D), f32),
        jax.ShapeDtypeStruct((8, D), f32),
    ]
    return pl.pallas_call(
        late_cross_kernel,
        grid_spec=pltpu.PrefetchScalarGridSpec(
            num_scalar_prefetch=1,
            grid=(packs,),
            in_specs=[
                by_pack(grad.shape),
                by_pack(memory.shape),
                by_pack(memory_pos.shape),
                whole(weights.shape),
            ]
            + [by_pack(array.shape) for array in saved],
            out_specs=[by_pack(outs[0].shape), by_pack(outs[1].shape)]
            + [whole(out.shape) for out in outs[2:]],
            scratch_shapes=[
                pltpu.VMEM((slots + 32, D), f32),
                pltpu.VMEM((ROWS, D), f32),
                pltpu.VMEM((ROWS, D), bf16),
                pltpu.VMEM((tokens, D), f32),
                pltpu.VMEM((wide, D), bf16),
                pltpu.VMEM((wide, D), bf16),
                pltpu.VMEM((SIZES[-1], wide), bf16),
                pltpu.VMEM((SIZES[-1], wide), bf16),
                pltpu.VMEM((1, wide), f32),
                pltpu.VMEM((QP, D), f32),
            ],
        ),
        out_shape=outs,
        compiler_params=params(1),
        cost_estimate=pl.CostEstimate(
            flops=packs * 12_000_000_000, bytes_accessed=packs * 9_000_000, transcendentals=0
        ),
        name="late_cross",
    )(bounds, grad, memory, memory_pos, weights, *saved)


def late_self(bounds, grad, grad_query, target, weights, saved, sums, block, ordered):
    packs, slots, unused = target.shape
    wide = HEADS * QP
    half, height, unused = block
    outs = [
        jax.ShapeDtypeStruct(target.shape, f32),
        jax.ShapeDtypeStruct(block, f32),
        jax.ShapeDtypeStruct(block, bf16),
    ]
    return pl.pallas_call(
        functools.partial(late_self_kernel, ordered),
        grid_spec=pltpu.PrefetchScalarGridSpec(
            num_scalar_prefetch=1,
            grid=(packs,),
            in_specs=[
                by_pack(grad.shape),
                by_pack(grad_query.shape),
                by_pack(target.shape),
                whole(weights.shape),
            ]
            + [by_pack(array.shape) for array in saved]
            + [whole(array.shape) for array in sums],
            out_specs=[by_pack(target.shape), whole(block), whole(block)],
            scratch_shapes=[
                pltpu.VMEM((D, D), f32),
                pltpu.VMEM((slots + 32, D), f32),
                pltpu.VMEM((ROWS, D), f32),
                pltpu.VMEM((ROWS, D), f32),
                pltpu.VMEM((ROWS, D), bf16),
                pltpu.VMEM((ROWS, D), bf16),
                pltpu.VMEM((ROWS, D), bf16),
                pltpu.VMEM((ROWS, D), bf16),
                pltpu.VMEM((2, wide, D), bf16),
                pltpu.VMEM((2, wide, D), bf16),
                pltpu.VMEM((2 * QP, wide), bf16),
                pltpu.VMEM((2 * QP, wide), bf16),
                pltpu.VMEM((D, D), f32),
                pltpu.VMEM(weights.shape, f32),
                pltpu.VMEM((2 * half, height, D), f32),
            ],
        ),
        out_shape=outs,
        compiler_params=params(1),
        cost_estimate=pl.CostEstimate(
            flops=packs * 10_000_000_000, bytes_accessed=packs * 7_000_000, transcendentals=0
        ),
        name="late_self",
    )(bounds, grad, grad_query, target, weights, *saved, *sums)


def stack(parts):
    return jnp.concatenate(parts, axis=0)


def fold(keep, received, count):
    for part in received:
        keep = keep + part.astype(f32)
    size = keep.shape[0] // count
    pieces = [keep[index * size : (index + 1) * size] for index in range(count)]
    return pieces[:1] + [piece.astype(bf16) for piece in pieces[1:]]


def run_of_images(segment, me):
    edge = jnp.arange(16, dtype=jnp.int32)
    below = segment[:, None, :] < edge[None, :, None]
    counts = jnp.sum(below.astype(jnp.int32), axis=-1)
    images = jnp.max(jnp.where(segment < IMG_MAX, segment + 1, 0), axis=-1)
    result = jnp.where(edge[None, :] == IMG_MAX + 1, images[:, None], counts)
    return jnp.where(edge[None, :] == ME, me, result)


def taller(rows):
    return jnp.pad(rows, ((0, -rows.shape[0] % 16), (0, 0)))


def pack_early(project, output, classes, box_final, query_pos, gains, biases):
    share = project.shape[1]
    columns = [
        classes,
        box_final,
        gains.T,
        biases.T,
        jnp.zeros((share, POS - BIAS - 13), bf16),
        query_pos.T,
        jnp.zeros((share, D - POS - NQ), bf16),
    ]
    small = jnp.concatenate(columns, axis=1)
    return taller(jnp.concatenate([project.reshape(-1, D), output.reshape(-1, D), small], axis=0))


def pack_middle(box, shrink, expand, expand_bias):
    extra = jnp.pad(expand_bias[None], ((1, EXTRA - 2), (0, D - expand_bias.shape[0])))
    return taller(jnp.concatenate([shrink, expand.T, box[0], box[1], extra], axis=0))


def pack_kernel(
    project,
    output,
    classes,
    final_t,
    gains,
    shifts_t,
    places_t,
    shrink,
    expand_t,
    box,
    row,
    out,
):
    share = project.shape[1]
    small = nn(classes[...], lanes_of(CLS, 0, D)) + tn(final_t[...], lanes_of(4, CLS, D))
    small += tn(gains[...], lanes_of(4, GAIN, D)) + nn(shifts_t[...], lanes_of(13, BIAS, D))
    small += nn(places_t[...], lanes_of(NQ, POS, D))
    first = [project[...].astype(f32).reshape(-1, D), output[...].astype(f32).reshape(-1, D), small]
    first = jnp.concatenate(first, axis=0)
    rest = -first.shape[0] % 16
    count = row.shape[1]
    vector = nn(row[...], lanes_of(count, 0, D))
    index = lax.broadcasted_iota(jnp.int32, (EXTRA, 1), 0)
    extra = jnp.where(index == 1, vector, 0.0)
    blocks = [first, jnp.zeros((rest, D), f32), shrink[...].astype(f32), expand_t[...].astype(f32)]
    blocks += [box[...].astype(f32).reshape(2 * share, D), extra]
    out[...] = jnp.concatenate(blocks, axis=0).astype(bf16)


def pack_both(project, output, classes, final, places, gains, shifts, box, shrink, expand, row):
    share = project.shape[1]
    early_rows = (SMALL + 1) * share
    early_rows += -early_rows % 16
    if share % 8:
        first = pack_early(project, output, classes, final, places, gains, shifts)
        return jnp.concatenate([first, pack_middle(box, shrink, expand, row)]), early_rows
    rows = early_rows + 2 * shrink.shape[0] + 2 * share + EXTRA
    block = pl.pallas_call(
        pack_kernel,
        out_shape=jax.ShapeDtypeStruct((rows, D), bf16),
        name="pack",
    )(
        project,
        output,
        classes,
        final.T,
        gains,
        shifts.T,
        places.T,
        shrink,
        expand.T,
        box,
        row[None],
    )
    return block, early_rows


def block_rows(devices):
    return [FF_BLOCKS * D // devices] * 2 + [D // devices] * 2


def cut(blocks, devices):
    marks = [0]
    for rows in block_rows(devices):
        marks.append(marks[-1] + rows)
    return [blocks[:, low:high] for low, high in zip(marks, marks[1:])], blocks[:, marks[-1] :]


def regroup(blocks, devices, parts):
    pieces, extra = cut(blocks, devices)
    pieces = [piece.reshape(parts, -1, D) for piece in pieces]
    head = jnp.broadcast_to(extra[0:1, 0:1], (parts, 1, D))
    row = extra[:, 1, : FF_BLOCKS * D // devices].reshape(parts, 1, -1)
    row = jnp.pad(row, ((0, 0), (0, EXTRA - 2), (0, D - row.shape[2])))
    result = jnp.concatenate(pieces + [head, row], axis=1)
    return jnp.pad(result, ((0, 0), (0, -result.shape[1] % 16), (0, 0)))


def regroup_units(blocks, devices, parts):
    units = SMALL + 1
    share = D // devices
    result = blocks[:, : units * share].reshape(devices, units, share, D).swapaxes(0, 1)
    result = result.reshape(units, parts, D // parts, D).swapaxes(0, 1).reshape(parts, -1, D)
    return jnp.pad(result, ((0, 0), (0, -result.shape[1] % 16), (0, 0)))


def parts_of(devices):
    return devices if FF_BLOCKS * D // devices % 16 == 0 else FF_BLOCKS


def bit_groups(devices):
    bits = [1 << k for k in range(1, devices.bit_length() - 1)]
    groups = [(1,)]
    while bits:
        groups.append((bits[0], bits[-1]) if len(bits) > 1 else (bits[0],))
        bits = bits[1:-1]
    return groups


def order_of(distance, devices):
    place = 0
    for bits in bit_groups(devices):
        for bit in bits[::-1]:
            place = 2 * place + distance // bit % 2
    return place


def mixes(bits):
    result = [0]
    for bit in bits:
        result += [mix | bit for mix in result]
    return result


def swap(value, bits, devices):
    return lax.ppermute(value, AXES, [(k, k ^ bits) for k in range(devices)])


def trade(held, bits, devices):
    return [swap(held, mix, devices) if mix else held for mix in mixes(bits)]


def deliver(sends, bits, devices):
    return [swap(send, mix, devices) for mix, send in zip(mixes(bits)[1:], sends)]


def counted(blocks, devices, me):
    places = [order_of(device, devices) for device in range(devices)]
    order = jnp.array(places)[jnp.arange(devices) ^ me]
    return jnp.take(blocks, order, axis=0)


def stepped(blocks, devices, me):
    distances = [0] * devices
    for device in range(devices):
        distances[order_of(device, devices)] = device
    return jnp.take(blocks, jnp.array(distances) ^ me, axis=0)


def unpack_middle(block, devices):
    pieces, extra = cut(block[None], devices)
    shrink, expand, box_one, box_two = [piece[0] for piece in pieces]
    row = extra[0, 1, 0 : shrink.shape[0]]
    return shrink, expand.T, jnp.stack([box_one, box_two]), row, extra[0, 0, 0 : CLS + 4]


def finish_kernel(count, keep, *refs):
    total_block = keep[0]
    for ref in refs[:count]:
        total_block += ref[0].astype(f32)
    project, output, classes, final_t, places_t, gains, shifts_t = refs[count:]
    share = project.shape[1]
    project[...] = total_block[: 6 * share].reshape(6, share, D)
    output[...] = total_block[6 * share : 8 * share].reshape(2, share, D)
    small = total_block[8 * share : 9 * share]
    classes[...] = small[:, 0:CLS]
    places_t[...] = small[:, POS : POS + NQ]
    shifts_t[...] = small[:, BIAS : BIAS + 13]
    turned = small[:, 0:POS].T
    final_t[...] = turned[CLS : CLS + 4]
    gains[...] = turned[GAIN : GAIN + 4]


def finish_early(keep, received, devices):
    share = D // devices
    if share % 8:
        return unpack_early(fold(keep, received, 1)[0][0], devices)
    shapes = [(6, share, D), (2, share, D), (share, CLS), (4, share), (share, NQ), (4, share)]
    shapes.append((share, 13))
    project, output, classes, final_t, places_t, gains, shifts_t = pl.pallas_call(
        functools.partial(finish_kernel, len(received)),
        out_shape=[jax.ShapeDtypeStruct(shape, f32) for shape in shapes],
        name="finish",
    )(keep, *received)
    return project, output, classes, final_t.T, places_t.T, gains, shifts_t.T


def unpack_early(block, devices):
    units = SMALL + 1
    share = D // devices
    block = block[: units * share].reshape(units, share, D)
    small = block[SMALL]
    return (
        block[0:6],
        block[6:8],
        small[:, 0:CLS],
        small[:, CLS : CLS + 4],
        small[:, POS : POS + NQ].T,
        small[:, GAIN : GAIN + 4].T,
        small[:, BIAS : BIAS + 13].T,
    )


def per_device(
    target,
    memory,
    memory_pos,
    segment,
    project_weight,
    output_weight,
    expand_weight,
    shrink_weight,
    box_weight,
    class_weight,
    box_final,
    query_pos,
    norm_gains,
    biases,
    expand_bias,
    head_bias,
    output_cotangent,
    logit_cotangent,
    box_cotangent,
):
    devices = lax.axis_size(AXES)
    me = lax.axis_index(AXES)
    groups = bit_groups(devices)
    parts = parts_of(devices)
    ordered = parts == devices
    slots = target.shape[1]

    both, height = pack_both(
        project_weight,
        output_weight,
        class_weight,
        box_final,
        query_pos,
        norm_gains,
        biases,
        box_weight,
        shrink_weight,
        expand_weight,
        expand_bias,
    )
    both = both[None]
    both_parts = trade(both, groups[-1], devices)
    both_parts, logit_cotangent, box_cotangent = lax.optimization_barrier(
        (both_parts, logit_cotangent, box_cotangent)
    )
    early_held = stack([part[:, :height] for part in both_parts])
    middle_held = stack([part[:, height:] for part in both_parts])
    for bits in groups[-2:1:-1]:
        early_held = stack(trade(early_held, bits, devices))
    early_parts = trade(early_held, groups[1], devices)
    bounds = run_of_images(segment, me)
    head_row = jnp.pad(head_bias.astype(f32), (0, POS - CLS - 4))
    head_row = jnp.broadcast_to(head_row[None], (8, POS))
    rest = jnp.zeros(logit_cotangent.shape[:2] + (POS - CLS - 4,), bf16)
    head_cotangent = jnp.concatenate([logit_cotangent, box_cotangent, rest], axis=-1)
    early_parts, bounds, head_row, head_cotangent, middle_held = lax.optimization_barrier(
        (early_parts, bounds, head_row, head_cotangent, middle_held)
    )
    early_mine = stack(early_parts)
    early_other = swap(early_mine, 1, devices)
    if not ordered:
        blocks = counted(jnp.concatenate([early_mine, early_other]), devices, me)
        blocks = regroup_units(blocks, devices, parts)
        early_mine, early_other = blocks[: parts // 2], blocks[parts // 2 :]
    middle_parts = trade(middle_held, groups[-2], devices)
    rows, *saved = early_self(
        bounds, target, memory, memory_pos, early_mine, early_other, ordered
    )
    query, key, value, mean, weights = saved[5:]
    middle_parts, query = lax.optimization_barrier((middle_parts, query))
    for bits in groups[-3:0:-1]:
        middle_parts = trade(stack(middle_parts), bits, devices)
    middle_mine = stack(middle_parts)
    middle_mine, query = lax.optimization_barrier((middle_mine, query))
    middle_other = swap(middle_mine, 1, devices)
    after, context, logs = early_cross(bounds, rows, query, key, value, mean, weights, slots)
    if not ordered:
        blocks = counted(jnp.concatenate([middle_mine, middle_other]), devices, me)
        blocks = regroup(blocks, devices, parts)
        middle_mine, middle_other = blocks[: parts // 2], blocks[parts // 2 :]
    layer, grad, keep, send, dhead, drow = middle(
        bounds,
        after,
        [output_cotangent, head_cotangent],
        middle_mine,
        middle_other,
        weights,
        head_row,
        ordered,
    )

    def real_blocks(keep, send, change):
        if ordered:
            return keep, send
        blocks = jnp.concatenate([keep, send.astype(f32)])
        blocks = stepped(change(blocks, parts, devices), devices, me)
        return blocks[: devices // 2], blocks[devices // 2 :].astype(bf16)

    def counts(index):
        return 1 << len(groups[index]) if index < len(groups) else 1

    keep, send = real_blocks(keep, send, regroup)
    grad, keep, send = lax.optimization_barrier((grad, keep, send))
    received = deliver([send], groups[0], devices)
    grad_query, dmemory, dcross, dcross_rows = late_cross(
        bounds, grad, memory, memory_pos, weights, [query, key, value, context, logs]
    )
    grad_query, received = lax.optimization_barrier((grad_query, received))
    keep, *sends = fold(keep, received, counts(1))
    grad_query, keep, sends = lax.optimization_barrier((grad_query, keep, sends))
    received = deliver(sends, groups[1], devices)
    sums = [dcross, dcross_rows, dhead, drow]
    block = early_mine.shape
    dtarget, early_keep, early_send = late_self(
        bounds, grad, grad_query, target, weights, saved[:5], sums, block, ordered
    )
    early_keep, early_send, received = lax.optimization_barrier(
        (early_keep, early_send, received)
    )
    early_keep, early_send = real_blocks(early_keep, early_send, regroup_units)
    early_received = deliver([early_send], groups[0], devices)
    for index in range(2, len(groups)):
        keep, *sends = fold(keep, received, counts(index))
        received = deliver(sends, groups[index], devices)
    early_keep, *early_sends = fold(early_keep, early_received, counts(1))
    early_received = deliver(early_sends, groups[1], devices)
    early_received, received = lax.optimization_barrier((early_received, received))
    for index in range(2, len(groups)):
        early_keep, *early_sends = fold(early_keep, early_received, counts(index))
        early_received = deliver(early_sends, groups[index], devices)
    middle_sum = fold(keep, received, 1)[0]
    middle_grads = unpack_middle(middle_sum[0], devices)
    early_received, middle_grads = lax.optimization_barrier((early_received, middle_grads))
    shrink, expand, box, expand_row, head = middle_grads
    project, output, classes, final, places, gains, shifts = finish_early(
        early_keep, early_received, devices
    )
    return (
        layer,
        dtarget,
        dmemory,
        project,
        output,
        expand,
        shrink,
        box,
        classes,
        final,
        places,
        gains,
        shifts,
        expand_row,
        head,
    )


def solution(mesh):
    both = ("dp", "fsdp")
    by_rows = P(both, None, None)
    return jax.shard_map(
        per_device,
        mesh=mesh,
        in_specs=(
            by_rows,
            by_rows,
            by_rows,
            P(both, None),
            P(None, both, None),
            P(None, both, None),
            P(None, both),
            P(both, None),
            P(None, both, None),
            P(both, None),
            P(both, None),
            P(None, both),
            P(None, both),
            P(None, both),
            P(both),
            P(),
            by_rows,
            by_rows,
            by_rows,
        ),
        out_specs=(
            by_rows,
            by_rows,
            by_rows,
            P(None, both, None),
            P(None, both, None),
            P(None, both),
            P(both, None),
            P(None, both, None),
            P(both, None),
            P(both, None),
            P(None, both),
            P(None, both),
            P(None, both),
            P(both),
            P(),
        ),
        check_vma=False,
    )
```

```python
import functools

import jax
import jax.numpy as jnp
from jax import lax
from jax.experimental import pallas as pl
from jax.experimental.pallas import tpu as pltpu
from jax.sharding import PartitionSpec as P

D = 256
HEADS = 8
NQ = 100
CLS = 92
IMG_MAX = 12
HEAD_DIM = 32
QP = 128
ROWS = IMG_MAX * QP
TURNS = 3
PAIRS = HEADS // 2
BLOCK = 256
SIZES = (128, 192, 256, 384, 512)
SHORT = (128, 192, 256, 512)
CHUNK = 512
STEP = 400
FF_BLOCKS = 8
GAIN = 96
BIAS = 100
POS = 128
SMALL = 8
EXTRA = 16
ME = 14

epsilon = 1e-05
masked = -1000000000.0
scale = HEAD_DIM ** (-0.5)
log2e = 1.4426950408889634
gelu_a = 0.7978845608028654
gelu_b = gelu_a * 0.044715
AXES = ("dp", "fsdp")
f32 = jnp.float32
bf16 = jnp.bfloat16


def nn(left, right):
    return jnp.dot(left, right, preferred_element_type=f32)


def nt(left, right):
    return lax.dot_general(left, right, (((1,), (1,)), ((), ())), preferred_element_type=f32)


def tn(left, right):
    return lax.dot_general(left, right, (((0,), (0,)), ((), ())), preferred_element_type=f32)


def total(value):
    return jnp.sum(value, axis=0, keepdims=True)


def norm_parts(value):
    middle = jnp.mean(value, axis=-1, keepdims=True)
    centered = value - middle
    spread = jnp.mean(centered * centered, axis=-1, keepdims=True)
    inverse = lax.rsqrt(spread + epsilon)
    return centered * inverse, inverse


def norm_back(unit, inverse, gain, grad):
    scaled = grad * gain
    first = jnp.mean(scaled, axis=-1, keepdims=True)
    second = jnp.mean(scaled * unit, axis=-1, keepdims=True)
    return inverse * (scaled - first - unit * second)


def gelu_parts(value):
    square = value * value
    cdf = 0.5 + 0.5 * jnp.tanh(value * (gelu_a + gelu_b * square))
    result = value * cdf
    slope = cdf + (result - result * cdf) * (2.0 * gelu_a + 6.0 * gelu_b * square)
    return result, slope


def spread_heads(value, spread_ref):
    lane = lax.broadcasted_iota(jnp.int32, (1, D), 1) // HEAD_DIM
    for head in range(HEADS):
        keep = (lane == head).astype(f32).astype(bf16)
        spread_ref[head * QP : (head + 1) * QP, :] = value * keep


def pair_rows(ref, pair):
    side = pair // 2 * (D // 2)
    return ref[2 * QP * pair : 2 * QP * (pair + 1), side : side + D // 2]


def long_rows(ref, pair):
    return ref[2 * QP * pair : 2 * QP * (pair + 1), :]


def head_lane(lanes):
    return lax.broadcasted_iota(jnp.int32, (1, lanes), 1) // HEAD_DIM


def join_pairs(products):
    lane = head_lane(D)
    result = products[0][:QP]
    for head in range(1, HEADS):
        part = products[head // 2][(head % 2) * QP : (head % 2 + 1) * QP]
        result = jnp.where(lane == head, part, result)
    return result


def join_halves(products):
    lane = head_lane(D // 2)
    halves = []
    for half in range(2):
        low, high = products[2 * half : 2 * half + 2]
        part = jnp.where(lane == 2, high[:QP], high[QP:])
        part = jnp.where(lane == 1, low[QP:], part)
        halves.append(jnp.where(lane == 0, low[:QP], part))
    return jnp.concatenate(halves, axis=1)


def half_lanes(value, pair):
    side = pair // 2 * (D // 2)
    return value[:, side : side + D // 2]


def row_loop(size, step):
    def run(body):
        @pl.loop(0, size // step)
        def _(index):
            start = pl.multiple_of(index * step, step)
            body(start, pl.ds(start, step))

    return run


def chunk_loop(size, step):
    def run(body):
        for start in range(0, size, step):
            body(start, slice(start, start + step))

    return run


def attend_block(key, value, spread_ref, valid, halves):
    scores = [nt(half_lanes(key, pair), pair_rows(spread_ref, pair)) for pair in range(PAIRS)]
    attends = []
    logs = []
    for pair in range(PAIRS):
        kept = jnp.where(valid, scores[pair], masked)
        top = jnp.max(kept, axis=0, keepdims=True)
        raised = jnp.exp2((kept - top) * (scale * log2e))
        sums = total(raised)
        attends.append((raised * (1.0 / sums)).astype(bf16))
        logs.append(top * (scale * log2e) + jnp.log2(sums))
    if halves:
        products = [tn(attends[pair], half_lanes(value, pair)) for pair in range(PAIRS)]
        context = join_halves(products)
    else:
        context = join_pairs([tn(attends[pair], value) for pair in range(PAIRS)])
    return context, jnp.concatenate(logs, axis=1)


def place_of(device, bounds, ordered, parts):
    return order_of(device ^ bounds[0, ME], parts) if ordered else device


def early_self_kernel(
    ordered,
    bounds,
    target_ref,
    memory_ref,
    pos_ref,
    mine_ref,
    other_ref,
    after_ref,
    qs_ref,
    ks_ref,
    vs_ref,
    cs_ref,
    inner_ref,
    cq_ref,
    ck_ref,
    cv_ref,
    mean_ref,
    log_ref,
    w_ref,
    small_ref,
    flat_ref,
    rows_ref,
    spread_ref,
    block_ref,
    unit_ref,
):
    pack = pl.program_id(0)
    slots = target_ref.shape[1]
    tokens = memory_ref.shape[1]
    near = mine_ref.shape[0]
    parts = 2 * near
    share = D // parts

    @pl.when(pack == 0)
    def _():
        block_ref[0:near] = mine_ref[...]
        block_ref[near:] = other_ref[...]

        @pl.loop(0, parts)
        def _(device):
            block = block_ref[place_of(device, bounds, ordered, parts)].astype(f32)
            rows = pl.ds(pl.multiple_of(device * share, share), share)
            for unit in range(SMALL + 1):
                unit_ref[unit, rows, :] = block[unit * share : (unit + 1) * share]

        w_ref[...] = unit_ref[...].astype(bf16)
        small_ref[...] = unit_ref[SMALL].T

    def bias(index):
        return small_ref[BIAS + index : BIAS + index + 1, :]

    def gain(index):
        return small_ref[GAIN + index : GAIN + index + 1, :]

    inside = lax.broadcasted_iota(jnp.int32, (QP, 1), 0) < NQ
    position = small_ref[POS : POS + QP, :]
    positions = jnp.concatenate([position] * (CHUNK // QP), axis=0)

    mean_ref[0] = jnp.zeros((1, D), f32)
    @chunk_loop(tokens, CHUNK)
    def _(start, rows):
        memory = memory_ref[0, rows, :]
        joined = (memory.astype(f32) + pos_ref[0, rows, :].astype(f32)).astype(bf16)
        ck_ref[0, rows, :] = nn(joined, w_ref[4]).astype(bf16)
        value = (nn(memory, w_ref[5]) + bias(4)).astype(bf16)
        cv_ref[0, rows, :] = value
        mean_ref[0] += total(value.astype(f32)) * (1.0 / tokens)

    flat_ref[0:slots, :] = target_ref[0].astype(f32)
    for image in range(IMG_MAX):
        part = flat_ref[image * NQ : image * NQ + QP, :]
        rows_ref[image * QP : (image + 1) * QP, :] = jnp.where(inside, part, 0.0)

    @chunk_loop(ROWS, CHUNK)
    def _(start, rows):
        target = rows_ref[rows, :]
        joined = (target + positions).astype(bf16)
        qs_ref[0, rows, :] = (nn(joined, w_ref[0]) + bias(0)).astype(bf16)
        ks_ref[0, rows, :] = nn(joined, w_ref[1]).astype(bf16)
        vs_ref[0, rows, :] = (nn(target.astype(bf16), w_ref[2]) + bias(1)).astype(bf16)

    @pl.loop(0, IMG_MAX // TURNS)
    def _(step):
        for turn in range(TURNS):
            rows = pl.ds(pl.multiple_of((TURNS * step + turn) * QP, QP), QP)
            spread = spread_ref.at[turn]
            spread_heads(qs_ref[0, rows, :], spread)
            context, logs = attend_block(
                ks_ref[0, rows, :], vs_ref[0, rows, :], spread, inside, True
            )
            cs_ref[0, rows, :] = context.astype(bf16)
            log_ref[0, TURNS * step + turn] = logs

    @chunk_loop(ROWS, CHUNK)
    def _(start, rows):
        value = rows_ref[rows, :] + nn(cs_ref[0, rows, :], w_ref[6]) + bias(2)
        inner_ref[0, rows, :] = value
        unit, unused = norm_parts(value)
        after = unit * gain(0) + bias(9)
        after_ref[0, rows, :] = after
        query = nn((after + positions).astype(bf16), w_ref[3]) + bias(3)
        cq_ref[0, rows, :] = query.astype(bf16)


def early_cross_kernel(
    bounds,
    rows_in_ref,
    cq_ref,
    ck_ref,
    cv_ref,
    mean_ref,
    w_ref,
    small_in_ref,
    after_ref,
    cc_ref,
    log_ref,
    rows_ref,
    spread_ref,
    score_ref,
    top_ref,
    sum_ref,
    out_ref,
    bias_ref,
):
    pack = pl.program_id(0)
    tokens = ck_ref.shape[1]

    @pl.when(pack == 0)
    def _():
        bias_ref[...] = small_in_ref[0].astype(f32).T[BIAS + 5 : BIAS + 6]

    @pl.loop(0, IMG_MAX)
    def _(image):
        rows = pl.ds(pl.multiple_of(image * QP, QP), QP)
        first = bounds[pack, image]
        last = bounds[pack, image + 1]
        origin = (first // 16) * 16
        blocks = (last - origin + (BLOCK - 1)) // BLOCK
        spread = spread_ref
        spread_heads(cq_ref[0, rows, :], spread)

        def place_at(block, size=BLOCK):
            wanted = origin + block * size
            start = pl.multiple_of(jnp.minimum(wanted, tokens - size), 16)
            token = start + lax.broadcasted_iota(jnp.int32, (size, 1), 0)
            valid = (token >= jnp.maximum(first, wanted)) & (token < last)
            return pl.ds(start, size), valid

        def fits(index):
            below = SHORT[index - 1] if index else 0
            return (last > first) & (last - origin > below) & (last - origin <= SHORT[index])

        @pl.when(last == first)
        def _():
            cc_ref[0, rows, :] = jnp.broadcast_to(mean_ref[0], (QP, D)).astype(bf16)
            log_ref[0, image] = jnp.zeros((1, HEADS * QP), f32)

        def in_one(size):
            place, valid = place_at(0, size)
            context, logs = attend_block(
                ck_ref[0, place, :], cv_ref[0, place, :], spread, valid, False
            )
            cc_ref[0, rows, :] = context.astype(bf16)
            log_ref[0, image] = logs

        for index, size in enumerate(SHORT):
            pl.when(fits(index))(functools.partial(in_one, size))

        @pl.when(last - origin > SHORT[-1])
        def _():
            top_ref[...] = jnp.full_like(top_ref, masked)
            sum_ref[...] = jnp.zeros_like(sum_ref)
            out_ref[...] = jnp.zeros_like(out_ref)

            @pl.loop(0, blocks)
            def _(block):
                place, valid = place_at(block)
                kept = pl.ds(pl.multiple_of(block * BLOCK, BLOCK), BLOCK)
                key = ck_ref[0, place, :]
                for pair in range(PAIRS):
                    lanes = slice(2 * QP * pair, 2 * QP * (pair + 1))
                    scores = jnp.where(valid, nt(key, long_rows(spread, pair)), masked)
                    score_ref[kept, lanes] = scores
                    top = jnp.max(scores, axis=0, keepdims=True)
                    top_ref[:, lanes] = jnp.maximum(top_ref[:, lanes], top)

            @pl.loop(0, blocks)
            def _(block):
                kept = pl.ds(pl.multiple_of(block * BLOCK, BLOCK), BLOCK)
                raised = jnp.exp2((score_ref[kept, :] - top_ref[...]) * (scale * log2e))
                score_ref[kept, :] = raised
                sum_ref[...] += total(raised)

            @pl.loop(0, blocks)
            def _(block):
                place, unused = place_at(block)
                kept = pl.ds(pl.multiple_of(block * BLOCK, BLOCK), BLOCK)
                value = cv_ref[0, place, :]
                products = []
                for pair in range(PAIRS):
                    lanes = slice(2 * QP * pair, 2 * QP * (pair + 1))
                    attend = (score_ref[kept, lanes] * (1.0 / sum_ref[:, lanes])).astype(bf16)
                    products.append(tn(attend, value))
                out_ref[...] += join_pairs(products)

            cc_ref[0, rows, :] = out_ref[...].astype(bf16)
            log_ref[0, image] = top_ref[...] * (scale * log2e) + jnp.log2(sum_ref[...])

    @chunk_loop(ROWS, CHUNK)
    def _(start, rows):
        rows_ref[rows, :] = rows_in_ref[0, rows, :] + nn(cc_ref[0, rows, :], w_ref[0]) + bias_ref[...]
    for image in range(IMG_MAX):
        after_ref[0, image * NQ : (image + 1) * NQ, :] = rows_ref[image * QP : image * QP + NQ, :]


def lanes_of(count, first, lanes=POS):
    row = lax.broadcasted_iota(jnp.int32, (count, lanes), 0)
    lane = lax.broadcasted_iota(jnp.int32, (count, lanes), 1)
    return (row + first == lane).astype(f32).astype(bf16)


def middle_kernel(
    ordered,
    bounds,
    x_ref,
    cot_ref,
    head_cot_ref,
    mine_ref,
    other_ref,
    small_in_ref,
    head_bias_ref,
    layer_ref,
    grad_ref,
    keep_ref,
    send_ref,
    dhead_ref,
    drow_ref,
    small_ref,
    bias_ref,
    box_ref,
    low_ref,
    cross_ref,
    sum_ref,
    branch_ref,
    hidden_ref,
    slope_ref,
    ff_ref,
    dff_ref,
    unit_ref,
):
    pack = pl.program_id(0)
    slots = x_ref.shape[1]
    half = mine_ref.shape[0]
    parts = 2 * half
    ff = FF_BLOCKS * D // parts
    share = D // parts
    near = D // ff
    boxes = 2 * ff
    extra = 2 * ff + 2 * share

    @pl.when(pack == 0)
    def _():
        small_ref[...] = small_in_ref[0].astype(f32).T
        ff_ref[0:half] = mine_ref[...]
        ff_ref[half:] = other_ref[...]

        @pl.loop(0, parts)
        def _(device):
            place = place_of(device, bounds, ordered, parts)
            pair = ff_ref[place, boxes:extra, :].astype(f32)
            rows = pl.ds(pl.multiple_of(device * share, share), share)
            unit_ref[0, rows, :] = pair[:share]
            unit_ref[1, rows, :] = pair[share:]

        box_ref[...] = unit_ref[...].astype(bf16)
        unit_ref[...] = jnp.zeros_like(unit_ref)
        for block in range(FF_BLOCKS):
            rows = [ff_ref[block * near + k, extra : extra + 16, :] for k in range(near)]
            rows = [row.astype(f32)[1:2, 0:ff] for row in rows]
            bias_ref[block] = jnp.concatenate(rows, axis=1)
        bias_ref[FF_BLOCKS:] = jnp.zeros((FF_BLOCKS, 1, D), f32)
        dff_ref[...] = jnp.zeros_like(dff_ref)
        dhead_ref[...] = jnp.zeros_like(dhead_ref)
        drow_ref[...] = jnp.zeros_like(drow_ref)

    def bias(index):
        return small_ref[BIAS + index : BIAS + index + 1, :]

    def gain(index):
        return small_ref[GAIN + index : GAIN + index + 1, :]

    def add_row(column, value):
        row = column - GAIN
        drow_ref[row : row + 1, :] += value

    def near_block(block):
        return pl.ds(block * near, near)

    def shrink(block):
        return ff_ref[near_block(block), 0:ff, :].reshape(D, D)

    def expand(block):
        return ff_ref[near_block(block), ff:boxes, :].reshape(D, D)

    @row_loop(slots, STEP)
    def _(start, rows):
        unit, unused = norm_parts(x_ref[0, rows, :])
        after_cross = unit * gain(1) + bias(10)
        cross_ref[rows, :] = after_cross
        low_ref[rows, :] = after_cross.astype(bf16)

    sum_ref[...] = cross_ref[...] + bias(6)
    hidden_ref[FF_BLOCKS - 1] = jnp.zeros((slots, D), bf16)

    @pl.loop(0, FF_BLOCKS)
    def _(block):
        before = (block + FF_BLOCKS - 1) % FF_BLOCKS
        sum_ref[...] += nn(hidden_ref[before], shrink(before))
        value, slope = gelu_parts(nt(low_ref[...], expand(block)) + bias_ref[block])
        hidden_ref[block] = value.astype(bf16)
        slope_ref[block] = slope

    sum_ref[...] += nn(hidden_ref[FF_BLOCKS - 1], shrink(FF_BLOCKS - 1))

    head_weight = small_in_ref[0, :, 0:POS]
    lane = lax.broadcasted_iota(jnp.int32, (1, POS), 1)
    is_box = (lane >= CLS) & (lane < CLS + 4)
    @chunk_loop(slots, STEP)
    def _(start, rows):
        slot = start + lax.broadcasted_iota(jnp.int32, (STEP, 1), 0)
        live = (slot < bounds[pack, IMG_MAX + 1] * NQ).astype(f32)
        unit_ffn, inverse_ffn = norm_parts(sum_ref[rows, :])
        after_ffn = unit_ffn * gain(2) + bias(11)
        layer_ref[0, rows, :] = (after_ffn * live).astype(bf16)
        unit_last, inverse_last = norm_parts(after_ffn)
        normed = (unit_last * gain(3) + bias(12)).astype(bf16)
        one, one_slope = gelu_parts(nn(normed, box_ref[0]) + bias(7))
        box_one = one.astype(bf16)
        two, two_slope = gelu_parts(nn(box_one, box_ref[1]) + bias(8))
        box_two = two.astype(bf16)
        box = jax.nn.sigmoid(nn(box_two, head_weight) + head_bias_ref[0:1, :])

        head_cot = head_cot_ref[0, rows, :].astype(f32) * live
        grad_box = jnp.where(is_box, head_cot * box * (1.0 - box), 0.0).astype(bf16)
        grad_logit = jnp.where(lane < CLS, head_cot, 0.0).astype(bf16)
        drow_ref[31:32, 0:POS] += total(grad_box.astype(f32)) + total(grad_logit.astype(f32))
        normed_t = normed.T
        grad_two = (two_slope * nt(grad_box, head_weight)).astype(bf16)
        grad_one = (one_slope * nt(grad_two, box_ref[1])).astype(bf16)
        dhead_ref[...] += nn(normed_t, grad_logit) + tn(box_two, grad_box)
        unit_ref[0] += nn(normed_t, grad_one)
        unit_ref[1] += tn(box_one, grad_two)
        add_row(BIAS + 8, total(grad_two.astype(f32)))
        add_row(BIAS + 7, total(grad_one.astype(f32)))
        grad_normed = nt(grad_one, box_ref[0]) + nt(grad_logit, head_weight)
        add_row(GAIN + 3, total(grad_normed * unit_last))
        add_row(BIAS + 12, total(grad_normed))
        grad_after = cot_ref[0, rows, :].astype(f32) * live + norm_back(
            unit_last, inverse_last, gain(3), grad_normed
        )
        add_row(GAIN + 2, total(grad_after * unit_ffn))
        add_row(BIAS + 11, total(grad_after))
        grad_ffn = norm_back(unit_ffn, inverse_ffn, gain(2), grad_after)
        grad_branch = grad_ffn.astype(bf16)
        add_row(BIAS + 6, total(grad_branch.astype(f32)))
        sum_ref[rows, :] = grad_ffn
        branch_ref[rows, :] = grad_branch

    @pl.loop(0, FF_BLOCKS)
    def _(block):
        branch = branch_ref[...]
        dpre = (nt(branch, shrink(block)) * slope_ref[block]).astype(bf16)
        bias_ref[FF_BLOCKS + block] += total(dpre.astype(f32))
        dshrink = tn(hidden_ref[block], branch).reshape(near, ff, D)
        dff_ref[near_block(block), 0:ff, :] += dshrink
        dexpand = tn(dpre, low_ref[...]).reshape(near, ff, D)
        dff_ref[near_block(block), ff:boxes, :] += dexpand
        sum_ref[...] += nn(dpre, expand(block))

    @row_loop(slots, STEP)
    def _(start, rows):
        unit, inverse = norm_parts(x_ref[0, rows, :])
        grad = sum_ref[rows, :]
        add_row(GAIN + 1, total(grad * unit))
        add_row(BIAS + 10, total(grad))
        grad_ref[0, rows, :] = norm_back(unit, inverse, gain(1), grad)

    @pl.when(pack == pl.num_programs(0) - 1)
    def _():
        @pl.loop(0, parts)
        def _(device):
            place = place_of(device, bounds, ordered, parts)
            rows = pl.ds(pl.multiple_of(device * share, share), share)
            dff_ref[place, boxes : boxes + share, :] = unit_ref[0, rows, :]
            dff_ref[place, boxes + share : extra, :] = unit_ref[1, rows, :]

        for part in range(parts):
            dff_ref[part, extra : extra + 1, :] = drow_ref[31:32, :]
            side = part % near * ff
            values = bias_ref[FF_BLOCKS + part // near][:, side : side + ff]
            dff_ref[part, extra + 1 : extra + 2, 0:ff] = values
        keep_ref[...] = dff_ref[0:half]
        send_ref[...] = dff_ref[half:].astype(bf16)


def attend_back(key, value, spread, spread_grad, valid, logs, attend_ref, score_ref):
    scores = [nt(half_lanes(key, pair), pair_rows(spread, pair)) for pair in range(PAIRS)]
    grads = [nt(half_lanes(value, pair), pair_rows(spread_grad, pair)) for pair in range(PAIRS)]
    lows = []
    for pair in range(PAIRS):
        lanes = slice(2 * QP * pair, 2 * QP * (pair + 1))
        attend = jnp.exp2(scores[pair] * (scale * log2e) - logs[:, lanes])
        attend = jnp.where(valid, attend, 0.0)
        row_dot = total(attend * grads[pair])
        low = (attend * (grads[pair] - row_dot)).astype(bf16)
        attend_ref[:, lanes] = attend.astype(bf16)
        score_ref[:, lanes] = low
        lows.append(low)
    return join_halves([tn(lows[pair], half_lanes(key, pair)) for pair in range(PAIRS)]) * scale


def late_cross_kernel(
    bounds,
    grad_ref,
    memory_ref,
    pos_ref,
    w_ref,
    cq_ref,
    ck_ref,
    cv_ref,
    cc_ref,
    log_ref,
    gq_ref,
    dmemory_ref,
    dw_ref,
    drows_ref,
    flat_ref,
    grad_rows_ref,
    context_ref,
    dv_ref,
    spread_ref,
    spread_grad_ref,
    attend_ref,
    score_ref,
    sum_ref,
    out_ref,
):
    pack = pl.program_id(0)
    slots = grad_ref.shape[1]
    tokens = memory_ref.shape[1]

    @pl.when(pack == 0)
    def _():
        dw_ref[...] = jnp.zeros_like(dw_ref)
        drows_ref[...] = jnp.zeros_like(drows_ref)

    def add_row(row, value):
        drows_ref[row : row + 1, :] += value

    inside = lax.broadcasted_iota(jnp.int32, (QP, 1), 0) < NQ

    flat_ref[0:slots, :] = grad_ref[0]
    for image in range(IMG_MAX):
        part = flat_ref[image * NQ : image * NQ + QP, :]
        grad_rows_ref[image * QP : (image + 1) * QP, :] = jnp.where(inside, part, 0.0)
    @chunk_loop(ROWS, CHUNK)
    def _(start, rows):
        branch = grad_rows_ref[rows, :].astype(bf16)
        add_row(1, total(branch.astype(f32)))
        dw_ref[2] += tn(cc_ref[0, rows, :], branch)
        context_ref[rows, :] = nt(branch, w_ref[7]).astype(bf16)
    dmemory_ref[...] = jnp.zeros_like(dmemory_ref)
    dv_ref[...] = jnp.zeros_like(dv_ref)

    @pl.loop(0, IMG_MAX)
    def _(image):
        rows = pl.ds(pl.multiple_of(image * QP, QP), QP)
        first = bounds[pack, image]
        last = bounds[pack, image + 1]
        origin = (first // 16) * 16
        blocks = (last - origin + (BLOCK - 1)) // BLOCK
        spread = spread_ref
        spread_grad = spread_grad_ref
        attend_low = attend_ref
        score_low = score_ref
        spread_heads(cq_ref[0, rows, :], spread)
        spread_heads(context_ref[rows, :], spread_grad)
        logs = log_ref[0, image]

        def place_at(block, size=BLOCK):
            wanted = origin + block * size
            start = pl.multiple_of(jnp.minimum(wanted, tokens - size), 16)
            token = start + lax.broadcasted_iota(jnp.int32, (size, 1), 0)
            valid = (token >= jnp.maximum(first, wanted)) & (token < last)
            return pl.ds(start, size), valid

        def fits(index):
            below = SIZES[index - 1] if index else 0
            return (last > first) & (last - origin > below) & (last - origin <= SIZES[index])

        @pl.when(last == first)
        def _():
            gq_ref[0, rows, :] = jnp.zeros((QP, D), bf16)

        def in_one(size):
            place, valid = place_at(0, size)
            attend_part = attend_low.at[0:size]
            score_part = score_low.at[0:size]
            grad_query = attend_back(
                ck_ref[0, place, :],
                cv_ref[0, place, :],
                spread,
                spread_grad,
                valid,
                logs,
                attend_part,
                score_part,
            )
            gq_ref[0, rows, :] = grad_query.astype(bf16)
            dv_ref[place, :] += nn(attend_part[...], spread_grad[...])
            dmemory_ref[0, place, :] += nn(score_part[...], spread[...])

        for index, size in enumerate(SIZES):
            pl.when(fits(index))(functools.partial(in_one, size))

        @pl.when(last - origin > SIZES[-1])
        def _():
            sum_ref[...] = jnp.zeros_like(sum_ref)
            out_ref[...] = jnp.zeros_like(out_ref)

            @pl.loop(0, blocks)
            def _(block):
                place, valid = place_at(block)
                for pair in range(PAIRS):
                    lanes = slice(2 * QP * pair, 2 * QP * (pair + 1))
                    scores = nt(ck_ref[0, place, :], long_rows(spread, pair))
                    attend = jnp.exp2(scores * (scale * log2e) - logs[:, lanes])
                    attend = jnp.where(valid, attend, 0.0)
                    grad_attend = nt(cv_ref[0, place, :], long_rows(spread_grad, pair))
                    sum_ref[:, lanes] += total(attend * grad_attend)

            @pl.loop(0, blocks)
            def _(block):
                place, valid = place_at(block)
                key = ck_ref[0, place, :]
                products = []
                for pair in range(PAIRS):
                    lanes = slice(2 * QP * pair, 2 * QP * (pair + 1))
                    scores = nt(ck_ref[0, place, :], long_rows(spread, pair))
                    attend = jnp.exp2(scores * (scale * log2e) - logs[:, lanes])
                    attend = jnp.where(valid, attend, 0.0)
                    grad_attend = nt(cv_ref[0, place, :], long_rows(spread_grad, pair))
                    grad_scores = attend * (grad_attend - sum_ref[:, lanes])
                    grad_scores = grad_scores.astype(bf16)
                    attend_low[0:BLOCK, lanes] = attend.astype(bf16)
                    score_low[0:BLOCK, lanes] = grad_scores
                    products.append(tn(grad_scores, half_lanes(key, pair)))
                out_ref[...] += join_halves(products)
                dv_ref[place, :] += nn(attend_low[0:BLOCK, :], spread_grad[...])
                dmemory_ref[0, place, :] += nn(score_low[0:BLOCK, :], spread[...])

            gq_ref[0, rows, :] = (out_ref[...] * scale).astype(bf16)

    @chunk_loop(tokens, CHUNK)
    def _(start, rows):
        memory = memory_ref[0, rows, :]
        joined = (memory.astype(f32) + pos_ref[0, rows, :].astype(f32)).astype(bf16)
        grad_key = (dmemory_ref[0, rows, :] * scale).astype(bf16)
        grad_value = dv_ref[rows, :].astype(bf16)
        dmemory_ref[0, rows, :] = nt(grad_key, w_ref[4]) + nt(grad_value, w_ref[5])
        add_row(0, total(grad_value.astype(f32)))
        dw_ref[0] += tn(joined, grad_key)
        dw_ref[1] += tn(memory, grad_value)


def late_self_kernel(
    ordered,
    bounds,
    grad_ref,
    gcq_ref,
    target_ref,
    w_ref,
    qs_ref,
    ks_ref,
    vs_ref,
    cs_ref,
    inner_ref,
    log_ref,
    dcross_ref,
    dcross_rows_ref,
    dhead_ref,
    drow_ref,
    dtarget_ref,
    keep_ref,
    send_ref,
    small_ref,
    flat_ref,
    grad_rows_ref,
    place_ref,
    context_ref,
    gq_ref,
    gk_ref,
    gv_ref,
    spread_ref,
    spread_grad_ref,
    attend_ref,
    score_ref,
    drows_ref,
    dw_ref,
    block_ref,
):
    pack = pl.program_id(0)
    slots = target_ref.shape[1]

    @pl.when(pack == 0)
    def _():
        small_ref[...] = w_ref[SMALL].astype(f32).T
        dw_ref[0:4] = jnp.zeros((4, D, D), f32)
        dw_ref[4:6] = dcross_ref[0:2]
        dw_ref[6] = jnp.zeros((D, D), f32)
        dw_ref[7] = dcross_ref[2]
        drows_ref[...] = jnp.zeros_like(drows_ref)
        drows_ref[GAIN : GAIN + 32, :] = drow_ref[...]
        drows_ref[BIAS + 4 : BIAS + 6, :] += dcross_rows_ref[0:2, :]

    def bias(index):
        return small_ref[BIAS + index : BIAS + index + 1, :]

    def gain(index):
        return small_ref[GAIN + index : GAIN + index + 1, :]

    def add_row(row, value):
        drows_ref[row : row + 1, :] += value

    inside = lax.broadcasted_iota(jnp.int32, (QP, 1), 0) < NQ
    position = small_ref[POS : POS + QP, :]
    positions = jnp.concatenate([position] * (CHUNK // QP), axis=0)

    flat_ref[0:slots, :] = grad_ref[0]
    for image in range(IMG_MAX):
        part = flat_ref[image * NQ : image * NQ + QP, :]
        grad_rows_ref[image * QP : (image + 1) * QP, :] = jnp.where(inside, part, 0.0)
    flat_ref[0:slots, :] = target_ref[0].astype(f32)

    @chunk_loop(ROWS, CHUNK)
    def _(start, rows):
        unit, inverse = norm_parts(inner_ref[0, rows, :])
        cross_in = (unit * gain(0) + bias(9) + positions).astype(bf16)
        grad_query = gcq_ref[0, rows, :]
        add_row(BIAS + 3, total(grad_query.astype(f32)))
        dw_ref[3] += tn(cross_in, grad_query)
        place = nt(grad_query, w_ref[3])
        place_ref[rows, :] = place
        grad = grad_rows_ref[rows, :] + place
        add_row(GAIN, total(grad * unit))
        add_row(BIAS + 9, total(grad))
        grad = norm_back(unit, inverse, gain(0), grad)
        grad_rows_ref[rows, :] = grad
        branch = grad.astype(bf16)
        add_row(BIAS + 2, total(branch.astype(f32)))
        dw_ref[6] += tn(cs_ref[0, rows, :], branch)
        context_ref[rows, :] = nt(branch, w_ref[6]).astype(bf16)

    @pl.loop(0, IMG_MAX // TURNS)
    def _(step):
        for turn in range(TURNS):
            rows = pl.ds(pl.multiple_of((TURNS * step + turn) * QP, QP), QP)
            spread = spread_ref.at[turn]
            spread_grad = spread_grad_ref.at[turn]
            attend_low = attend_ref.at[turn * QP : (turn + 1) * QP]
            score_low = score_ref.at[turn * QP : (turn + 1) * QP]
            spread_heads(qs_ref[0, rows, :], spread)
            spread_heads(context_ref[rows, :], spread_grad)
            grad_query = attend_back(
                ks_ref[0, rows, :],
                vs_ref[0, rows, :],
                spread,
                spread_grad,
                inside,
                log_ref[0, TURNS * step + turn],
                attend_low,
                score_low,
            )
            gq_ref[rows, :] = grad_query.astype(bf16)
            gv_ref[rows, :] = nn(attend_low[...], spread_grad[...]).astype(bf16)
            gk_ref[rows, :] = (nn(score_low[...], spread[...]) * scale).astype(bf16)

    for start in range(0, ROWS, CHUNK):
        rows = slice(start, start + CHUNK)
        images = range(start // QP, (start + CHUNK) // QP)
        parts = [flat_ref[image * NQ : image * NQ + QP, :] for image in images]
        target = jnp.concatenate([jnp.where(inside, part, 0.0) for part in parts], axis=0)
        joined_t = (target + positions).astype(bf16).T
        grad_query = gq_ref[rows, :]
        grad_key = gk_ref[rows, :]
        grad_value = gv_ref[rows, :]
        add_row(BIAS + 0, total(grad_query.astype(f32)))
        add_row(BIAS + 1, total(grad_value.astype(f32)))
        dw_ref[0] += nn(joined_t, grad_query)
        dw_ref[1] += nn(joined_t, grad_key)
        dw_ref[2] += tn(target.astype(bf16), grad_value)
        grad_joined = nt(grad_query, w_ref[0]) + nt(grad_key, w_ref[1])
        grad_rows_ref[rows, :] += grad_joined + nt(grad_value, w_ref[2])
        grad_place = grad_joined + place_ref[rows, :]
        for image in range(CHUNK // QP):
            drows_ref[POS : POS + QP, :] += grad_place[image * QP : (image + 1) * QP, :]
    for image in range(IMG_MAX):
        part = grad_rows_ref[image * QP : image * QP + NQ, :]
        dtarget_ref[0, image * NQ : (image + 1) * NQ, :] = part

    @pl.when(pack == pl.num_programs(0) - 1)
    def _():
        small = drows_ref[...].T
        dw_ref[SMALL, :, POS:] = small[:, POS:]
        dw_ref[SMALL, :, :POS] = small[:, :POS] + dhead_ref[...]
        half, height, unused = keep_ref.shape
        parts = 2 * half
        share = D // parts
        used = (SMALL + 1) * share
        if height > used:
            block_ref[:, used:, :] = jnp.zeros((parts, height - used, D), f32)

        @pl.loop(0, parts)
        def _(device):
            place = place_of(device, bounds, ordered, parts)
            rows = pl.ds(pl.multiple_of(device * share, share), share)
            for unit in range(SMALL + 1):
                block_ref[place, unit * share : (unit + 1) * share, :] = dw_ref[unit, rows, :]

        keep_ref[...] = block_ref[0:half]
        send_ref[...] = block_ref[half:].astype(bf16)


def whole(shape):
    zeros = (0,) * len(shape)
    return pl.BlockSpec(shape, lambda *unused: zeros)


def by_pack(shape):
    zeros = (0,) * (len(shape) - 1)
    return pl.BlockSpec((1,) + tuple(shape[1:]), lambda pack, *unused: (pack,) + zeros)


LIMIT = 60 * 1024 * 1024


def params(axes):
    return pltpu.CompilerParams(
        dimension_semantics=("arbitrary",) * axes, vmem_limit_bytes=LIMIT
    )


def early_self(bounds, target, memory, memory_pos, mine, other, ordered):
    packs, slots, unused = target.shape
    tokens = memory.shape[1]
    height = mine.shape[1]
    wide = HEADS * QP
    low_rows = jax.ShapeDtypeStruct((packs, ROWS, D), bf16)
    rows = jax.ShapeDtypeStruct((packs, ROWS, D), f32)
    low_tokens = jax.ShapeDtypeStruct((packs, tokens, D), bf16)
    mean = jax.ShapeDtypeStruct((packs, 1, D), f32)
    logs = jax.ShapeDtypeStruct((packs, IMG_MAX, 1, wide), f32)
    outs = [rows] + [low_rows] * 4 + [rows, low_rows, low_tokens, low_tokens, mean, logs]
    units = jax.ShapeDtypeStruct((SMALL + 1, D, D), bf16)
    return pl.pallas_call(
        functools.partial(early_self_kernel, ordered),
        grid_spec=pltpu.PrefetchScalarGridSpec(
            num_scalar_prefetch=1,
            grid=(packs,),
            in_specs=[
                by_pack(target.shape),
                by_pack(memory.shape),
                by_pack(memory_pos.shape),
                whole(mine.shape),
                whole(other.shape),
            ],
            out_specs=[by_pack(out.shape) for out in outs] + [whole(units.shape)],
            scratch_shapes=[
                pltpu.VMEM((D, D), f32),
                pltpu.VMEM((slots + 32, D), f32),
                pltpu.VMEM((ROWS, D), f32),
                pltpu.VMEM((TURNS, wide, D), bf16),
                pltpu.VMEM((2 * mine.shape[0], height, D), bf16),
                pltpu.VMEM((SMALL + 1, D, D), f32),
            ],
        ),
        out_shape=outs + [units],
        compiler_params=params(1),
        cost_estimate=pl.CostEstimate(
            flops=packs * 8_000_000_000, bytes_accessed=packs * 9_000_000, transcendentals=0
        ),
        name="early_self",
    )(bounds, target, memory, memory_pos, mine, other)


def early_cross(bounds, rows, query, key, value, mean, weights, slots):
    packs = rows.shape[0]
    tokens = key.shape[1]
    wide = HEADS * QP
    outs = [
        jax.ShapeDtypeStruct((packs, slots, D), f32),
        jax.ShapeDtypeStruct(query.shape, bf16),
        jax.ShapeDtypeStruct((packs, IMG_MAX, 1, wide), f32),
    ]
    arrays = [rows, query, key, value, mean]
    return pl.pallas_call(
        early_cross_kernel,
        grid_spec=pltpu.PrefetchScalarGridSpec(
            num_scalar_prefetch=1,
            grid=(packs,),
            in_specs=[by_pack(array.shape) for array in arrays]
            + [
                pl.BlockSpec((1, D, D), lambda *unused: (7, 0, 0)),
                pl.BlockSpec((1, D, D), lambda *unused: (SMALL, 0, 0)),
            ],
            out_specs=[by_pack(out.shape) for out in outs],
            scratch_shapes=[
                pltpu.VMEM((ROWS, D), f32),
                pltpu.VMEM((wide, D), bf16),
                pltpu.VMEM((tokens, wide), f32),
                pltpu.VMEM((1, wide), f32),
                pltpu.VMEM((1, wide), f32),
                pltpu.VMEM((QP, D), f32),
                pltpu.VMEM((1, D), f32),
            ],
        ),
        out_shape=outs,
        compiler_params=params(1),
        cost_estimate=pl.CostEstimate(
            flops=packs * 8_000_000_000, bytes_accessed=packs * 7_000_000, transcendentals=0
        ),
        name="early_cross",
    )(bounds, *arrays, weights, weights)


def middle(bounds, x, cotangents, mine, other, small, head_bias, ordered):
    packs, slots, unused = x.shape
    half, height, unused = mine.shape
    outs = [
        jax.ShapeDtypeStruct(x.shape, bf16),
        jax.ShapeDtypeStruct(x.shape, f32),
        jax.ShapeDtypeStruct(mine.shape, f32),
        jax.ShapeDtypeStruct(mine.shape, bf16),
        jax.ShapeDtypeStruct((D, POS), f32),
        jax.ShapeDtypeStruct((32, D), f32),
    ]
    return pl.pallas_call(
        functools.partial(middle_kernel, ordered),
        grid_spec=pltpu.PrefetchScalarGridSpec(
            num_scalar_prefetch=1,
            grid=(packs,),
            in_specs=[
                by_pack(x.shape),
                *[by_pack(array.shape) for array in cotangents],
                whole(mine.shape),
                whole(other.shape),
                pl.BlockSpec((1, D, D), lambda *unused: (SMALL, 0, 0)),
                whole(head_bias.shape),
            ],
            out_specs=[by_pack(x.shape), by_pack(x.shape)] + [whole(out.shape) for out in outs[2:]],
            scratch_shapes=[
                pltpu.VMEM((D, D), f32),
                pltpu.VMEM((2 * FF_BLOCKS, 1, D), f32),
                pltpu.VMEM((2, D, D), bf16),
                pltpu.VMEM((slots, D), bf16),
                pltpu.VMEM((slots, D), f32),
                pltpu.VMEM((slots, D), f32),
                pltpu.VMEM((slots, D), bf16),
                pltpu.VMEM((FF_BLOCKS, slots, D), bf16),
                pltpu.VMEM((FF_BLOCKS, slots, D), f32),
                pltpu.VMEM((2 * half, height, D), bf16),
                pltpu.VMEM((2 * half, height, D), f32),
                pltpu.VMEM((2, D, D), f32),
            ],
        ),
        out_shape=outs,
        compiler_params=params(1),
        cost_estimate=pl.CostEstimate(
            flops=packs * 10_000_000_000, bytes_accessed=packs * 9_000_000, transcendentals=0
        ),
        name="middle",
    )(bounds, x, *cotangents, mine, other, small, head_bias)


def late_cross(bounds, grad, memory, memory_pos, weights, saved):
    packs, slots, unused = grad.shape
    tokens = memory.shape[1]
    wide = HEADS * QP
    outs = [
        jax.ShapeDtypeStruct((packs, ROWS, D), bf16),
        jax.ShapeDtypeStruct(memory.shape, f32),
        jax.ShapeDtypeStruct((3, D, D), f32),
        jax.ShapeDtypeStruct((8, D), f32),
    ]
    return pl.pallas_call(
        late_cross_kernel,
        grid_spec=pltpu.PrefetchScalarGridSpec(
            num_scalar_prefetch=1,
            grid=(packs,),
            in_specs=[
                by_pack(grad.shape),
                by_pack(memory.shape),
                by_pack(memory_pos.shape),
                whole(weights.shape),
            ]
            + [by_pack(array.shape) for array in saved],
            out_specs=[by_pack(outs[0].shape), by_pack(outs[1].shape)]
            + [whole(out.shape) for out in outs[2:]],
            scratch_shapes=[
                pltpu.VMEM((slots + 32, D), f32),
                pltpu.VMEM((ROWS, D), f32),
                pltpu.VMEM((ROWS, D), bf16),
                pltpu.VMEM((tokens, D), f32),
                pltpu.VMEM((wide, D), bf16),
                pltpu.VMEM((wide, D), bf16),
                pltpu.VMEM((SIZES[-1], wide), bf16),
                pltpu.VMEM((SIZES[-1], wide), bf16),
                pltpu.VMEM((1, wide), f32),
                pltpu.VMEM((QP, D), f32),
            ],
        ),
        out_shape=outs,
        compiler_params=params(1),
        cost_estimate=pl.CostEstimate(
            flops=packs * 12_000_000_000, bytes_accessed=packs * 9_000_000, transcendentals=0
        ),
        name="late_cross",
    )(bounds, grad, memory, memory_pos, weights, *saved)


def late_self(bounds, grad, grad_query, target, weights, saved, sums, block, ordered):
    packs, slots, unused = target.shape
    wide = HEADS * QP
    half, height, unused = block
    outs = [
        jax.ShapeDtypeStruct(target.shape, f32),
        jax.ShapeDtypeStruct(block, f32),
        jax.ShapeDtypeStruct(block, bf16),
    ]
    return pl.pallas_call(
        functools.partial(late_self_kernel, ordered),
        grid_spec=pltpu.PrefetchScalarGridSpec(
            num_scalar_prefetch=1,
            grid=(packs,),
            in_specs=[
                by_pack(grad.shape),
                by_pack(grad_query.shape),
                by_pack(target.shape),
                whole(weights.shape),
            ]
            + [by_pack(array.shape) for array in saved]
            + [whole(array.shape) for array in sums],
            out_specs=[by_pack(target.shape), whole(block), whole(block)],
            scratch_shapes=[
                pltpu.VMEM((D, D), f32),
                pltpu.VMEM((slots + 32, D), f32),
                pltpu.VMEM((ROWS, D), f32),
                pltpu.VMEM((ROWS, D), f32),
                pltpu.VMEM((ROWS, D), bf16),
                pltpu.VMEM((ROWS, D), bf16),
                pltpu.VMEM((ROWS, D), bf16),
                pltpu.VMEM((ROWS, D), bf16),
                pltpu.VMEM((TURNS, wide, D), bf16),
                pltpu.VMEM((TURNS, wide, D), bf16),
                pltpu.VMEM((TURNS * QP, wide), bf16),
                pltpu.VMEM((TURNS * QP, wide), bf16),
                pltpu.VMEM((D, D), f32),
                pltpu.VMEM(weights.shape, f32),
                pltpu.VMEM((2 * half, height, D), f32),
            ],
        ),
        out_shape=outs,
        compiler_params=params(1),
        cost_estimate=pl.CostEstimate(
            flops=packs * 10_000_000_000, bytes_accessed=packs * 7_000_000, transcendentals=0
        ),
        name="late_self",
    )(bounds, grad, grad_query, target, weights, *saved, *sums)


def stack(parts):
    return jnp.concatenate(parts, axis=0)


def fold(keep, received, count):
    for part in received:
        keep = keep + part.astype(f32)
    size = keep.shape[0] // count
    pieces = [keep[index * size : (index + 1) * size] for index in range(count)]
    return pieces[:1] + [piece.astype(bf16) for piece in pieces[1:]]


def run_of_images(segment, me):
    edge = jnp.arange(16, dtype=jnp.int32)
    below = segment[:, None, :] < edge[None, :, None]
    counts = jnp.sum(below.astype(jnp.int32), axis=-1)
    images = jnp.max(jnp.where(segment < IMG_MAX, segment + 1, 0), axis=-1)
    result = jnp.where(edge[None, :] == IMG_MAX + 1, images[:, None], counts)
    return jnp.where(edge[None, :] == ME, me, result)


def taller(rows):
    return jnp.pad(rows, ((0, -rows.shape[0] % 16), (0, 0)))


def pack_early(project, output, classes, box_final, query_pos, gains, biases):
    share = project.shape[1]
    columns = [
        classes,
        box_final,
        gains.T,
        biases.T,
        jnp.zeros((share, POS - BIAS - 13), bf16),
        query_pos.T,
        jnp.zeros((share, D - POS - NQ), bf16),
    ]
    small = jnp.concatenate(columns, axis=1)
    return taller(jnp.concatenate([project.reshape(-1, D), output.reshape(-1, D), small], axis=0))


def pack_middle(box, shrink, expand, expand_bias):
    extra = jnp.pad(expand_bias[None], ((1, EXTRA - 2), (0, D - expand_bias.shape[0])))
    return taller(jnp.concatenate([shrink, expand.T, box[0], box[1], extra], axis=0))


def pack_kernel(
    project,
    output,
    classes,
    final_t,
    gains,
    shifts_t,
    places_t,
    shrink,
    expand_t,
    box,
    row,
    out,
):
    share = project.shape[1]
    small = nn(classes[...], lanes_of(CLS, 0, D)) + tn(final_t[...], lanes_of(4, CLS, D))
    small += tn(gains[...], lanes_of(4, GAIN, D)) + nn(shifts_t[...], lanes_of(13, BIAS, D))
    small += nn(places_t[...], lanes_of(NQ, POS, D))
    first = [project[...].astype(f32).reshape(-1, D), output[...].astype(f32).reshape(-1, D), small]
    first = jnp.concatenate(first, axis=0)
    rest = -first.shape[0] % 16
    count = row.shape[1]
    vector = nn(row[...], lanes_of(count, 0, D))
    index = lax.broadcasted_iota(jnp.int32, (EXTRA, 1), 0)
    extra = jnp.where(index == 1, vector, 0.0)
    blocks = [first, jnp.zeros((rest, D), f32), shrink[...].astype(f32), expand_t[...].astype(f32)]
    blocks += [box[...].astype(f32).reshape(2 * share, D), extra]
    out[...] = jnp.concatenate(blocks, axis=0).astype(bf16)


def pack_both(project, output, classes, final, places, gains, shifts, box, shrink, expand, row):
    share = project.shape[1]
    early_rows = (SMALL + 1) * share
    early_rows += -early_rows % 16
    if share % 8:
        first = pack_early(project, output, classes, final, places, gains, shifts)
        return jnp.concatenate([first, pack_middle(box, shrink, expand, row)]), early_rows
    rows = early_rows + 2 * shrink.shape[0] + 2 * share + EXTRA
    block = pl.pallas_call(
        pack_kernel,
        out_shape=jax.ShapeDtypeStruct((rows, D), bf16),
        name="pack",
    )(
        project,
        output,
        classes,
        final.T,
        gains,
        shifts.T,
        places.T,
        shrink,
        expand.T,
        box,
        row[None],
    )
    return block, early_rows


def block_rows(devices):
    return [FF_BLOCKS * D // devices] * 2 + [D // devices] * 2


def cut(blocks, devices):
    marks = [0]
    for rows in block_rows(devices):
        marks.append(marks[-1] + rows)
    return [blocks[:, low:high] for low, high in zip(marks, marks[1:])], blocks[:, marks[-1] :]


def regroup(blocks, devices, parts):
    pieces, extra = cut(blocks, devices)
    pieces = [piece.reshape(parts, -1, D) for piece in pieces]
    head = jnp.broadcast_to(extra[0:1, 0:1], (parts, 1, D))
    row = extra[:, 1, : FF_BLOCKS * D // devices].reshape(parts, 1, -1)
    row = jnp.pad(row, ((0, 0), (0, EXTRA - 2), (0, D - row.shape[2])))
    result = jnp.concatenate(pieces + [head, row], axis=1)
    return jnp.pad(result, ((0, 0), (0, -result.shape[1] % 16), (0, 0)))


def regroup_units(blocks, devices, parts):
    units = SMALL + 1
    share = D // devices
    result = blocks[:, : units * share].reshape(devices, units, share, D).swapaxes(0, 1)
    result = result.reshape(units, parts, D // parts, D).swapaxes(0, 1).reshape(parts, -1, D)
    return jnp.pad(result, ((0, 0), (0, -result.shape[1] % 16), (0, 0)))


def parts_of(devices):
    return devices if FF_BLOCKS * D // devices % 16 == 0 else FF_BLOCKS


def bit_groups(devices):
    bits = [1 << k for k in range(1, devices.bit_length() - 1)]
    groups = [(1,)]
    while bits:
        groups.append((bits[0], bits[-1]) if len(bits) > 1 else (bits[0],))
        bits = bits[1:-1]
    return groups


def order_of(distance, devices):
    place = 0
    for bits in bit_groups(devices):
        for bit in bits[::-1]:
            place = 2 * place + distance // bit % 2
    return place


def mixes(bits):
    result = [0]
    for bit in bits:
        result += [mix | bit for mix in result]
    return result


def swap(value, bits, devices):
    return lax.ppermute(value, AXES, [(k, k ^ bits) for k in range(devices)])


def trade(held, bits, devices):
    return [swap(held, mix, devices) if mix else held for mix in mixes(bits)]


def deliver(sends, bits, devices):
    return [swap(send, mix, devices) for mix, send in zip(mixes(bits)[1:], sends)]


def counted(blocks, devices, me):
    places = [order_of(device, devices) for device in range(devices)]
    order = jnp.array(places)[jnp.arange(devices) ^ me]
    return jnp.take(blocks, order, axis=0)


def stepped(blocks, devices, me):
    distances = [0] * devices
    for device in range(devices):
        distances[order_of(device, devices)] = device
    return jnp.take(blocks, jnp.array(distances) ^ me, axis=0)


def unpack_middle(block, devices):
    pieces, extra = cut(block[None], devices)
    shrink, expand, box_one, box_two = [piece[0] for piece in pieces]
    row = extra[0, 1, 0 : shrink.shape[0]]
    return shrink, expand.T, jnp.stack([box_one, box_two]), row, extra[0, 0, 0 : CLS + 4]


def finish_kernel(count, keep, *refs):
    total_block = keep[0]
    for ref in refs[:count]:
        total_block += ref[0].astype(f32)
    project, output, classes, final_t, places_t, gains, shifts_t = refs[count:]
    share = project.shape[1]
    project[...] = total_block[: 6 * share].reshape(6, share, D)
    output[...] = total_block[6 * share : 8 * share].reshape(2, share, D)
    small = total_block[8 * share : 9 * share]
    classes[...] = small[:, 0:CLS]
    places_t[...] = small[:, POS : POS + NQ]
    shifts_t[...] = small[:, BIAS : BIAS + 13]
    turned = small[:, 0:POS].T
    final_t[...] = turned[CLS : CLS + 4]
    gains[...] = turned[GAIN : GAIN + 4]


def finish_early(keep, received, devices):
    share = D // devices
    if share % 8:
        return unpack_early(fold(keep, received, 1)[0][0], devices)
    shapes = [(6, share, D), (2, share, D), (share, CLS), (4, share), (share, NQ), (4, share)]
    shapes.append((share, 13))
    project, output, classes, final_t, places_t, gains, shifts_t = pl.pallas_call(
        functools.partial(finish_kernel, len(received)),
        out_shape=[jax.ShapeDtypeStruct(shape, f32) for shape in shapes],
        name="finish",
    )(keep, *received)
    return project, output, classes, final_t.T, places_t.T, gains, shifts_t.T


def unpack_early(block, devices):
    units = SMALL + 1
    share = D // devices
    block = block[: units * share].reshape(units, share, D)
    small = block[SMALL]
    return (
        block[0:6],
        block[6:8],
        small[:, 0:CLS],
        small[:, CLS : CLS + 4],
        small[:, POS : POS + NQ].T,
        small[:, GAIN : GAIN + 4].T,
        small[:, BIAS : BIAS + 13].T,
    )


def per_device(
    target,
    memory,
    memory_pos,
    segment,
    project_weight,
    output_weight,
    expand_weight,
    shrink_weight,
    box_weight,
    class_weight,
    box_final,
    query_pos,
    norm_gains,
    biases,
    expand_bias,
    head_bias,
    output_cotangent,
    logit_cotangent,
    box_cotangent,
):
    devices = lax.axis_size(AXES)
    me = lax.axis_index(AXES)
    groups = bit_groups(devices)
    parts = parts_of(devices)
    ordered = parts == devices
    slots = target.shape[1]

    both, height = pack_both(
        project_weight,
        output_weight,
        class_weight,
        box_final,
        query_pos,
        norm_gains,
        biases,
        box_weight,
        shrink_weight,
        expand_weight,
        expand_bias,
    )
    both = both[None]
    both_parts = trade(both, groups[-1], devices)
    both_parts, logit_cotangent, box_cotangent = lax.optimization_barrier(
        (both_parts, logit_cotangent, box_cotangent)
    )
    early_held = stack([part[:, :height] for part in both_parts])
    middle_held = stack([part[:, height:] for part in both_parts])
    for bits in groups[-2:1:-1]:
        early_held = stack(trade(early_held, bits, devices))
    early_parts = trade(early_held, groups[1], devices)
    bounds = run_of_images(segment, me)
    head_row = jnp.pad(head_bias.astype(f32), (0, POS - CLS - 4))
    head_row = jnp.broadcast_to(head_row[None], (8, POS))
    rest = jnp.zeros(logit_cotangent.shape[:2] + (POS - CLS - 4,), bf16)
    head_cotangent = jnp.concatenate([logit_cotangent, box_cotangent, rest], axis=-1)
    early_parts, bounds, head_row, head_cotangent, middle_held = lax.optimization_barrier(
        (early_parts, bounds, head_row, head_cotangent, middle_held)
    )
    early_mine = stack(early_parts)
    early_other = swap(early_mine, 1, devices)
    if not ordered:
        blocks = counted(jnp.concatenate([early_mine, early_other]), devices, me)
        blocks = regroup_units(blocks, devices, parts)
        early_mine, early_other = blocks[: parts // 2], blocks[parts // 2 :]
    middle_parts = trade(middle_held, groups[-2], devices)
    rows, *saved = early_self(
        bounds, target, memory, memory_pos, early_mine, early_other, ordered
    )
    query, key, value, mean, self_logs, weights = saved[5:]
    middle_parts, query = lax.optimization_barrier((middle_parts, query))
    for bits in groups[-3:0:-1]:
        middle_parts = trade(stack(middle_parts), bits, devices)
    middle_mine = stack(middle_parts)
    middle_mine, query = lax.optimization_barrier((middle_mine, query))
    middle_other = swap(middle_mine, 1, devices)
    after, context, logs = early_cross(bounds, rows, query, key, value, mean, weights, slots)
    if not ordered:
        blocks = counted(jnp.concatenate([middle_mine, middle_other]), devices, me)
        blocks = regroup(blocks, devices, parts)
        middle_mine, middle_other = blocks[: parts // 2], blocks[parts // 2 :]
    layer, grad, keep, send, dhead, drow = middle(
        bounds,
        after,
        [output_cotangent, head_cotangent],
        middle_mine,
        middle_other,
        weights,
        head_row,
        ordered,
    )

    def real_blocks(keep, send, change):
        if ordered:
            return keep, send
        blocks = jnp.concatenate([keep, send.astype(f32)])
        blocks = stepped(change(blocks, parts, devices), devices, me)
        return blocks[: devices // 2], blocks[devices // 2 :].astype(bf16)

    def counts(index):
        return 1 << len(groups[index]) if index < len(groups) else 1

    keep, send = real_blocks(keep, send, regroup)
    grad, keep, send = lax.optimization_barrier((grad, keep, send))
    received = deliver([send], groups[0], devices)
    grad_query, dmemory, dcross, dcross_rows = late_cross(
        bounds, grad, memory, memory_pos, weights, [query, key, value, context, logs]
    )
    grad_query, received = lax.optimization_barrier((grad_query, received))
    keep, *sends = fold(keep, received, counts(1))
    grad_query, keep, sends = lax.optimization_barrier((grad_query, keep, sends))
    received = deliver(sends, groups[1], devices)
    sums = [dcross, dcross_rows, dhead, drow]
    block = early_mine.shape
    late_saved = saved[:5] + [self_logs]
    dtarget, early_keep, early_send = late_self(
        bounds, grad, grad_query, target, weights, late_saved, sums, block, ordered
    )
    early_keep, early_send, received = lax.optimization_barrier(
        (early_keep, early_send, received)
    )
    early_keep, early_send = real_blocks(early_keep, early_send, regroup_units)
    early_received = deliver([early_send], groups[0], devices)
    for index in range(2, len(groups)):
        keep, *sends = fold(keep, received, counts(index))
        received = deliver(sends, groups[index], devices)
    early_keep, *early_sends = fold(early_keep, early_received, counts(1))
    early_received = deliver(early_sends, groups[1], devices)
    early_received, received = lax.optimization_barrier((early_received, received))
    for index in range(2, len(groups)):
        early_keep, *early_sends = fold(early_keep, early_received, counts(index))
        early_received = deliver(early_sends, groups[index], devices)
    middle_sum = fold(keep, received, 1)[0]
    middle_grads = unpack_middle(middle_sum[0], devices)
    early_received, middle_grads = lax.optimization_barrier((early_received, middle_grads))
    shrink, expand, box, expand_row, head = middle_grads
    project, output, classes, final, places, gains, shifts = finish_early(
        early_keep, early_received, devices
    )
    return (
        layer,
        dtarget,
        dmemory,
        project,
        output,
        expand,
        shrink,
        box,
        classes,
        final,
        places,
        gains,
        shifts,
        expand_row,
        head,
    )


def solution(mesh):
    both = ("dp", "fsdp")
    by_rows = P(both, None, None)
    return jax.shard_map(
        per_device,
        mesh=mesh,
        in_specs=(
            by_rows,
            by_rows,
            by_rows,
            P(both, None),
            P(None, both, None),
            P(None, both, None),
            P(None, both),
            P(both, None),
            P(None, both, None),
            P(both, None),
            P(both, None),
            P(None, both),
            P(None, both),
            P(None, both),
            P(both),
            P(),
            by_rows,
            by_rows,
            by_rows,
        ),
        out_specs=(
            by_rows,
            by_rows,
            by_rows,
            P(None, both, None),
            P(None, both, None),
            P(None, both),
            P(both, None),
            P(None, both, None),
            P(both, None),
            P(both, None),
            P(None, both),
            P(None, both),
            P(None, both),
            P(both),
            P(),
        ),
        check_vma=False,
    )
```

```python
import functools

import jax
import jax.numpy as jnp
from jax import lax
from jax.experimental import pallas as pl
from jax.experimental.pallas import tpu as pltpu
from jax.sharding import PartitionSpec as P

D = 256
HEADS = 8
NQ = 100
CLS = 92
IMG_MAX = 12
HEAD_DIM = 32
QP = 128
ROWS = IMG_MAX * QP
TURNS = 3
PAIRS = HEADS // 2
BLOCK = 256
SIZES = (128, 192, 256, 384, 512)
SHORT = (128, 192, 256, 512)
CHUNK = 512
STEP = 400
FF_BLOCKS = 8
GAIN = 96
BIAS = 100
POS = 128
SMALL = 8
EXTRA = 16
ME = 14

epsilon = 1e-05
masked = -1000000000.0
scale = HEAD_DIM ** (-0.5)
log2e = 1.4426950408889634
gelu_a = 0.7978845608028654
gelu_b = gelu_a * 0.044715
AXES = ("dp", "fsdp")
f32 = jnp.float32
bf16 = jnp.bfloat16


def nn(left, right):
    return jnp.dot(left, right, preferred_element_type=f32)


def nt(left, right):
    return lax.dot_general(left, right, (((1,), (1,)), ((), ())), preferred_element_type=f32)


def tn(left, right):
    return lax.dot_general(left, right, (((0,), (0,)), ((), ())), preferred_element_type=f32)


def total(value):
    return jnp.sum(value, axis=0, keepdims=True)


def norm_parts(value):
    middle = jnp.mean(value, axis=-1, keepdims=True)
    centered = value - middle
    spread = jnp.mean(centered * centered, axis=-1, keepdims=True)
    inverse = lax.rsqrt(spread + epsilon)
    return centered * inverse, inverse


def norm_back(unit, inverse, gain, grad):
    scaled = grad * gain
    first = jnp.mean(scaled, axis=-1, keepdims=True)
    second = jnp.mean(scaled * unit, axis=-1, keepdims=True)
    return inverse * (scaled - first - unit * second)


def gelu_parts(value):
    square = value * value
    cdf = 0.5 + 0.5 * jnp.tanh(value * (gelu_a + gelu_b * square))
    result = value * cdf
    slope = cdf + (result - result * cdf) * (2.0 * gelu_a + 6.0 * gelu_b * square)
    return result, slope


def spread_heads(value, spread_ref):
    lane = lax.broadcasted_iota(jnp.int32, (1, D), 1) // HEAD_DIM
    for head in range(HEADS):
        keep = (lane == head).astype(f32).astype(bf16)
        spread_ref[head * QP : (head + 1) * QP, :] = value * keep


def pair_rows(ref, pair):
    side = pair // 2 * (D // 2)
    return ref[2 * QP * pair : 2 * QP * (pair + 1), side : side + D // 2]


def long_rows(ref, pair):
    return ref[2 * QP * pair : 2 * QP * (pair + 1), :]


def head_lane(lanes):
    return lax.broadcasted_iota(jnp.int32, (1, lanes), 1) // HEAD_DIM


def join_pairs(products):
    lane = head_lane(D)
    result = products[0][:QP]
    for head in range(1, HEADS):
        part = products[head // 2][(head % 2) * QP : (head % 2 + 1) * QP]
        result = jnp.where(lane == head, part, result)
    return result


def join_halves(products):
    lane = head_lane(D // 2)
    halves = []
    for half in range(2):
        low, high = products[2 * half : 2 * half + 2]
        part = jnp.where(lane == 2, high[:QP], high[QP:])
        part = jnp.where(lane == 1, low[QP:], part)
        halves.append(jnp.where(lane == 0, low[:QP], part))
    return jnp.concatenate(halves, axis=1)


def half_lanes(value, pair):
    side = pair // 2 * (D // 2)
    return value[:, side : side + D // 2]


def row_loop(size, step):
    def run(body):
        @pl.loop(0, size // step)
        def _(index):
            start = pl.multiple_of(index * step, step)
            body(start, pl.ds(start, step))

    return run


def chunk_loop(size, step):
    def run(body):
        for start in range(0, size, step):
            body(start, slice(start, start + step))

    return run


def attend_block(key, value, spread_ref, valid, halves):
    scores = [nt(half_lanes(key, pair), pair_rows(spread_ref, pair)) for pair in range(PAIRS)]
    attends = []
    logs = []
    for pair in range(PAIRS):
        kept = jnp.where(valid, scores[pair], masked)
        top = jnp.max(kept, axis=0, keepdims=True)
        raised = jnp.exp2((kept - top) * (scale * log2e))
        sums = total(raised)
        attends.append((raised * (1.0 / sums)).astype(bf16))
        logs.append(top * (scale * log2e) + jnp.log2(sums))
    if halves:
        products = [tn(attends[pair], half_lanes(value, pair)) for pair in range(PAIRS)]
        context = join_halves(products)
    else:
        context = join_pairs([tn(attends[pair], value) for pair in range(PAIRS)])
    return context, jnp.concatenate(logs, axis=1)


def place_of(device, bounds, ordered, parts):
    return order_of(device ^ bounds[0, ME], parts) if ordered else device


def early_self_kernel(
    ordered,
    bounds,
    target_ref,
    memory_ref,
    pos_ref,
    mine_ref,
    other_ref,
    after_ref,
    qs_ref,
    ks_ref,
    vs_ref,
    cs_ref,
    inner_ref,
    cq_ref,
    ck_ref,
    cv_ref,
    mean_ref,
    log_ref,
    w_ref,
    small_ref,
    flat_ref,
    rows_ref,
    spread_ref,
    block_ref,
    unit_ref,
):
    pack = pl.program_id(0)
    slots = target_ref.shape[1]
    tokens = memory_ref.shape[1]
    near = mine_ref.shape[0]
    parts = 2 * near
    share = D // parts

    @pl.when(pack == 0)
    def _():
        block_ref[0:near] = mine_ref[...]
        block_ref[near:] = other_ref[...]

        @pl.loop(0, parts)
        def _(device):
            block = block_ref[place_of(device, bounds, ordered, parts)].astype(f32)
            rows = pl.ds(pl.multiple_of(device * share, share), share)
            for unit in range(SMALL + 1):
                unit_ref[unit, rows, :] = block[unit * share : (unit + 1) * share]

        w_ref[...] = unit_ref[...].astype(bf16)
        small_ref[...] = unit_ref[SMALL].T

    def bias(index):
        return small_ref[BIAS + index : BIAS + index + 1, :]

    def gain(index):
        return small_ref[GAIN + index : GAIN + index + 1, :]

    inside = lax.broadcasted_iota(jnp.int32, (QP, 1), 0) < NQ
    position = small_ref[POS : POS + QP, :]
    positions = jnp.concatenate([position] * (CHUNK // QP), axis=0)

    mean_ref[0] = jnp.zeros((1, D), f32)
    @chunk_loop(tokens, CHUNK)
    def _(start, rows):
        memory = memory_ref[0, rows, :]
        joined = (memory.astype(f32) + pos_ref[0, rows, :].astype(f32)).astype(bf16)
        ck_ref[0, rows, :] = nn(joined, w_ref[4]).astype(bf16)
        value = (nn(memory, w_ref[5]) + bias(4)).astype(bf16)
        cv_ref[0, rows, :] = value
        mean_ref[0] += total(value.astype(f32)) * (1.0 / tokens)

    flat_ref[0:slots, :] = target_ref[0].astype(f32)
    for image in range(IMG_MAX):
        part = flat_ref[image * NQ : image * NQ + QP, :]
        rows_ref[image * QP : (image + 1) * QP, :] = jnp.where(inside, part, 0.0)

    @chunk_loop(ROWS, CHUNK)
    def _(start, rows):
        target = rows_ref[rows, :]
        joined = (target + positions).astype(bf16)
        qs_ref[0, rows, :] = (nn(joined, w_ref[0]) + bias(0)).astype(bf16)
        ks_ref[0, rows, :] = nn(joined, w_ref[1]).astype(bf16)
        vs_ref[0, rows, :] = (nn(target.astype(bf16), w_ref[2]) + bias(1)).astype(bf16)

    @pl.loop(0, IMG_MAX // TURNS)
    def _(step):
        for turn in range(TURNS):
            rows = pl.ds(pl.multiple_of((TURNS * step + turn) * QP, QP), QP)
            spread = spread_ref.at[turn]
            spread_heads(qs_ref[0, rows, :], spread)
            context, logs = attend_block(
                ks_ref[0, rows, :], vs_ref[0, rows, :], spread, inside, True
            )
            cs_ref[0, rows, :] = context.astype(bf16)
            log_ref[0, TURNS * step + turn] = logs

    @chunk_loop(ROWS, CHUNK)
    def _(start, rows):
        value = rows_ref[rows, :] + nn(cs_ref[0, rows, :], w_ref[6]) + bias(2)
        inner_ref[0, rows, :] = value
        unit, unused = norm_parts(value)
        after = unit * gain(0) + bias(9)
        after_ref[0, rows, :] = after
        query = nn((after + positions).astype(bf16), w_ref[3]) + bias(3)
        cq_ref[0, rows, :] = query.astype(bf16)


def early_cross_kernel(
    bounds,
    rows_in_ref,
    cq_ref,
    ck_ref,
    cv_ref,
    mean_ref,
    w_ref,
    small_in_ref,
    after_ref,
    cc_ref,
    log_ref,
    rows_ref,
    spread_ref,
    score_ref,
    top_ref,
    sum_ref,
    out_ref,
    bias_ref,
):
    pack = pl.program_id(0)
    tokens = ck_ref.shape[1]

    @pl.when(pack == 0)
    def _():
        bias_ref[...] = small_in_ref[0].astype(f32).T[BIAS + 5 : BIAS + 6]

    @pl.loop(0, IMG_MAX)
    def _(image):
        rows = pl.ds(pl.multiple_of(image * QP, QP), QP)
        first = bounds[pack, image]
        last = bounds[pack, image + 1]
        origin = (first // 16) * 16
        blocks = (last - origin + (BLOCK - 1)) // BLOCK
        spread = spread_ref
        spread_heads(cq_ref[0, rows, :], spread)

        def place_at(block, size=BLOCK):
            wanted = origin + block * size
            start = pl.multiple_of(jnp.minimum(wanted, tokens - size), 16)
            token = start + lax.broadcasted_iota(jnp.int32, (size, 1), 0)
            valid = (token >= jnp.maximum(first, wanted)) & (token < last)
            return pl.ds(start, size), valid

        def fits(index):
            below = SHORT[index - 1] if index else 0
            return (last > first) & (last - origin > below) & (last - origin <= SHORT[index])

        @pl.when(last == first)
        def _():
            cc_ref[0, rows, :] = jnp.broadcast_to(mean_ref[0], (QP, D)).astype(bf16)
            log_ref[0, image] = jnp.zeros((1, HEADS * QP), f32)

        def in_one(size):
            place, valid = place_at(0, size)
            context, logs = attend_block(
                ck_ref[0, place, :], cv_ref[0, place, :], spread, valid, False
            )
            cc_ref[0, rows, :] = context.astype(bf16)
            log_ref[0, image] = logs

        for index, size in enumerate(SHORT):
            pl.when(fits(index))(functools.partial(in_one, size))

        @pl.when(last - origin > SHORT[-1])
        def _():
            top_ref[...] = jnp.full_like(top_ref, masked)
            sum_ref[...] = jnp.zeros_like(sum_ref)
            out_ref[...] = jnp.zeros_like(out_ref)

            @pl.loop(0, blocks)
            def _(block):
                place, valid = place_at(block)
                kept = pl.ds(pl.multiple_of(block * BLOCK, BLOCK), BLOCK)
                key = ck_ref[0, place, :]
                for pair in range(PAIRS):
                    lanes = slice(2 * QP * pair, 2 * QP * (pair + 1))
                    scores = jnp.where(valid, nt(key, long_rows(spread, pair)), masked)
                    score_ref[kept, lanes] = scores
                    top = jnp.max(scores, axis=0, keepdims=True)
                    top_ref[:, lanes] = jnp.maximum(top_ref[:, lanes], top)

            @pl.loop(0, blocks)
            def _(block):
                kept = pl.ds(pl.multiple_of(block * BLOCK, BLOCK), BLOCK)
                raised = jnp.exp2((score_ref[kept, :] - top_ref[...]) * (scale * log2e))
                score_ref[kept, :] = raised
                sum_ref[...] += total(raised)

            @pl.loop(0, blocks)
            def _(block):
                place, unused = place_at(block)
                kept = pl.ds(pl.multiple_of(block * BLOCK, BLOCK), BLOCK)
                value = cv_ref[0, place, :]
                products = []
                for pair in range(PAIRS):
                    lanes = slice(2 * QP * pair, 2 * QP * (pair + 1))
                    attend = (score_ref[kept, lanes] * (1.0 / sum_ref[:, lanes])).astype(bf16)
                    products.append(tn(attend, value))
                out_ref[...] += join_pairs(products)

            cc_ref[0, rows, :] = out_ref[...].astype(bf16)
            log_ref[0, image] = top_ref[...] * (scale * log2e) + jnp.log2(sum_ref[...])

    @row_loop(ROWS, CHUNK)
    def _(start, rows):
        rows_ref[rows, :] = rows_in_ref[0, rows, :] + nn(cc_ref[0, rows, :], w_ref[0]) + bias_ref[...]
    for image in range(IMG_MAX):
        after_ref[0, image * NQ : (image + 1) * NQ, :] = rows_ref[image * QP : image * QP + NQ, :]


def lanes_of(count, first, lanes=POS):
    row = lax.broadcasted_iota(jnp.int32, (count, lanes), 0)
    lane = lax.broadcasted_iota(jnp.int32, (count, lanes), 1)
    return (row + first == lane).astype(f32).astype(bf16)


def middle_kernel(
    ordered,
    bounds,
    x_ref,
    cot_ref,
    head_cot_ref,
    mine_ref,
    other_ref,
    small_in_ref,
    head_bias_ref,
    layer_ref,
    grad_ref,
    keep_ref,
    send_ref,
    dhead_ref,
    drow_ref,
    small_ref,
    bias_ref,
    box_ref,
    low_ref,
    cross_ref,
    sum_ref,
    branch_ref,
    hidden_ref,
    slope_ref,
    ff_ref,
    dff_ref,
    unit_ref,
):
    pack = pl.program_id(0)
    slots = x_ref.shape[1]
    half = mine_ref.shape[0]
    parts = 2 * half
    ff = FF_BLOCKS * D // parts
    share = D // parts
    near = D // ff
    boxes = 2 * ff
    extra = 2 * ff + 2 * share

    @pl.when(pack == 0)
    def _():
        small_ref[...] = small_in_ref[0].astype(f32).T
        ff_ref[0:half] = mine_ref[...]
        ff_ref[half:] = other_ref[...]

        @pl.loop(0, parts)
        def _(device):
            place = place_of(device, bounds, ordered, parts)
            pair = ff_ref[place, boxes:extra, :].astype(f32)
            rows = pl.ds(pl.multiple_of(device * share, share), share)
            unit_ref[0, rows, :] = pair[:share]
            unit_ref[1, rows, :] = pair[share:]

        box_ref[...] = unit_ref[...].astype(bf16)
        unit_ref[...] = jnp.zeros_like(unit_ref)
        for block in range(FF_BLOCKS):
            rows = [ff_ref[block * near + k, extra : extra + 16, :] for k in range(near)]
            rows = [row.astype(f32)[1:2, 0:ff] for row in rows]
            bias_ref[block] = jnp.concatenate(rows, axis=1)
        bias_ref[FF_BLOCKS:] = jnp.zeros((FF_BLOCKS, 1, D), f32)
        dff_ref[...] = jnp.zeros_like(dff_ref)
        dhead_ref[...] = jnp.zeros_like(dhead_ref)
        drow_ref[...] = jnp.zeros_like(drow_ref)

    def bias(index):
        return small_ref[BIAS + index : BIAS + index + 1, :]

    def gain(index):
        return small_ref[GAIN + index : GAIN + index + 1, :]

    def add_row(column, value):
        row = column - GAIN
        drow_ref[row : row + 1, :] += value

    def near_block(block):
        return pl.ds(block * near, near)

    def shrink(block):
        return ff_ref[near_block(block), 0:ff, :].reshape(D, D)

    def expand(block):
        return ff_ref[near_block(block), ff:boxes, :].reshape(D, D)

    @row_loop(slots, STEP)
    def _(start, rows):
        unit, unused = norm_parts(x_ref[0, rows, :])
        after_cross = unit * gain(1) + bias(10)
        cross_ref[rows, :] = after_cross
        low_ref[rows, :] = after_cross.astype(bf16)

    sum_ref[...] = cross_ref[...] + bias(6)
    hidden_ref[FF_BLOCKS - 1] = jnp.zeros((slots, D), bf16)

    @pl.loop(0, FF_BLOCKS)
    def _(block):
        before = (block + FF_BLOCKS - 1) % FF_BLOCKS
        sum_ref[...] += nn(hidden_ref[before], shrink(before))
        value, slope = gelu_parts(nt(low_ref[...], expand(block)) + bias_ref[block])
        hidden_ref[block] = value.astype(bf16)
        slope_ref[block] = slope

    sum_ref[...] += nn(hidden_ref[FF_BLOCKS - 1], shrink(FF_BLOCKS - 1))

    head_weight = small_in_ref[0, :, 0:POS]
    head_bias = nn(head_bias_ref[...], lanes_of(CLS + 4, 0))
    lane = lax.broadcasted_iota(jnp.int32, (1, POS), 1)
    is_box = (lane >= CLS) & (lane < CLS + 4)
    @chunk_loop(slots, STEP)
    def _(start, rows):
        slot = start + lax.broadcasted_iota(jnp.int32, (STEP, 1), 0)
        live = (slot < bounds[pack, IMG_MAX + 1] * NQ).astype(f32)
        unit_ffn, inverse_ffn = norm_parts(sum_ref[rows, :])
        after_ffn = unit_ffn * gain(2) + bias(11)
        layer_ref[0, rows, :] = (after_ffn * live).astype(bf16)
        unit_last, inverse_last = norm_parts(after_ffn)
        normed = (unit_last * gain(3) + bias(12)).astype(bf16)
        one, one_slope = gelu_parts(nn(normed, box_ref[0]) + bias(7))
        box_one = one.astype(bf16)
        two, two_slope = gelu_parts(nn(box_one, box_ref[1]) + bias(8))
        box_two = two.astype(bf16)
        box = jax.nn.sigmoid(nn(box_two, head_weight) + head_bias)

        head_cot = head_cot_ref[0, rows, :].astype(f32) * live
        grad_box = jnp.where(is_box, head_cot * box * (1.0 - box), 0.0).astype(bf16)
        grad_logit = jnp.where(lane < CLS, head_cot, 0.0).astype(bf16)
        drow_ref[31:32, 0:POS] += total(grad_box.astype(f32)) + total(grad_logit.astype(f32))
        normed_t = normed.T
        grad_two = (two_slope * nt(grad_box, head_weight)).astype(bf16)
        grad_one = (one_slope * nt(grad_two, box_ref[1])).astype(bf16)
        dhead_ref[...] += nn(normed_t, grad_logit) + tn(box_two, grad_box)
        unit_ref[0] += nn(normed_t, grad_one)
        unit_ref[1] += tn(box_one, grad_two)
        add_row(BIAS + 8, total(grad_two.astype(f32)))
        add_row(BIAS + 7, total(grad_one.astype(f32)))
        grad_normed = nt(grad_one, box_ref[0]) + nt(grad_logit, head_weight)
        add_row(GAIN + 3, total(grad_normed * unit_last))
        add_row(BIAS + 12, total(grad_normed))
        grad_after = cot_ref[0, rows, :].astype(f32) * live + norm_back(
            unit_last, inverse_last, gain(3), grad_normed
        )
        add_row(GAIN + 2, total(grad_after * unit_ffn))
        add_row(BIAS + 11, total(grad_after))
        grad_ffn = norm_back(unit_ffn, inverse_ffn, gain(2), grad_after)
        grad_branch = grad_ffn.astype(bf16)
        add_row(BIAS + 6, total(grad_branch.astype(f32)))
        sum_ref[rows, :] = grad_ffn
        branch_ref[rows, :] = grad_branch

    @pl.loop(0, FF_BLOCKS)
    def _(block):
        branch = branch_ref[...]
        dpre = (nt(branch, shrink(block)) * slope_ref[block]).astype(bf16)
        bias_ref[FF_BLOCKS + block] += total(dpre.astype(f32))
        dshrink = tn(hidden_ref[block], branch).reshape(near, ff, D)
        dff_ref[near_block(block), 0:ff, :] += dshrink
        dexpand = tn(dpre, low_ref[...]).reshape(near, ff, D)
        dff_ref[near_block(block), ff:boxes, :] += dexpand
        sum_ref[...] += nn(dpre, expand(block))

    @row_loop(slots, STEP)
    def _(start, rows):
        unit, inverse = norm_parts(x_ref[0, rows, :])
        grad = sum_ref[rows, :]
        add_row(GAIN + 1, total(grad * unit))
        add_row(BIAS + 10, total(grad))
        grad_ref[0, rows, :] = norm_back(unit, inverse, gain(1), grad)

    @pl.when(pack == pl.num_programs(0) - 1)
    def _():
        @pl.loop(0, parts)
        def _(device):
            place = place_of(device, bounds, ordered, parts)
            rows = pl.ds(pl.multiple_of(device * share, share), share)
            dff_ref[place, boxes : boxes + share, :] = unit_ref[0, rows, :]
            dff_ref[place, boxes + share : extra, :] = unit_ref[1, rows, :]

        for part in range(parts):
            dff_ref[part, extra : extra + 1, :] = drow_ref[31:32, :]
            side = part % near * ff
            values = bias_ref[FF_BLOCKS + part // near][:, side : side + ff]
            dff_ref[part, extra + 1 : extra + 2, 0:ff] = values
        keep_ref[...] = dff_ref[0:half]
        send_ref[...] = dff_ref[half:].astype(bf16)


def attend_back(key, value, spread, spread_grad, valid, logs, attend_ref, score_ref):
    scores = [nt(half_lanes(key, pair), pair_rows(spread, pair)) for pair in range(PAIRS)]
    grads = [nt(half_lanes(value, pair), pair_rows(spread_grad, pair)) for pair in range(PAIRS)]
    lows = []
    for pair in range(PAIRS):
        lanes = slice(2 * QP * pair, 2 * QP * (pair + 1))
        attend = jnp.exp2(scores[pair] * (scale * log2e) - logs[:, lanes])
        attend = jnp.where(valid, attend, 0.0)
        row_dot = total(attend * grads[pair])
        low = (attend * (grads[pair] - row_dot)).astype(bf16)
        attend_ref[:, lanes] = attend.astype(bf16)
        score_ref[:, lanes] = low
        lows.append(low)
    return join_halves([tn(lows[pair], half_lanes(key, pair)) for pair in range(PAIRS)]) * scale


def late_cross_kernel(
    bounds,
    grad_ref,
    memory_ref,
    pos_ref,
    w_ref,
    cq_ref,
    ck_ref,
    cv_ref,
    cc_ref,
    log_ref,
    gq_ref,
    dmemory_ref,
    dw_ref,
    drows_ref,
    flat_ref,
    grad_rows_ref,
    context_ref,
    dv_ref,
    spread_ref,
    spread_grad_ref,
    attend_ref,
    score_ref,
    sum_ref,
    out_ref,
):
    pack = pl.program_id(0)
    slots = grad_ref.shape[1]
    tokens = memory_ref.shape[1]

    @pl.when(pack == 0)
    def _():
        dw_ref[...] = jnp.zeros_like(dw_ref)
        drows_ref[...] = jnp.zeros_like(drows_ref)

    def add_row(row, value):
        drows_ref[row : row + 1, :] += value

    inside = lax.broadcasted_iota(jnp.int32, (QP, 1), 0) < NQ

    flat_ref[0:slots, :] = grad_ref[0]
    for image in range(IMG_MAX):
        part = flat_ref[image * NQ : image * NQ + QP, :]
        grad_rows_ref[image * QP : (image + 1) * QP, :] = jnp.where(inside, part, 0.0)
    @chunk_loop(ROWS, CHUNK)
    def _(start, rows):
        branch = grad_rows_ref[rows, :].astype(bf16)
        add_row(1, total(branch.astype(f32)))
        dw_ref[2] += tn(cc_ref[0, rows, :], branch)
        context_ref[rows, :] = nt(branch, w_ref[7]).astype(bf16)
    dmemory_ref[...] = jnp.zeros_like(dmemory_ref)
    dv_ref[...] = jnp.zeros_like(dv_ref)

    @pl.loop(0, IMG_MAX)
    def _(image):
        rows = pl.ds(pl.multiple_of(image * QP, QP), QP)
        first = bounds[pack, image]
        last = bounds[pack, image + 1]
        origin = (first // 16) * 16
        blocks = (last - origin + (BLOCK - 1)) // BLOCK
        spread = spread_ref
        spread_grad = spread_grad_ref
        attend_low = attend_ref
        score_low = score_ref
        spread_heads(cq_ref[0, rows, :], spread)
        spread_heads(context_ref[rows, :], spread_grad)
        logs = log_ref[0, image]

        def place_at(block, size=BLOCK):
            wanted = origin + block * size
            start = pl.multiple_of(jnp.minimum(wanted, tokens - size), 16)
            token = start + lax.broadcasted_iota(jnp.int32, (size, 1), 0)
            valid = (token >= jnp.maximum(first, wanted)) & (token < last)
            return pl.ds(start, size), valid

        def fits(index):
            below = SIZES[index - 1] if index else 0
            return (last > first) & (last - origin > below) & (last - origin <= SIZES[index])

        @pl.when(last == first)
        def _():
            gq_ref[0, rows, :] = jnp.zeros((QP, D), bf16)

        def in_one(size):
            place, valid = place_at(0, size)
            attend_part = attend_low.at[0:size]
            score_part = score_low.at[0:size]
            grad_query = attend_back(
                ck_ref[0, place, :],
                cv_ref[0, place, :],
                spread,
                spread_grad,
                valid,
                logs,
                attend_part,
                score_part,
            )
            gq_ref[0, rows, :] = grad_query.astype(bf16)
            dv_ref[place, :] += nn(attend_part[...], spread_grad[...])
            dmemory_ref[0, place, :] += nn(score_part[...], spread[...])

        for index, size in enumerate(SIZES):
            pl.when(fits(index))(functools.partial(in_one, size))

        @pl.when(last - origin > SIZES[-1])
        def _():
            sum_ref[...] = jnp.zeros_like(sum_ref)
            out_ref[...] = jnp.zeros_like(out_ref)

            @pl.loop(0, blocks)
            def _(block):
                place, valid = place_at(block)
                for pair in range(PAIRS):
                    lanes = slice(2 * QP * pair, 2 * QP * (pair + 1))
                    scores = nt(ck_ref[0, place, :], long_rows(spread, pair))
                    attend = jnp.exp2(scores * (scale * log2e) - logs[:, lanes])
                    attend = jnp.where(valid, attend, 0.0)
                    grad_attend = nt(cv_ref[0, place, :], long_rows(spread_grad, pair))
                    sum_ref[:, lanes] += total(attend * grad_attend)

            @pl.loop(0, blocks)
            def _(block):
                place, valid = place_at(block)
                key = ck_ref[0, place, :]
                products = []
                for pair in range(PAIRS):
                    lanes = slice(2 * QP * pair, 2 * QP * (pair + 1))
                    scores = nt(ck_ref[0, place, :], long_rows(spread, pair))
                    attend = jnp.exp2(scores * (scale * log2e) - logs[:, lanes])
                    attend = jnp.where(valid, attend, 0.0)
                    grad_attend = nt(cv_ref[0, place, :], long_rows(spread_grad, pair))
                    grad_scores = attend * (grad_attend - sum_ref[:, lanes])
                    grad_scores = grad_scores.astype(bf16)
                    attend_low[0:BLOCK, lanes] = attend.astype(bf16)
                    score_low[0:BLOCK, lanes] = grad_scores
                    products.append(tn(grad_scores, half_lanes(key, pair)))
                out_ref[...] += join_halves(products)
                dv_ref[place, :] += nn(attend_low[0:BLOCK, :], spread_grad[...])
                dmemory_ref[0, place, :] += nn(score_low[0:BLOCK, :], spread[...])

            gq_ref[0, rows, :] = (out_ref[...] * scale).astype(bf16)

    @chunk_loop(tokens, CHUNK)
    def _(start, rows):
        memory = memory_ref[0, rows, :]
        joined = (memory.astype(f32) + pos_ref[0, rows, :].astype(f32)).astype(bf16)
        grad_key = (dmemory_ref[0, rows, :] * scale).astype(bf16)
        grad_value = dv_ref[rows, :].astype(bf16)
        dmemory_ref[0, rows, :] = nt(grad_key, w_ref[4]) + nt(grad_value, w_ref[5])
        add_row(0, total(grad_value.astype(f32)))
        dw_ref[0] += tn(joined, grad_key)
        dw_ref[1] += tn(memory, grad_value)


def late_self_kernel(
    ordered,
    bounds,
    grad_ref,
    gcq_ref,
    target_ref,
    w_ref,
    qs_ref,
    ks_ref,
    vs_ref,
    cs_ref,
    inner_ref,
    log_ref,
    dcross_ref,
    dcross_rows_ref,
    dhead_ref,
    drow_ref,
    dtarget_ref,
    keep_ref,
    send_ref,
    small_ref,
    flat_ref,
    grad_rows_ref,
    place_ref,
    context_ref,
    gq_ref,
    gk_ref,
    gv_ref,
    spread_ref,
    spread_grad_ref,
    attend_ref,
    score_ref,
    drows_ref,
    dw_ref,
    block_ref,
):
    pack = pl.program_id(0)
    slots = target_ref.shape[1]

    @pl.when(pack == 0)
    def _():
        small_ref[...] = w_ref[SMALL].astype(f32).T
        dw_ref[0:4] = jnp.zeros((4, D, D), f32)
        dw_ref[4:6] = dcross_ref[0:2]
        dw_ref[6] = jnp.zeros((D, D), f32)
        dw_ref[7] = dcross_ref[2]
        drows_ref[...] = jnp.zeros_like(drows_ref)
        drows_ref[GAIN : GAIN + 32, :] = drow_ref[...]
        drows_ref[BIAS + 4 : BIAS + 6, :] += dcross_rows_ref[0:2, :]

    def bias(index):
        return small_ref[BIAS + index : BIAS + index + 1, :]

    def gain(index):
        return small_ref[GAIN + index : GAIN + index + 1, :]

    def add_row(row, value):
        drows_ref[row : row + 1, :] += value

    inside = lax.broadcasted_iota(jnp.int32, (QP, 1), 0) < NQ
    position = small_ref[POS : POS + QP, :]
    positions = jnp.concatenate([position] * (CHUNK // QP), axis=0)

    flat_ref[0:slots, :] = grad_ref[0]
    for image in range(IMG_MAX):
        part = flat_ref[image * NQ : image * NQ + QP, :]
        grad_rows_ref[image * QP : (image + 1) * QP, :] = jnp.where(inside, part, 0.0)
    flat_ref[0:slots, :] = target_ref[0].astype(f32)

    @chunk_loop(ROWS, CHUNK)
    def _(start, rows):
        unit, inverse = norm_parts(inner_ref[0, rows, :])
        cross_in = (unit * gain(0) + bias(9) + positions).astype(bf16)
        grad_query = gcq_ref[0, rows, :]
        add_row(BIAS + 3, total(grad_query.astype(f32)))
        dw_ref[3] += tn(cross_in, grad_query)
        place = nt(grad_query, w_ref[3])
        place_ref[rows, :] = place
        grad = grad_rows_ref[rows, :] + place
        add_row(GAIN, total(grad * unit))
        add_row(BIAS + 9, total(grad))
        grad = norm_back(unit, inverse, gain(0), grad)
        grad_rows_ref[rows, :] = grad
        branch = grad.astype(bf16)
        add_row(BIAS + 2, total(branch.astype(f32)))
        dw_ref[6] += tn(cs_ref[0, rows, :], branch)
        context_ref[rows, :] = nt(branch, w_ref[6]).astype(bf16)

    @pl.loop(0, IMG_MAX // TURNS)
    def _(step):
        for turn in range(TURNS):
            rows = pl.ds(pl.multiple_of((TURNS * step + turn) * QP, QP), QP)
            spread = spread_ref.at[turn]
            spread_grad = spread_grad_ref.at[turn]
            attend_low = attend_ref.at[turn * QP : (turn + 1) * QP]
            score_low = score_ref.at[turn * QP : (turn + 1) * QP]
            spread_heads(qs_ref[0, rows, :], spread)
            spread_heads(context_ref[rows, :], spread_grad)
            grad_query = attend_back(
                ks_ref[0, rows, :],
                vs_ref[0, rows, :],
                spread,
                spread_grad,
                inside,
                log_ref[0, TURNS * step + turn],
                attend_low,
                score_low,
            )
            gq_ref[rows, :] = grad_query.astype(bf16)
            gv_ref[rows, :] = nn(attend_low[...], spread_grad[...]).astype(bf16)
            gk_ref[rows, :] = (nn(score_low[...], spread[...]) * scale).astype(bf16)

    for start in range(0, ROWS, CHUNK):
        rows = slice(start, start + CHUNK)
        images = range(start // QP, (start + CHUNK) // QP)
        parts = [flat_ref[image * NQ : image * NQ + QP, :] for image in images]
        target = jnp.concatenate([jnp.where(inside, part, 0.0) for part in parts], axis=0)
        joined_t = (target + positions).astype(bf16).T
        grad_query = gq_ref[rows, :]
        grad_key = gk_ref[rows, :]
        grad_value = gv_ref[rows, :]
        add_row(BIAS + 0, total(grad_query.astype(f32)))
        add_row(BIAS + 1, total(grad_value.astype(f32)))
        dw_ref[0] += nn(joined_t, grad_query)
        dw_ref[1] += nn(joined_t, grad_key)
        dw_ref[2] += tn(target.astype(bf16), grad_value)
        grad_joined = nt(grad_query, w_ref[0]) + nt(grad_key, w_ref[1])
        grad_rows_ref[rows, :] += grad_joined + nt(grad_value, w_ref[2])
        grad_place = grad_joined + place_ref[rows, :]
        for image in range(CHUNK // QP):
            drows_ref[POS : POS + QP, :] += grad_place[image * QP : (image + 1) * QP, :]
    for image in range(IMG_MAX):
        part = grad_rows_ref[image * QP : image * QP + NQ, :]
        dtarget_ref[0, image * NQ : (image + 1) * NQ, :] = part

    @pl.when(pack == pl.num_programs(0) - 1)
    def _():
        small = drows_ref[...].T
        dw_ref[SMALL, :, POS:] = small[:, POS:]
        dw_ref[SMALL, :, :POS] = small[:, :POS] + dhead_ref[...]
        half, height, unused = keep_ref.shape
        parts = 2 * half
        share = D // parts
        used = (SMALL + 1) * share
        if height > used:
            block_ref[:, used:, :] = jnp.zeros((parts, height - used, D), f32)

        @pl.loop(0, parts)
        def _(device):
            place = place_of(device, bounds, ordered, parts)
            rows = pl.ds(pl.multiple_of(device * share, share), share)
            for unit in range(SMALL + 1):
                block_ref[place, unit * share : (unit + 1) * share, :] = dw_ref[unit, rows, :]

        keep_ref[...] = block_ref[0:half]
        send_ref[...] = block_ref[half:].astype(bf16)


def whole(shape):
    zeros = (0,) * len(shape)
    return pl.BlockSpec(shape, lambda *unused: zeros)


def by_pack(shape):
    zeros = (0,) * (len(shape) - 1)
    return pl.BlockSpec((1,) + tuple(shape[1:]), lambda pack, *unused: (pack,) + zeros)


LIMIT = 60 * 1024 * 1024


def params(axes):
    return pltpu.CompilerParams(
        dimension_semantics=("arbitrary",) * axes, vmem_limit_bytes=LIMIT
    )


def early_self(bounds, target, memory, memory_pos, mine, other, ordered):
    packs, slots, unused = target.shape
    tokens = memory.shape[1]
    height = mine.shape[1]
    wide = HEADS * QP
    low_rows = jax.ShapeDtypeStruct((packs, ROWS, D), bf16)
    rows = jax.ShapeDtypeStruct((packs, ROWS, D), f32)
    low_tokens = jax.ShapeDtypeStruct((packs, tokens, D), bf16)
    mean = jax.ShapeDtypeStruct((packs, 1, D), f32)
    logs = jax.ShapeDtypeStruct((packs, IMG_MAX, 1, wide), f32)
    outs = [rows] + [low_rows] * 4 + [rows, low_rows, low_tokens, low_tokens, mean, logs]
    units = jax.ShapeDtypeStruct((SMALL + 1, D, D), bf16)
    return pl.pallas_call(
        functools.partial(early_self_kernel, ordered),
        grid_spec=pltpu.PrefetchScalarGridSpec(
            num_scalar_prefetch=1,
            grid=(packs,),
            in_specs=[
                by_pack(target.shape),
                by_pack(memory.shape),
                by_pack(memory_pos.shape),
                whole(mine.shape),
                whole(other.shape),
            ],
            out_specs=[by_pack(out.shape) for out in outs] + [whole(units.shape)],
            scratch_shapes=[
                pltpu.VMEM((D, D), f32),
                pltpu.VMEM((slots + 32, D), f32),
                pltpu.VMEM((ROWS, D), f32),
                pltpu.VMEM((TURNS, wide, D), bf16),
                pltpu.VMEM((2 * mine.shape[0], height, D), bf16),
                pltpu.VMEM((SMALL + 1, D, D), f32),
            ],
        ),
        out_shape=outs + [units],
        compiler_params=params(1),
        cost_estimate=pl.CostEstimate(
            flops=packs * 8_000_000_000, bytes_accessed=packs * 9_000_000, transcendentals=0
        ),
        name="early_self",
    )(bounds, target, memory, memory_pos, mine, other)


def early_cross(bounds, rows, query, key, value, mean, weights, slots):
    packs = rows.shape[0]
    tokens = key.shape[1]
    wide = HEADS * QP
    outs = [
        jax.ShapeDtypeStruct((packs, slots, D), f32),
        jax.ShapeDtypeStruct(query.shape, bf16),
        jax.ShapeDtypeStruct((packs, IMG_MAX, 1, wide), f32),
    ]
    arrays = [rows, query, key, value, mean]
    return pl.pallas_call(
        early_cross_kernel,
        grid_spec=pltpu.PrefetchScalarGridSpec(
            num_scalar_prefetch=1,
            grid=(packs,),
            in_specs=[by_pack(array.shape) for array in arrays]
            + [
                pl.BlockSpec((1, D, D), lambda *unused: (7, 0, 0)),
                pl.BlockSpec((1, D, D), lambda *unused: (SMALL, 0, 0)),
            ],
            out_specs=[by_pack(out.shape) for out in outs],
            scratch_shapes=[
                pltpu.VMEM((ROWS, D), f32),
                pltpu.VMEM((wide, D), bf16),
                pltpu.VMEM((tokens, wide), f32),
                pltpu.VMEM((1, wide), f32),
                pltpu.VMEM((1, wide), f32),
                pltpu.VMEM((QP, D), f32),
                pltpu.VMEM((1, D), f32),
            ],
        ),
        out_shape=outs,
        compiler_params=params(1),
        cost_estimate=pl.CostEstimate(
            flops=packs * 8_000_000_000, bytes_accessed=packs * 7_000_000, transcendentals=0
        ),
        name="early_cross",
    )(bounds, *arrays, weights, weights)


def middle(bounds, x, cotangents, mine, other, small, head_bias, ordered):
    packs, slots, unused = x.shape
    half, height, unused = mine.shape
    outs = [
        jax.ShapeDtypeStruct(x.shape, bf16),
        jax.ShapeDtypeStruct(x.shape, f32),
        jax.ShapeDtypeStruct(mine.shape, f32),
        jax.ShapeDtypeStruct(mine.shape, bf16),
        jax.ShapeDtypeStruct((D, POS), f32),
        jax.ShapeDtypeStruct((32, D), f32),
    ]
    return pl.pallas_call(
        functools.partial(middle_kernel, ordered),
        grid_spec=pltpu.PrefetchScalarGridSpec(
            num_scalar_prefetch=1,
            grid=(packs,),
            in_specs=[
                by_pack(x.shape),
                *[by_pack(array.shape) for array in cotangents],
                whole(mine.shape),
                whole(other.shape),
                pl.BlockSpec((1, D, D), lambda *unused: (SMALL, 0, 0)),
                whole(head_bias.shape),
            ],
            out_specs=[by_pack(x.shape), by_pack(x.shape)] + [whole(out.shape) for out in outs[2:]],
            scratch_shapes=[
                pltpu.VMEM((D, D), f32),
                pltpu.VMEM((2 * FF_BLOCKS, 1, D), f32),
                pltpu.VMEM((2, D, D), bf16),
                pltpu.VMEM((slots, D), bf16),
                pltpu.VMEM((slots, D), f32),
                pltpu.VMEM((slots, D), f32),
                pltpu.VMEM((slots, D), bf16),
                pltpu.VMEM((FF_BLOCKS, slots, D), bf16),
                pltpu.VMEM((FF_BLOCKS, slots, D), f32),
                pltpu.VMEM((2 * half, height, D), bf16),
                pltpu.VMEM((2 * half, height, D), f32),
                pltpu.VMEM((2, D, D), f32),
            ],
        ),
        out_shape=outs,
        compiler_params=params(1),
        cost_estimate=pl.CostEstimate(
            flops=packs * 10_000_000_000, bytes_accessed=packs * 9_000_000, transcendentals=0
        ),
        name="middle",
    )(bounds, x, *cotangents, mine, other, small, head_bias)


def late_cross(bounds, grad, memory, memory_pos, weights, saved):
    packs, slots, unused = grad.shape
    tokens = memory.shape[1]
    wide = HEADS * QP
    outs = [
        jax.ShapeDtypeStruct((packs, ROWS, D), bf16),
        jax.ShapeDtypeStruct(memory.shape, f32),
        jax.ShapeDtypeStruct((3, D, D), f32),
        jax.ShapeDtypeStruct((8, D), f32),
    ]
    return pl.pallas_call(
        late_cross_kernel,
        grid_spec=pltpu.PrefetchScalarGridSpec(
            num_scalar_prefetch=1,
            grid=(packs,),
            in_specs=[
                by_pack(grad.shape),
                by_pack(memory.shape),
                by_pack(memory_pos.shape),
                whole(weights.shape),
            ]
            + [by_pack(array.shape) for array in saved],
            out_specs=[by_pack(outs[0].shape), by_pack(outs[1].shape)]
            + [whole(out.shape) for out in outs[2:]],
            scratch_shapes=[
                pltpu.VMEM((slots + 32, D), f32),
                pltpu.VMEM((ROWS, D), f32),
                pltpu.VMEM((ROWS, D), bf16),
                pltpu.VMEM((tokens, D), f32),
                pltpu.VMEM((wide, D), bf16),
                pltpu.VMEM((wide, D), bf16),
                pltpu.VMEM((SIZES[-1], wide), bf16),
                pltpu.VMEM((SIZES[-1], wide), bf16),
                pltpu.VMEM((1, wide), f32),
                pltpu.VMEM((QP, D), f32),
            ],
        ),
        out_shape=outs,
        compiler_params=params(1),
        cost_estimate=pl.CostEstimate(
            flops=packs * 12_000_000_000, bytes_accessed=packs * 9_000_000, transcendentals=0
        ),
        name="late_cross",
    )(bounds, grad, memory, memory_pos, weights, *saved)


def late_self(bounds, grad, grad_query, target, weights, saved, sums, block, ordered):
    packs, slots, unused = target.shape
    wide = HEADS * QP
    half, height, unused = block
    outs = [
        jax.ShapeDtypeStruct(target.shape, f32),
        jax.ShapeDtypeStruct(block, f32),
        jax.ShapeDtypeStruct(block, bf16),
    ]
    return pl.pallas_call(
        functools.partial(late_self_kernel, ordered),
        grid_spec=pltpu.PrefetchScalarGridSpec(
            num_scalar_prefetch=1,
            grid=(packs,),
            in_specs=[
                by_pack(grad.shape),
                by_pack(grad_query.shape),
                by_pack(target.shape),
                whole(weights.shape),
            ]
            + [by_pack(array.shape) for array in saved]
            + [whole(array.shape) for array in sums],
            out_specs=[by_pack(target.shape), whole(block), whole(block)],
            scratch_shapes=[
                pltpu.VMEM((D, D), f32),
                pltpu.VMEM((slots + 32, D), f32),
                pltpu.VMEM((ROWS, D), f32),
                pltpu.VMEM((ROWS, D), f32),
                pltpu.VMEM((ROWS, D), bf16),
                pltpu.VMEM((ROWS, D), bf16),
                pltpu.VMEM((ROWS, D), bf16),
                pltpu.VMEM((ROWS, D), bf16),
                pltpu.VMEM((TURNS, wide, D), bf16),
                pltpu.VMEM((TURNS, wide, D), bf16),
                pltpu.VMEM((TURNS * QP, wide), bf16),
                pltpu.VMEM((TURNS * QP, wide), bf16),
                pltpu.VMEM((D, D), f32),
                pltpu.VMEM(weights.shape, f32),
                pltpu.VMEM((2 * half, height, D), f32),
            ],
        ),
        out_shape=outs,
        compiler_params=params(1),
        cost_estimate=pl.CostEstimate(
            flops=packs * 10_000_000_000, bytes_accessed=packs * 7_000_000, transcendentals=0
        ),
        name="late_self",
    )(bounds, grad, grad_query, target, weights, *saved, *sums)


def stack(parts):
    return jnp.concatenate(parts, axis=0)


def fold(keep, received, count):
    for part in received:
        keep = keep + part.astype(f32)
    size = keep.shape[0] // count
    pieces = [keep[index * size : (index + 1) * size] for index in range(count)]
    return pieces[:1] + [piece.astype(bf16) for piece in pieces[1:]]


def run_of_images(segment, me):
    edge = jnp.arange(16, dtype=jnp.int32)
    below = segment[:, None, :] < edge[None, :, None]
    counts = jnp.sum(below.astype(jnp.int32), axis=-1)
    images = jnp.max(jnp.where(segment < IMG_MAX, segment + 1, 0), axis=-1)
    result = jnp.where(edge[None, :] == IMG_MAX + 1, images[:, None], counts)
    return jnp.where(edge[None, :] == ME, me, result)


def taller(rows):
    return jnp.pad(rows, ((0, -rows.shape[0] % 16), (0, 0)))


def pack_early(project, output, classes, box_final, query_pos, gains, biases):
    share = project.shape[1]
    columns = [
        classes,
        box_final,
        gains.T,
        biases.T,
        jnp.zeros((share, POS - BIAS - 13), bf16),
        query_pos.T,
        jnp.zeros((share, D - POS - NQ), bf16),
    ]
    small = jnp.concatenate(columns, axis=1)
    return taller(jnp.concatenate([project.reshape(-1, D), output.reshape(-1, D), small], axis=0))


def pack_middle(box, shrink, expand, expand_bias):
    extra = jnp.pad(expand_bias[None], ((1, EXTRA - 2), (0, D - expand_bias.shape[0])))
    return taller(jnp.concatenate([shrink, expand.T, box[0], box[1], extra], axis=0))


def pack_kernel(
    project,
    output,
    classes,
    final_t,
    gains,
    shifts_t,
    places_t,
    shrink,
    expand_t,
    box,
    row,
    out,
):
    share = project.shape[1]
    small = nn(classes[...], lanes_of(CLS, 0, D)) + tn(final_t[...], lanes_of(4, CLS, D))
    small += tn(gains[...], lanes_of(4, GAIN, D)) + nn(shifts_t[...], lanes_of(13, BIAS, D))
    small += nn(places_t[...], lanes_of(NQ, POS, D))
    first = [project[...].astype(f32).reshape(-1, D), output[...].astype(f32).reshape(-1, D), small]
    first = jnp.concatenate(first, axis=0)
    rest = -first.shape[0] % 16
    count = row.shape[1]
    vector = nn(row[...], lanes_of(count, 0, D))
    index = lax.broadcasted_iota(jnp.int32, (EXTRA, 1), 0)
    extra = jnp.where(index == 1, vector, 0.0)
    blocks = [first, jnp.zeros((rest, D), f32), shrink[...].astype(f32), expand_t[...].astype(f32)]
    blocks += [box[...].astype(f32).reshape(2 * share, D), extra]
    out[...] = jnp.concatenate(blocks, axis=0).astype(bf16)


def pack_both(project, output, classes, final, places, gains, shifts, box, shrink, expand, row):
    share = project.shape[1]
    early_rows = (SMALL + 1) * share
    early_rows += -early_rows % 16
    if share % 8:
        first = pack_early(project, output, classes, final, places, gains, shifts)
        return jnp.concatenate([first, pack_middle(box, shrink, expand, row)]), early_rows
    rows = early_rows + 2 * shrink.shape[0] + 2 * share + EXTRA
    block = pl.pallas_call(
        pack_kernel,
        out_shape=jax.ShapeDtypeStruct((rows, D), bf16),
        name="pack",
    )(
        project,
        output,
        classes,
        final.T,
        gains,
        shifts.T,
        places.T,
        shrink,
        expand.T,
        box,
        row[None],
    )
    return block, early_rows


def block_rows(devices):
    return [FF_BLOCKS * D // devices] * 2 + [D // devices] * 2


def cut(blocks, devices):
    marks = [0]
    for rows in block_rows(devices):
        marks.append(marks[-1] + rows)
    return [blocks[:, low:high] for low, high in zip(marks, marks[1:])], blocks[:, marks[-1] :]


def regroup(blocks, devices, parts):
    pieces, extra = cut(blocks, devices)
    pieces = [piece.reshape(parts, -1, D) for piece in pieces]
    head = jnp.broadcast_to(extra[0:1, 0:1], (parts, 1, D))
    row = extra[:, 1, : FF_BLOCKS * D // devices].reshape(parts, 1, -1)
    row = jnp.pad(row, ((0, 0), (0, EXTRA - 2), (0, D - row.shape[2])))
    result = jnp.concatenate(pieces + [head, row], axis=1)
    return jnp.pad(result, ((0, 0), (0, -result.shape[1] % 16), (0, 0)))


def regroup_units(blocks, devices, parts):
    units = SMALL + 1
    share = D // devices
    result = blocks[:, : units * share].reshape(devices, units, share, D).swapaxes(0, 1)
    result = result.reshape(units, parts, D // parts, D).swapaxes(0, 1).reshape(parts, -1, D)
    return jnp.pad(result, ((0, 0), (0, -result.shape[1] % 16), (0, 0)))


def parts_of(devices):
    return devices if FF_BLOCKS * D // devices % 16 == 0 else FF_BLOCKS


def bit_groups(devices):
    bits = [1 << k for k in range(1, devices.bit_length() - 1)]
    groups = [(1,)]
    while bits:
        groups.append((bits[0], bits[-1]) if len(bits) > 1 else (bits[0],))
        bits = bits[1:-1]
    return groups


def order_of(distance, devices):
    place = 0
    for bits in bit_groups(devices):
        for bit in bits[::-1]:
            place = 2 * place + distance // bit % 2
    return place


def mixes(bits):
    result = [0]
    for bit in bits:
        result += [mix | bit for mix in result]
    return result


def swap(value, bits, devices):
    return lax.ppermute(value, AXES, [(k, k ^ bits) for k in range(devices)])


def trade(held, bits, devices):
    return [swap(held, mix, devices) if mix else held for mix in mixes(bits)]


def deliver(sends, bits, devices):
    return [swap(send, mix, devices) for mix, send in zip(mixes(bits)[1:], sends)]


def counted(blocks, devices, me):
    places = [order_of(device, devices) for device in range(devices)]
    order = jnp.array(places)[jnp.arange(devices) ^ me]
    return jnp.take(blocks, order, axis=0)


def stepped(blocks, devices, me):
    distances = [0] * devices
    for device in range(devices):
        distances[order_of(device, devices)] = device
    return jnp.take(blocks, jnp.array(distances) ^ me, axis=0)


def unpack_middle(block, devices):
    pieces, extra = cut(block[None], devices)
    shrink, expand, box_one, box_two = [piece[0] for piece in pieces]
    row = extra[0, 1, 0 : shrink.shape[0]]
    return shrink, expand.T, jnp.stack([box_one, box_two]), row, extra[0, 0, 0 : CLS + 4]


def finish_kernel(count, keep, *refs):
    total_block = keep[0]
    for ref in refs[:count]:
        total_block += ref[0].astype(f32)
    project, output, classes, final_t, places_t, gains, shifts_t = refs[count:]
    share = project.shape[1]
    project[...] = total_block[: 6 * share].reshape(6, share, D)
    output[...] = total_block[6 * share : 8 * share].reshape(2, share, D)
    small = total_block[8 * share : 9 * share]
    classes[...] = small[:, 0:CLS]
    places_t[...] = small[:, POS : POS + NQ]
    shifts_t[...] = small[:, BIAS : BIAS + 13]
    turned = small[:, 0:POS].T
    final_t[...] = turned[CLS : CLS + 4]
    gains[...] = turned[GAIN : GAIN + 4]


def finish_early(keep, received, devices):
    share = D // devices
    if share % 8:
        return unpack_early(fold(keep, received, 1)[0][0], devices)
    shapes = [(6, share, D), (2, share, D), (share, CLS), (4, share), (share, NQ), (4, share)]
    shapes.append((share, 13))
    project, output, classes, final_t, places_t, gains, shifts_t = pl.pallas_call(
        functools.partial(finish_kernel, len(received)),
        out_shape=[jax.ShapeDtypeStruct(shape, f32) for shape in shapes],
        name="finish",
    )(keep, *received)
    return project, output, classes, final_t.T, places_t.T, gains, shifts_t.T


def unpack_early(block, devices):
    units = SMALL + 1
    share = D // devices
    block = block[: units * share].reshape(units, share, D)
    small = block[SMALL]
    return (
        block[0:6],
        block[6:8],
        small[:, 0:CLS],
        small[:, CLS : CLS + 4],
        small[:, POS : POS + NQ].T,
        small[:, GAIN : GAIN + 4].T,
        small[:, BIAS : BIAS + 13].T,
    )


def per_device(
    target,
    memory,
    memory_pos,
    segment,
    project_weight,
    output_weight,
    expand_weight,
    shrink_weight,
    box_weight,
    class_weight,
    box_final,
    query_pos,
    norm_gains,
    biases,
    expand_bias,
    head_bias,
    output_cotangent,
    logit_cotangent,
    box_cotangent,
):
    devices = lax.axis_size(AXES)
    me = lax.axis_index(AXES)
    groups = bit_groups(devices)
    parts = parts_of(devices)
    ordered = parts == devices
    slots = target.shape[1]

    both, height = pack_both(
        project_weight,
        output_weight,
        class_weight,
        box_final,
        query_pos,
        norm_gains,
        biases,
        box_weight,
        shrink_weight,
        expand_weight,
        expand_bias,
    )
    both = both[None]
    both_parts = trade(both, groups[-1], devices)
    both_parts, logit_cotangent, box_cotangent = lax.optimization_barrier(
        (both_parts, logit_cotangent, box_cotangent)
    )
    early_held = stack([part[:, :height] for part in both_parts])
    middle_held = stack([part[:, height:] for part in both_parts])
    for bits in groups[-2:1:-1]:
        early_held = stack(trade(early_held, bits, devices))
    early_parts = trade(early_held, groups[1], devices)
    bounds = run_of_images(segment, me)
    head_row = head_bias[None]
    rest = jnp.zeros(logit_cotangent.shape[:2] + (POS - CLS - 4,), bf16)
    head_cotangent = jnp.concatenate([logit_cotangent, box_cotangent, rest], axis=-1)
    early_parts, bounds, head_row, head_cotangent, middle_held = lax.optimization_barrier(
        (early_parts, bounds, head_row, head_cotangent, middle_held)
    )
    early_mine = stack(early_parts)
    early_other = swap(early_mine, 1, devices)
    if not ordered:
        blocks = counted(jnp.concatenate([early_mine, early_other]), devices, me)
        blocks = regroup_units(blocks, devices, parts)
        early_mine, early_other = blocks[: parts // 2], blocks[parts // 2 :]
    middle_parts = trade(middle_held, groups[-2], devices)
    rows, *saved = early_self(
        bounds, target, memory, memory_pos, early_mine, early_other, ordered
    )
    query, key, value, mean, self_logs, weights = saved[5:]
    middle_parts, query = lax.optimization_barrier((middle_parts, query))
    for bits in groups[-3:0:-1]:
        middle_parts = trade(stack(middle_parts), bits, devices)
    middle_mine = stack(middle_parts)
    middle_mine, query = lax.optimization_barrier((middle_mine, query))
    middle_other = swap(middle_mine, 1, devices)
    after, context, logs = early_cross(bounds, rows, query, key, value, mean, weights, slots)
    if not ordered:
        blocks = counted(jnp.concatenate([middle_mine, middle_other]), devices, me)
        blocks = regroup(blocks, devices, parts)
        middle_mine, middle_other = blocks[: parts // 2], blocks[parts // 2 :]
    layer, grad, keep, send, dhead, drow = middle(
        bounds,
        after,
        [output_cotangent, head_cotangent],
        middle_mine,
        middle_other,
        weights,
        head_row,
        ordered,
    )

    def real_blocks(keep, send, change):
        if ordered:
            return keep, send
        blocks = jnp.concatenate([keep, send.astype(f32)])
        blocks = stepped(change(blocks, parts, devices), devices, me)
        return blocks[: devices // 2], blocks[devices // 2 :].astype(bf16)

    def counts(index):
        return 1 << len(groups[index]) if index < len(groups) else 1

    keep, send = real_blocks(keep, send, regroup)
    grad, keep, send = lax.optimization_barrier((grad, keep, send))
    received = deliver([send], groups[0], devices)
    grad_query, dmemory, dcross, dcross_rows = late_cross(
        bounds, grad, memory, memory_pos, weights, [query, key, value, context, logs]
    )
    grad_query, received = lax.optimization_barrier((grad_query, received))
    keep, *sends = fold(keep, received, counts(1))
    grad_query, keep, sends = lax.optimization_barrier((grad_query, keep, sends))
    received = deliver(sends, groups[1], devices)
    sums = [dcross, dcross_rows, dhead, drow]
    block = early_mine.shape
    late_saved = saved[:5] + [self_logs]
    dtarget, early_keep, early_send = late_self(
        bounds, grad, grad_query, target, weights, late_saved, sums, block, ordered
    )
    early_keep, early_send, received = lax.optimization_barrier(
        (early_keep, early_send, received)
    )
    early_keep, early_send = real_blocks(early_keep, early_send, regroup_units)
    early_received = deliver([early_send], groups[0], devices)
    for index in range(2, len(groups)):
        keep, *sends = fold(keep, received, counts(index))
        received = deliver(sends, groups[index], devices)
    early_keep, *early_sends = fold(early_keep, early_received, counts(1))
    early_received = deliver(early_sends, groups[1], devices)
    early_received, received = lax.optimization_barrier((early_received, received))
    for index in range(2, len(groups)):
        early_keep, *early_sends = fold(early_keep, early_received, counts(index))
        early_received = deliver(early_sends, groups[index], devices)
    middle_sum = fold(keep, received, 1)[0]
    middle_grads = unpack_middle(middle_sum[0], devices)
    early_received, middle_grads = lax.optimization_barrier((early_received, middle_grads))
    shrink, expand, box, expand_row, head = middle_grads
    project, output, classes, final, places, gains, shifts = finish_early(
        early_keep, early_received, devices
    )
    return (
        layer,
        dtarget,
        dmemory,
        project,
        output,
        expand,
        shrink,
        box,
        classes,
        final,
        places,
        gains,
        shifts,
        expand_row,
        head,
    )


def solution(mesh):
    both = ("dp", "fsdp")
    by_rows = P(both, None, None)
    return jax.shard_map(
        per_device,
        mesh=mesh,
        in_specs=(
            by_rows,
            by_rows,
            by_rows,
            P(both, None),
            P(None, both, None),
            P(None, both, None),
            P(None, both),
            P(both, None),
            P(None, both, None),
            P(both, None),
            P(both, None),
            P(None, both),
            P(None, both),
            P(None, both),
            P(both),
            P(),
            by_rows,
            by_rows,
            by_rows,
        ),
        out_specs=(
            by_rows,
            by_rows,
            by_rows,
            P(None, both, None),
            P(None, both, None),
            P(None, both),
            P(both, None),
            P(None, both, None),
            P(both, None),
            P(both, None),
            P(None, both),
            P(None, both),
            P(None, both),
            P(both),
            P(),
        ),
        check_vma=False,
    )
```
